512 devices in a mesh: cls: 128 (over x, z, core), smp: 4 (over y).
Axes of the slice: x: 4, y: 4, z: 16, core: 2. Of those that a mesh axis runs over, the one named last changes fastest.
Arguments:
- counts: float32 [64, 131072], P('smp', 'cls'), may hold values from 0.1 to 300, as said below
- compat: bfloat16 [1024, 4, 128, 128], P('cls'), may hold values from 0.0099487305 to 1
- link_owner: int32 [1024, 4], P('cls'), may hold values from 0 to 127, all different within a row; in each aligned block of 8 rows (0 to 7, 8 to 15, ...) at most 2 rows name the same one
- link_local: int32 [1024, 4], P('cls'), may hold values from 0 to 3
- start: float32 [64, 65536], P('smp', 'cls'), may hold values from 0.2 to 5
Outputs:
- abundance: float32 [64, 65536], P('smp', 'cls')
The draws below stay inside these ranges and needn't reach their ends.
Inputs may be any that keep to these rules, and one draw needn't show every extreme that they name: `link_owner`: among the links of the class tiles of one index of cls, no owner is named more than 2 times, a bound that some block reaches; the 4 owners of one class tile differ. `counts`: Positive.
All inputs are finite; a program needn't handle non-finite values.
Results may differ from the reference program's by a relative error of at most 0.00048.
Values may be sent and summed in bfloat16 or wider, within the bound.
A program may use at most 64 MiB of HBM per device.

```python
import math
import jax
import jax.numpy as jnp
import numpy as np
from jax import lax

TILE = 128
K = 4
ITERS = 3
CT_DEV = 8
TT_DEV = 4
CAP = 2
CLASS_TILES = 1024
TRANS_TILES = 512
CLASSES = 131072
TRANSCRIPTS = 65536
SAMPLES = 64
N_CLS = 128


def draw_counts(key, part):
    key = jax.random.fold_in(key, 11)
    first = jax.random.fold_in(key, 0)
    rising = 3.0 ** (jnp.arange(CLASSES, dtype=jnp.float32) / CLASSES)
    base = jnp.exp(jax.random.uniform(first, (SAMPLES, CLASSES), jnp.float32, math.log(0.1), math.log(10.0)))
    return base * rising[None, :]


def set_ends(result, own_key, least, largest):
    shape = result.shape
    place = [jax.random.randint(jax.random.fold_in(own_key, axis), (), 0, shape[axis]) for axis in range(len(shape))]
    result = result.at[tuple(place)].set(least)
    longest = shape.index(max(shape))
    place[longest] = (place[longest] + 1) % shape[longest]
    return result.at[tuple(place)].set(largest)


def block_levels(rng, shape, cuts, least, high):
    gain = 1.0
    for dim, shards_of in cuts:
        draws = jax.random.uniform(jax.random.fold_in(jax.random.fold_in(rng, 6), dim), (shards_of,), jnp.float32, least / len(cuts), high / len(cuts))
        gain = gain * jnp.repeat(jnp.exp(draws), shape[dim] // shards_of).reshape((-1,) + (1,) * (len(shape) - 1 - dim))
    return gain


def assign_block(key, own, number, rows, number_of, top, reach, lean):
    sequence = jax.random.permutation(key, number_of)
    heavy_load, usual = shares(number_of, rows * top, reach, lean, True), shares(number_of, rows * top, reach, lean, False)
    places = jnp.arange(number_of)

    def named(sizes, turn):
        used = int((sizes > 0).sum())
        fixed = max(1, used // 4)
        moved = fixed + (places - fixed + turn * (used - fixed)) % max(1, number_of - fixed)
        return jnp.zeros((number_of,), jnp.int32).at[sequence[jnp.where(places < fixed, places, moved)]].set(jnp.asarray(sizes, jnp.int32))

    sizes = jnp.where(number % 4 == 0, named(heavy_load, number // 4), named(usual, number - number // 4 - 1))
    mixed = jax.random.permutation(jax.random.fold_in(own, 3), number_of)
    source_of, taker = mixed[0:number_of // 2 * 2:2], mixed[1:number_of // 2 * 2:2]
    room = jnp.minimum(sizes[source_of] - 1, reach - sizes[taker]) // 2
    room = jnp.where((source_of == sequence[0]) | (taker == sequence[0]) | (sizes[taker] == 0), 0, jnp.maximum(room, 0))
    moved = jax.random.randint(jax.random.fold_in(own, 4), (number_of // 2,), 0, 1 << 20) % (room + 1)
    sizes = sizes.at[source_of].add(-moved).at[taker].add(moved)
    members = jnp.searchsorted(jnp.cumsum(sizes), jnp.arange(rows * top), side="right").astype(jnp.int32)
    listing = members.reshape(top, rows).T
    listing = listing[jax.random.permutation(jax.random.fold_in(own, 1), rows)]
    turn = jax.random.randint(jax.random.fold_in(own, 2), (rows, 1), 0, top)
    return jnp.take_along_axis(listing, (jnp.arange(top)[None, :] + turn) % top, axis=1)


def shares(number_of, total, most, lean, full):
    portions = [(1 << 20) // math.isqrt(standing ** lean) + 1 for standing in range(1, number_of + 1)]
    largest = most if full else min(most, max(-(-total // number_of), total * portions[0] // sum(portions)))
    least = 1 if total - largest >= number_of - 1 else 0
    holding, rest = [largest] + [least] * (number_of - 1), total - largest - least * (number_of - 1)
    while rest > 0:
        candidates = [i for i in range(1, number_of) if holding[i] < largest] or [i for i in range(1, number_of) if holding[i] < most]
        whole, budget = sum([portions[i] for i in candidates]), rest
        for i in candidates:
            addition = min(most - holding[i], max(1, budget * portions[i] // whole), rest)
            holding[i] = holding[i] + addition
            rest = rest - addition
    return np.array(holding)


def setup_inputs(seed: int = 0) -> dict:
    splits = jax.random.split(jax.random.key(seed), 6)
    counts = draw_counts(jax.random.fold_in(splits[5], 71), 0)
    compat = jnp.clip(jnp.exp(math.log(1.0) - 4.61031033 * jax.random.uniform(splits[1], (CLASS_TILES, K, TILE, TILE), jnp.float32) ** block_levels(splits[1], (CLASS_TILES, K, TILE, TILE), ((0, 128),), -0.2, 0.2)), 0.0099487305, 1.0).astype(jnp.bfloat16)
    link_owner_keys = jax.random.split(jax.random.fold_in(splits[2], 1), CLASS_TILES // CT_DEV)
    link_owner_turns = jax.random.permutation(jax.random.fold_in(splits[2], 3), CLASS_TILES // CT_DEV)
    link_owner = jax.vmap(lambda own, number: assign_block(jax.random.fold_in(splits[2], 2), own, number, CT_DEV, N_CLS, K, CAP, 2))(link_owner_keys, link_owner_turns).reshape((CLASS_TILES, K))
    link_local = set_ends(jax.random.randint(splits[3], (CLASS_TILES, K), 0, TT_DEV), jax.random.fold_in(splits[3], 1), 0, TT_DEV - 1).astype(jnp.int32)
    start = jnp.clip(jnp.exp(math.log(5.0) - 3.218876 * jax.random.uniform(splits[4], (SAMPLES, TRANSCRIPTS), jnp.float32) ** block_levels(splits[4], (SAMPLES, TRANSCRIPTS), ((0, 4), (1, 128)), -0.2, 0.2)), 0.2, 5.0)
    return {"counts": counts, "compat": compat, "link_owner": link_owner, "link_local": link_local, "start": start}


MIXING = 0.3


def reference(counts, compat, link_owner, link_local, start):
    tile_ids = (link_owner * TT_DEV + link_local).astype(jnp.int32)
    total = jnp.sum(counts, axis=1)
    count_blocks = counts.reshape(SAMPLES, N_CLS, CT_DEV, TILE).transpose(1, 0, 2, 3)
    compat_blocks = compat.reshape(N_CLS, CT_DEV, K, TILE, TILE)
    index_blocks = tile_ids.reshape(N_CLS, CT_DEV * K)
    theta = start
    for sweep in range(ITERS):
        theta_b = theta.astype(jnp.bfloat16).reshape(SAMPLES, TRANS_TILES, TILE)

        def accumulate(returned, pieces):
            count_block, compat_block, index_block = pieces
            fetched = jnp.take(theta_b, index_block, axis=1).reshape(SAMPLES, CT_DEV, K, TILE)
            fetched = lax.optimization_barrier(fetched).astype(jnp.float32)
            expected = jnp.einsum("ikab,sikb->sia", compat_block.astype(jnp.float32), fetched)
            ratio = lax.optimization_barrier((count_block / expected).astype(jnp.bfloat16))
            share = jnp.einsum("sia,ikab->iksb", ratio.astype(jnp.float32), compat_block.astype(jnp.float32))
            share = lax.optimization_barrier(share.astype(jnp.bfloat16)).astype(jnp.float32)
            share = share.reshape(CT_DEV * K, SAMPLES, TILE)
            returned = returned + jax.ops.segment_sum(share, index_block, num_segments=TRANS_TILES)
            return returned, None

        empty_back = jnp.zeros((TRANS_TILES, SAMPLES, TILE), jnp.float32)
        returned, unused = lax.scan(accumulate, empty_back, (count_blocks, compat_blocks, index_blocks))
        returned = returned.transpose(1, 0, 2).reshape(SAMPLES, TRANSCRIPTS)
        updated = theta * returned / total[:, None]
        pooled = jnp.mean(updated, axis=0)
        theta = (1.0 - MIXING) * updated + MIXING * pooled[None, :]
    return theta * TRANSCRIPTS
```

```python
import functools

import jax
import jax.numpy as jnp
from jax import lax
from jax.experimental import pallas as pl
from jax.experimental.pallas import tpu as pltpu
from jax.sharding import PartitionSpec as P

TILE = 128
K = 4
ITERS = 3
MIXING = 0.3
MESH = pl.DeviceIdType.MESH
NX, NZ, NC, NY = 4, 16, 2, 4
TD = 4
LINKS = 32
COL = NZ * NC * TD
HALF = NZ * TD
STEP = 5
NEAR = (1, -1, 2, -2)


def em_kernel(
    tid, perm, keep, pos, counts, compat, start, out,
    th, xs, xr, sr, cum, d, cr, nr, sf, fr, tt, tx, tot, ps, theta,
    fz_s, fz_r, fc_s, fc_r, fx_s, fx_r, rx_s, rx_r, rc_s, rc_r,
    rn_s, rn_r, rf_s, rf_r, tz_s, tz_r, tg_s, tg_r, p_s, p_r,
):
    me = lax.axis_index("cls")
    y = lax.axis_index("smp")
    c = me % NC
    z = (me // NC) % NZ
    x = me // (NC * NZ)

    def zrel(off):
        return (z + off + NZ) % NZ

    def at(dx=0, dz=0, dc=0, dy=0):
        return (
            ((((x + dx) % NX) * NZ + zrel(dz)) * NC + (c + dc) % NC),
            (y + dy) % NY,
        )

    def copy(src, dst, send, recv, dev):
        return pltpu.make_async_remote_copy(
            src_ref=src, dst_ref=dst, send_sem=send, recv_sem=recv,
            device_id=dev, device_id_type=MESH,
        )

    peers = [dict(dz=o) for o in (1, -1, 2, -2, 3, -3, STEP, -STEP)]
    peers += [dict(dc=1)] + [dict(dx=o) for o in (1, 2, 3)] + [dict(dy=o) for o in (1, 2, 3)]
    group = [(dx, dc) for dx in range(NX) for dc in range(NC) if (dx, dc) != (0, 0)]
    peers += [dict(dx=dx, dc=1) for dx in (1, 2, 3)]
    barrier = pltpu.get_barrier_semaphore()
    for peer in peers:
        pl.semaphore_signal(barrier, inc=1, device_id=at(**peer), device_id_type=MESH)
    pl.semaphore_wait(barrier, len(peers))

    far = [(0, 0, STEP), (1, 0, -STEP)]
    near_own = [(2 + j, 0, o) for j, o in enumerate(NEAR)]
    near_low = [(6 + j, -STEP, o) for j, o in enumerate(NEAR)] + [(10, -STEP, 3)]
    near_high = [(11 + j, STEP, o) for j, o in enumerate(NEAR)]
    every = far + near_own + near_low + near_high

    def spread(blk, send, recv, arrived):
        def move(k, off, way):
            ref = blk(zrel(off))
            return copy(ref, ref, send.at[k], recv.at[k], at(dz=way))

        def take(k, off, way):
            ref = blk(zrel(off - way))
            copy(ref, ref, send.at[k], recv.at[k], at(dz=way)).wait_recv()
            arrived(1 + k, off - way)

        def first():
            for k, off, way in far + near_own:
                move(k, off, way).start()
            arrived(0, 0)

        def second():
            take(*far[0])
            for step in near_low:
                move(*step).start()
            take(*far[1])
            for step in near_high:
                move(*step).start()

        def third():
            for step in near_own + near_low + near_high:
                take(*step)

        def close():
            for step in every:
                move(*step).wait_send()

        return first, second, third, close

    def th_blk(core):
        def ref(zz):
            return th.at[pl.ds((zz * NC + core) * TD, TD)]

        return ref

    def to_core(k, off, mine=True):
        ref = th_blk(c if mine else 1 - c)(zrel(off))
        return copy(ref, ref, fc_s.at[k], fc_r.at[k], at(dc=1))

    f_first, f_second, f_third, f_close = spread(
        th_blk(c), fz_s, fz_r, lambda k, off: to_core(k, off).start()
    )
    core_steps = [(0, 0)] + [(1 + k, off - way) for k, off, way in every]
    t_first, t_second, t_third, t_close = spread(
        lambda zz: tt.at[zz], tz_s, tz_r, lambda k, off: None
    )

    theta[...] = start[...]
    cum[COL] = jnp.zeros((16, TILE), jnp.float32)

    def total_own():
        s = counts[:, 0:TILE]
        for i in range(1, counts.shape[1] // TILE):
            s = s + counts[:, i * TILE : (i + 1) * TILE]
        tt[z] = s

    def tg(j, dx, dc):
        return copy(tx.at[0], tx.at[1 + j], tg_s.at[j], tg_r.at[j], at(dx=dx, dc=dc))

    def sweep(r, carry):
        for t in range(TD):
            th[(z * NC + c) * TD + t] = theta[:, t * TILE : (t + 1) * TILE].astype(jnp.bfloat16)
        f_first()

        @pl.when(r == 0)
        def _():
            total_own()
            t_first()

        f_second()

        @pl.when(r == 0)
        def _():
            t_second()

        f_third()
        for k, off in core_steps:
            to_core(k, off, mine=False).wait_recv()

        def xcopy(dx):
            return copy(
                xs.at[pl.ds((dx - 1) * LINKS, LINKS)],
                xr.at[pl.ds(x * LINKS, LINKS)],
                fx_s.at[dx - 1],
                fx_r.at[dx - 1],
                at(dx=dx),
            )

        for dx in (2, 1, 3):
            row = ((x + dx) % NX) * LINKS

            def pick(l, _, dx=dx, row=row):
                xs[(dx - 1) * LINKS + l] = th[tid[row + l] % COL]
                return 0

            lax.fori_loop(0, LINKS, pick, 0, unroll=8)
            xcopy(dx).start()

        def pick_own(l, _):
            xr[x * LINKS + l] = th[tid[x * LINKS + l] % COL]
            return 0

        lax.fori_loop(0, LINKS, pick_own, 0, unroll=8)

        @pl.when(r == 0)
        def _():
            t_third()
            s = tt[0]
            for i in range(1, NZ):
                s = s + tt[i]
            tx[0] = s
            for j, (dx, dc) in enumerate(group):
                tg(j, dx, dc).start()

        def xwait(dx):
            ref = xr.at[pl.ds(((x + NX - dx) % NX) * LINKS, LINKS)]
            copy(ref, ref, fx_s.at[dx - 1], fx_r.at[dx - 1], at(dx=dx)).wait_recv()

        for dx in (1, 3, 2):
            xwait(dx)

        def tile(i, _):
            acc = jnp.zeros((16, TILE), jnp.float32)
            for k in range(K):
                l = i * K + k
                got = xr[(tid[x * LINKS + l] // COL) * LINKS + l]
                acc = acc + lax.dot_general(
                    got, compat[i, k], (((1,), (1,)), ((), ())),
                    preferred_element_type=jnp.float32,
                )
            ratio = (counts[:, pl.ds(pl.multiple_of(i * TILE, TILE), TILE)] / acc).astype(
                jnp.bfloat16
            )
            for k in range(K):
                sr[x * LINKS + i * K + k] = jnp.dot(
                    ratio, compat[i, k], preferred_element_type=jnp.float32
                ).astype(jnp.bfloat16)
            return 0

        lax.fori_loop(0, LINKS // K, tile, 0, unroll=2)

        def scopy(dx, src_x):
            ref = sr.at[pl.ds(src_x * LINKS, LINKS)]
            return copy(ref, ref, rx_s.at[dx - 1], rx_r.at[dx - 1], at(dx=dx))

        for dx in (2, 1, 3):
            scopy(dx, x).start()
        f_close()
        for k, off in core_steps:
            to_core(k, off).wait_send()
        for dx in (1, 3, 2):
            scopy(dx, (x + NX - dx) % NX).wait_recv()

        def add(j, acc):
            acc = jnp.where(keep[j] > 0, acc, 0.0) + sr[perm[j]].astype(jnp.float32)
            cum[j] = acc
            return acc

        lax.fori_loop(0, COL, add, jnp.zeros((16, TILE), jnp.float32), unroll=8)

        def dense(core):
            def one(i, _):
                for t in range(TD):
                    g = (i * NC + core) * TD + t
                    d[core * HALF + i * TD + t] = cum[pos[g]]
                return 0

            lax.fori_loop(0, NZ, one, 0, unroll=4)

        dense(1 - c)
        rcopy = copy(
            d.at[pl.ds((1 - c) * HALF, HALF)], cr, rc_s.at[0], rc_r.at[0], at(dc=1)
        )
        rcopy.start()
        dense(c)
        rcopy.wait_recv()

        def join(i, _):
            d[c * HALF + i] = d[c * HALF + i] + cr[i]
            return 0

        lax.fori_loop(0, HALF, join, 0, unroll=8)

        def dz(off):
            return d.at[pl.ds(c * HALF + zrel(off) * TD, TD)]

        kinds = (0, STEP, -STEP)
        nsteps = [
            (j * 3 + k, way, way + kind)
            for j, way in enumerate(NEAR)
            for k, kind in enumerate(kinds)
        ] + [(12, 3, 8)]

        def ncopy(slot, way, dest):
            return copy(
                dz(dest), nr.at[pl.ds(slot * TD, TD)], rn_s.at[slot], rn_r.at[slot], at(dz=way)
            )

        def fcopy(j, way):
            return copy(
                sf.at[pl.ds(j * TD, TD)], fr.at[pl.ds(j * TD, TD)], rf_s.at[j], rf_r.at[j],
                at(dz=way),
            )

        order = [n for n in nsteps if n[0] % 3 or n[0] == 12] + [
            n for n in nsteps if n[0] % 3 == 0 and n[0] != 12
        ]
        for n in order:
            ncopy(*n).start()
        for j, kind in ((0, STEP), (1, -STEP)):
            slots = [jj * 3 + 1 + j for jj in range(4)] + ([12] if j == 0 else [])
            for n in nsteps:
                if n[0] in slots:
                    ncopy(*n).wait_recv()
            for t in range(TD):
                acc = d[c * HALF + zrel(kind) * TD + t]
                for s in slots:
                    acc = acc + nr[s * TD + t]
                sf[j * TD + t] = acc
            fcopy(j, kind).start()
        own = [jj * 3 for jj in range(4)]
        for n in nsteps:
            if n[0] in own:
                ncopy(*n).wait_recv()

        @pl.when(r == 0)
        def _():
            for j, (dx, dc) in enumerate(group):
                tg(j, dx, dc).wait_recv()
            s = tx[0]
            for j in range(len(group)):
                s = s + tx[1 + j]
            tot[...] = jnp.broadcast_to(jnp.sum(s, axis=1, keepdims=True), (16, TILE))

        fcopy(0, STEP).wait_recv()
        fcopy(1, -STEP).wait_recv()
        for t in range(TD):
            acc = d[c * HALF + z * TD + t]
            for s in own:
                acc = acc + nr[s * TD + t]
            acc = acc + (fr[t] + fr[TD + t])
            cols = slice(t * TILE, (t + 1) * TILE)
            updated = theta[:, cols] * acc / tot[...]
            theta[:, cols] = updated
            ps[r * NY, :, cols] = jnp.sum(updated, axis=0, keepdims=True)

        def pcopy(dy):
            return copy(ps.at[r * NY], ps.at[r * NY + dy], p_s.at[r * 3 + dy - 1],
                        p_r.at[r * 3 + dy - 1], at(dy=dy))

        for dy in (2, 1, 3):
            pcopy(dy).start()
        for dx in (1, 2, 3):
            xcopy(dx).wait_send()
            scopy(dx, x).wait_send()
        rcopy.wait_send()
        for n in nsteps:
            ncopy(*n).wait_send()
        fcopy(0, STEP).wait_send()
        fcopy(1, -STEP).wait_send()

        @pl.when(r == 0)
        def _():
            t_close()
            for j, (dx, dc) in enumerate(group):
                tg(j, dx, dc).wait_send()

        for dy in (1, 3, 2):
            pcopy(dy).wait_recv()
        pooled = ps[r * NY] + ps[r * NY + 1] + ps[r * NY + 2] + ps[r * NY + 3]
        theta[...] = (1.0 - MIXING) * theta[...] + (MIXING / (16 * NY)) * pooled
        for dy in (1, 2, 3):
            pcopy(dy).wait_send()
        return carry

    lax.fori_loop(0, ITERS, sweep, 0)
    out[...] = theta[...] * 65536.0


def body(counts, compat, link_owner, link_local, start):
    x = lax.axis_index("cls") // (NZ * NC)
    mine = (link_owner * TD + link_local).reshape(-1)
    groups = [[(i * NZ + j) * NC + k for i in range(NX)] for j in range(NZ) for k in range(NC)]
    tid = lax.all_gather(mine, "cls", axis_index_groups=groups, tiled=True)
    key = jnp.where(tid // COL == x, tid % COL, COL)
    order = jnp.arange(COL, dtype=jnp.int32)
    before = (key[None, :] < key[:, None]) | (
        (key[None, :] == key[:, None]) & (order[None, :] < order[:, None])
    )
    rank = jnp.sum(before.astype(jnp.int32), axis=1)
    place = rank[None, :] == order[:, None]
    perm = jnp.sum(jnp.where(place, order[None, :], 0), axis=1)
    skey = jnp.sum(jnp.where(place, key[None, :], 0), axis=1)
    keep = jnp.concatenate(
        [jnp.zeros((1,), jnp.int32), (skey[1:] == skey[:-1]).astype(jnp.int32)]
    )
    upto = jnp.sum((key[None, :] <= order[:, None]).astype(jnp.int32), axis=1)
    some = jnp.any(key[None, :] == order[:, None], axis=1)
    pos = jnp.where(some, upto - 1, COL)
    smem = pl.BlockSpec(memory_space=pltpu.SMEM)
    vmem = pl.BlockSpec(memory_space=pltpu.VMEM)
    f32, bf16 = jnp.float32, jnp.bfloat16
    dma = pltpu.SemaphoreType.DMA

    def buf(n, dtype):
        return pltpu.VMEM((n, 16, TILE), dtype)

    return pl.pallas_call(
        em_kernel,
        out_shape=jax.ShapeDtypeStruct(start.shape, f32),
        in_specs=[smem] * 4 + [vmem] * 3,
        out_specs=vmem,
        scratch_shapes=[
            buf(COL, bf16),
            buf(3 * LINKS, bf16),
            buf(NX * LINKS, bf16),
            buf(NX * LINKS, bf16),
            buf(COL + 1, f32),
            buf(COL, f32),
            buf(HALF, f32),
            buf(13 * TD, f32),
            buf(2 * TD, f32),
            buf(2 * TD, f32),
            buf(NZ, f32),
            buf(NX * NC, f32),
            pltpu.VMEM((16, TILE), f32),
            pltpu.VMEM((ITERS * NY, 1, TD * TILE), f32),
            pltpu.VMEM((16, TD * TILE), f32),
            dma((15,)), dma((15,)),
            dma((16,)), dma((16,)),
            dma((3,)), dma((3,)),
            dma((3,)), dma((3,)),
            dma((1,)), dma((1,)),
            dma((13,)), dma((13,)),
            dma((2,)), dma((2,)),
            dma((15,)), dma((15,)),
            dma((7,)), dma((7,)),
            dma((9,)), dma((9,)),
        ],
        compiler_params=pltpu.CompilerParams(
            collective_id=0, has_side_effects=True, vmem_limit_bytes=40 << 20
        ),
        name="em_rounds",
    )(tid, perm, keep, pos, counts, compat, start)


def solution(mesh):
    placed = (
        P("smp", "cls"),
        P("cls", None, None, None),
        P("cls", None),
        P("cls", None),
        P("smp", "cls"),
    )
    return jax.shard_map(
        body, mesh=mesh, in_specs=placed, out_specs=P("smp", "cls"), check_vma=False
    )
```

```python
import functools

import jax
import jax.numpy as jnp
from jax import lax
from jax.experimental import pallas as pl
from jax.experimental.pallas import tpu as pltpu
from jax.sharding import PartitionSpec as P

TILE = 128
K = 4
ITERS = 3
MIXING = 0.3
MESH = pl.DeviceIdType.MESH
NX, NZ, NC, NY = 4, 16, 2, 4
TD = 4
CT = 8
LINKS = 32
COL = NZ * NC * TD
HALF = NZ * TD
STEP = 5
NEAR = (1, -1, 2, -2)


def em_kernel(
    owner_hbm, local_hbm, counts_hbm, compat_hbm, start_hbm, out,
    owner, local, counts, cb, tab, raw, lists, table, th, xs, xr, sr, cum, d, cr, nr, sf, fr, tt, tx, tot, ps, theta,
    fz_s, fz_r, fc_s, fc_r, fx_s, fx_r, rx_s, rx_r, rc_s, rc_r,
    rn_s, rn_r, rf_s, rf_r, tz_s, tz_r, tg_s, tg_r, p_s, p_r, l_s, l_r, in_s,
    pe, pr, rt, ex_s, ex_r, ey_s, ey_r, pe_s, pe_r, q_s, q_r,
):
    tid, perm, keep, pos, mytile = (table.at[i] for i in range(5))
    me = lax.axis_index("cls")
    y = lax.axis_index("smp")
    c = me % NC
    z = (me // NC) % NZ
    x = me // (NC * NZ)

    def zrel(off):
        return (z + off + NZ) % NZ

    def at(dx=0, dz=0, dc=0, dy=0):
        return (
            ((((x + dx) % NX) * NZ + zrel(dz)) * NC + (c + dc) % NC),
            (y + dy) % NY,
        )

    def copy(src, dst, send, recv, dev):
        return pltpu.make_async_remote_copy(
            src_ref=src, dst_ref=dst, send_sem=send, recv_sem=recv,
            device_id=dev, device_id_type=MESH,
        )

    peers = [dict(dz=o) for o in (1, -1, 2, -2, 3, -3, STEP, -STEP)]
    peers += [dict(dc=1)] + [dict(dx=o) for o in (1, 2, 3)] + [dict(dy=o) for o in (1, 2, 3)]
    group = [(dx, dc) for dx in range(NX) for dc in range(NC) if (dx, dc) != (0, 0)]
    peers += [dict(dx=dx, dc=1) for dx in (1, 2, 3)]
    barrier = pltpu.get_barrier_semaphore()
    for peer in peers:
        pl.semaphore_signal(barrier, inc=1, device_id=at(**peer), device_id_type=MESH)
    loads = [
        pltpu.make_async_copy(a, b, in_s.at[i])
        for i, (a, b) in enumerate(
            (
                (start_hbm, theta),
                (counts_hbm, counts),
                (compat_hbm, cb.at[pl.ds(x * LINKS, LINKS)]),
                (owner_hbm, owner),
                (local_hbm, local),
            )
        )
    ]
    for load in loads:
        load.start()
    lane = lax.broadcasted_iota(jnp.int32, (8, TILE), 1)
    raw[...] = jnp.zeros((8, TILE), jnp.int32)
    loads[3].wait()
    loads[4].wait()
    raw[0:K, 0:CT] = owner[...] * TD + local[...]
    row = raw[0:1, :]
    for k in range(1, K):
        row = row + pltpu.roll(raw[k : k + 1, :], k * CT, 1)
    for j in (1, 2):
        row = row + pltpu.roll(row, j * LINKS, 1)
    tab[0] = jnp.where(lane // LINKS == x, jnp.broadcast_to(row, (8, TILE)), 0)
    pl.semaphore_wait(barrier, len(peers))

    def lcopy(dx):
        return copy(tab.at[0], tab.at[dx], l_s.at[dx - 1], l_r.at[dx - 1], at(dx=dx))

    for dx in (2, 1, 3):
        lcopy(dx).start()

    def make_lists():
        for dx in (1, 3, 2):
            lcopy(dx).wait_recv()
        whole = tab[0, 0:1] + tab[1, 0:1] + tab[2, 0:1] + tab[3, 0:1]
        key = jnp.where(whole // COL == x, whole % COL, COL)
        keys = jnp.broadcast_to(key, (TILE, TILE))
        mine = jnp.transpose(keys)
        j = lax.broadcasted_iota(jnp.int32, (TILE, TILE), 0)
        i = lax.broadcasted_iota(jnp.int32, (TILE, TILE), 1)
        before = jnp.where(keys < mine, 1, 0) + jnp.where((keys == mine) & (i < j), 1, 0)
        rank = jnp.sum(before, axis=1, keepdims=True)
        place = rank == i
        order = jnp.sum(jnp.where(place, j, 0), axis=0, keepdims=True)
        ranked = jnp.sum(jnp.where(place, mine, 0), axis=0, keepdims=True)
        again = (ranked == pltpu.roll(ranked, 1, 1)) & (lane[0:1] > 0)
        upto = jnp.sum(jnp.where(mine <= i, 1, 0), axis=0, keepdims=True)
        some = jnp.sum(jnp.where(mine == i, 1, 0), axis=0, keepdims=True)
        lists[0:1, :] = whole
        lists[1:2, :] = order
        lists[2:3, :] = jnp.where(again, 1, 0)
        lists[3:4, :] = jnp.where(some > 0, upto - 1, COL)
        lists[4:5, :] = key
        load = pltpu.make_async_copy(lists, table, in_s.at[5])
        load.start()
        load.wait()
        for dx in (1, 2, 3):
            lcopy(dx).wait_send()

    far = [(0, 0, STEP), (1, 0, -STEP)]
    near_own = [(2 + j, 0, o) for j, o in enumerate(NEAR)]
    near_low = [(6 + j, -STEP, o) for j, o in enumerate(NEAR)] + [(10, -STEP, 3)]
    near_high = [(11 + j, STEP, o) for j, o in enumerate(NEAR)]
    every = far + near_own + near_low + near_high

    def spread(blk, send, recv, arrived):
        def move(k, off, way):
            ref = blk(zrel(off))
            return copy(ref, ref, send.at[k], recv.at[k], at(dz=way))

        def take(k, off, way):
            ref = blk(zrel(off - way))
            copy(ref, ref, send.at[k], recv.at[k], at(dz=way)).wait_recv()
            arrived(1 + k, off - way)

        def first():
            for k, off, way in far + near_own:
                move(k, off, way).start()
            arrived(0, 0)

        def second():
            take(*far[0])
            for step in near_low:
                move(*step).start()
            take(*far[1])
            for step in near_high:
                move(*step).start()

        def third():
            for step in near_own + near_low + near_high:
                take(*step)

        def close():
            for step in every:
                move(*step).wait_send()

        return first, second, third, close

    def th_blk(core):
        def ref(zz):
            return th.at[pl.ds((zz * NC + core) * TD, TD)]

        return ref

    def to_core(k, off, mine=True):
        ref = th_blk(c if mine else 1 - c)(zrel(off))
        return copy(ref, ref, fc_s.at[k], fc_r.at[k], at(dc=1))

    f_first, f_second, f_third, f_close = spread(
        th_blk(c), fz_s, fz_r, lambda k, off: to_core(k, off).start()
    )
    core_steps = [(0, 0)] + [(1 + k, off - way) for k, off, way in every]
    t_first, t_second, t_third, t_close = spread(
        lambda zz: tt.at[zz], tz_s, tz_r, lambda k, off: None
    )

    lists[...] = jnp.zeros((8, TILE), jnp.int32)
    loads[0].wait()
    cum[COL] = jnp.zeros((16, TILE), jnp.float32)
    th[COL] = jnp.zeros((16, TILE), jnp.bfloat16)

    def total_own():
        s = counts[:, 0:TILE]
        for i in range(1, counts.shape[1] // TILE):
            s = s + counts[:, i * TILE : (i + 1) * TILE]
        tt[z] = s

    def tg(j, dx, dc):
        return copy(tx.at[0], tx.at[1 + j], tg_s.at[j], tg_r.at[j], at(dx=dx, dc=dc))

    part = LINKS // NY

    def ex(dx, src_x):
        ref = cb.at[pl.ds(src_x * LINKS + y * part, part)]
        return copy(ref, ref, ex_s.at[dx - 1], ex_r.at[dx - 1], at(dx=dx))

    def ey(dx, dy, src_y):
        ref = cb.at[pl.ds(((x + NX - dx) % NX) * LINKS + src_y * part, part)]
        j = (dx - 1) * 3 + dy - 1
        return copy(ref, ref, ey_s.at[j], ey_r.at[j], at(dy=dy))

    def sweep(r, carry):
        for t in range(TD):
            th[(z * NC + c) * TD + t] = theta[:, t * TILE : (t + 1) * TILE].astype(jnp.bfloat16)
        f_first()

        @pl.when(r == 0)
        def _():
            loads[1].wait()
            total_own()
            t_first()
            loads[2].wait()
            for dx in (2, 1, 3):
                ex(dx, x).start()
            make_lists()

        f_second()

        @pl.when(r == 0)
        def _():
            t_second()

        f_third()
        for k, off in core_steps:
            to_core(k, off, mine=False).wait_recv()

        def xcopy(dx):
            return copy(
                xs.at[pl.ds((dx - 1) * LINKS, LINKS)],
                xr.at[pl.ds(x * LINKS, LINKS)],
                fx_s.at[dx - 1],
                fx_r.at[dx - 1],
                at(dx=dx),
            )

        def th_sent():
            f_close()
            for k, off in core_steps:
                to_core(k, off).wait_send()

        def by_tiles():
            for dx in (2, 1, 3):
                row = ((x + dx) % NX) * LINKS

                def pick(l, _, dx=dx, row=row):
                    xs[(dx - 1) * LINKS + l] = th[tid[row + l] % COL]
                    return 0

                lax.fori_loop(0, LINKS, pick, 0, unroll=8)
                xcopy(dx).start()

            def pick_own(l, _):
                xr[x * LINKS + l] = th[tid[x * LINKS + l] % COL]
                return 0

            lax.fori_loop(0, LINKS, pick_own, 0, unroll=8)

            t_third()
            s = tt[0]
            for i in range(1, NZ):
                s = s + tt[i]
            tx[0] = s
            for j, (dx, dc) in enumerate(group):
                tg(j, dx, dc).start()
            for dx in (1, 3, 2):
                ex(dx, (x + NX - dx) % NX).wait_recv()
                for dy in (2, 1, 3):
                    ey(dx, dy, y).start()

            def xwait(dx):
                ref = xr.at[pl.ds(((x + NX - dx) % NX) * LINKS, LINKS)]
                copy(ref, ref, fx_s.at[dx - 1], fx_r.at[dx - 1], at(dx=dx)).wait_recv()

            for dx in (1, 3, 2):
                xwait(dx)

            def tile(i, _):
                acc = jnp.zeros((16, TILE), jnp.float32)
                for k in range(K):
                    l = k * CT + i
                    got = xr[(tid[x * LINKS + l] // COL) * LINKS + l]
                    acc = acc + lax.dot_general(
                        got, cb[x * LINKS + i * K + k], (((1,), (1,)), ((), ())),
                        preferred_element_type=jnp.float32,
                    )
                ratio = (counts[:, pl.ds(pl.multiple_of(i * TILE, TILE), TILE)] / acc).astype(
                    jnp.bfloat16
                )
                for k in range(K):
                    sr[x * LINKS + k * CT + i] = jnp.dot(
                        ratio, cb[x * LINKS + i * K + k], preferred_element_type=jnp.float32
                    ).astype(jnp.bfloat16)
                return 0

            lax.fori_loop(0, LINKS // K, tile, 0, unroll=2)

            def scopy(dx, src_x):
                ref = sr.at[pl.ds(src_x * LINKS, LINKS)]
                return copy(ref, ref, rx_s.at[dx - 1], rx_r.at[dx - 1], at(dx=dx))

            for dx in (2, 1, 3):
                scopy(dx, x).start()
            th_sent()
            for dx in (1, 3, 2):
                scopy(dx, (x + NX - dx) % NX).wait_recv()
            for dx in (1, 2, 3):
                xcopy(dx).wait_send()
                scopy(dx, x).wait_send()
                ex(dx, x).wait_send()


        def pcopy_x(dx):
            return copy(
                pe.at[pl.ds(dx * CT, CT)], pr.at[pl.ds((dx - 1) * CT, CT)],
                pe_s.at[dx - 1], pe_r.at[dx - 1], at(dx=dx),
            )

        def qcopy(dx, src_x):
            ref = rt.at[pl.ds(src_x * CT, CT)]
            return copy(ref, ref, q_s.at[dx - 1], q_r.at[dx - 1], at(dx=dx))

        def by_sums():
            @pl.when(r == 1)
            def _():
                for dx in (1, 2, 3):
                    for dy in (1, 2, 3):
                        ey(dx, dy, (y + NY - dy) % NY).wait_recv()

            for dx in (2, 1, 3, 0):
                row = ((x + dx) % NX) * LINKS

                def part_sum(i, _, dx=dx, row=row):
                    acc = jnp.zeros((16, TILE), jnp.float32)
                    for k in range(K):
                        acc = acc + lax.dot_general(
                            th[mytile[row + k * CT + i]], cb[row + i * K + k],
                            (((1,), (1,)), ((), ())), preferred_element_type=jnp.float32,
                        )
                    pe[dx * CT + i] = acc
                    return 0

                lax.fori_loop(0, CT, part_sum, 0, unroll=4)
                if dx:
                    pcopy_x(dx).start()
            th_sent()
            for dx in (1, 3, 2):
                pcopy_x(dx).wait_recv()

            def ratio(i, _):
                acc = pe[i] + pr[i] + pr[CT + i] + pr[2 * CT + i]
                rt[x * CT + i] = (
                    counts[:, pl.ds(pl.multiple_of(i * TILE, TILE), TILE)] / acc
                ).astype(jnp.bfloat16)
                return 0

            lax.fori_loop(0, CT, ratio, 0, unroll=4)
            for dx in (2, 1, 3):
                qcopy(dx, x).start()
            for dx in (0, 1, 3, 2):
                src_x = (x + NX - dx) % NX
                if dx:
                    qcopy(dx, src_x).wait_recv()

                def shares(i, _, src_x=src_x):
                    for k in range(K):
                        sr[src_x * LINKS + k * CT + i] = jnp.dot(
                            rt[src_x * CT + i], cb[src_x * LINKS + i * K + k],
                            preferred_element_type=jnp.float32,
                        ).astype(jnp.bfloat16)
                    return 0

                lax.fori_loop(0, CT, shares, 0, unroll=4)
            for dx in (1, 2, 3):
                pcopy_x(dx).wait_send()
                qcopy(dx, x).wait_send()

            @pl.when(r == 1)
            def _():
                for dx in (1, 2, 3):
                    for dy in (1, 2, 3):
                        ey(dx, dy, y).wait_send()

        pl.when(r == 0)(by_tiles)
        pl.when(r > 0)(by_sums)

        def add(j, acc):
            acc = jnp.where(keep[j] > 0, acc, 0.0) + sr[perm[j]].astype(jnp.float32)
            cum[j] = acc
            return acc

        lax.fori_loop(0, COL, add, jnp.zeros((16, TILE), jnp.float32), unroll=8)

        def dense(core):
            def one(i, _):
                for t in range(TD):
                    g = (i * NC + core) * TD + t
                    d[core * HALF + i * TD + t] = cum[pos[g]]
                return 0

            lax.fori_loop(0, NZ, one, 0, unroll=4)

        dense(1 - c)
        rcopy = copy(
            d.at[pl.ds((1 - c) * HALF, HALF)], cr, rc_s.at[0], rc_r.at[0], at(dc=1)
        )
        rcopy.start()
        dense(c)
        rcopy.wait_recv()

        def join(i, _):
            d[c * HALF + i] = d[c * HALF + i] + cr[i]
            return 0

        lax.fori_loop(0, HALF, join, 0, unroll=8)

        def dz(off):
            return d.at[pl.ds(c * HALF + zrel(off) * TD, TD)]

        kinds = (0, STEP, -STEP)
        nsteps = [
            (j * 3 + k, way, way + kind)
            for j, way in enumerate(NEAR)
            for k, kind in enumerate(kinds)
        ] + [(12, 3, 8)]

        def ncopy(slot, way, dest):
            return copy(
                dz(dest), nr.at[pl.ds(slot * TD, TD)], rn_s.at[slot], rn_r.at[slot], at(dz=way)
            )

        def fcopy(j, way):
            return copy(
                sf.at[pl.ds(j * TD, TD)], fr.at[pl.ds(j * TD, TD)], rf_s.at[j], rf_r.at[j],
                at(dz=way),
            )

        order = [n for n in nsteps if n[0] % 3 or n[0] == 12] + [
            n for n in nsteps if n[0] % 3 == 0 and n[0] != 12
        ]
        for n in order:
            ncopy(*n).start()
        for j, kind in ((0, STEP), (1, -STEP)):
            slots = [jj * 3 + 1 + j for jj in range(4)] + ([12] if j == 0 else [])
            for n in nsteps:
                if n[0] in slots:
                    ncopy(*n).wait_recv()
            for t in range(TD):
                acc = d[c * HALF + zrel(kind) * TD + t]
                for s in slots:
                    acc = acc + nr[s * TD + t]
                sf[j * TD + t] = acc
            fcopy(j, kind).start()
        own = [jj * 3 for jj in range(4)]
        for n in nsteps:
            if n[0] in own:
                ncopy(*n).wait_recv()

        @pl.when(r == 0)
        def _():
            for j, (dx, dc) in enumerate(group):
                tg(j, dx, dc).wait_recv()
            s = tx[0]
            for j in range(len(group)):
                s = s + tx[1 + j]
            tot[...] = jnp.broadcast_to(jnp.sum(s, axis=1, keepdims=True), (16, TILE))

        fcopy(0, STEP).wait_recv()
        fcopy(1, -STEP).wait_recv()
        for t in range(TD):
            acc = d[c * HALF + z * TD + t]
            for s in own:
                acc = acc + nr[s * TD + t]
            acc = acc + (fr[t] + fr[TD + t])
            cols = slice(t * TILE, (t + 1) * TILE)
            updated = theta[:, cols] * acc / tot[...]
            theta[:, cols] = updated
            ps[r * NY, :, cols] = jnp.sum(updated, axis=0, keepdims=True)

        def pcopy(dy):
            return copy(ps.at[r * NY], ps.at[r * NY + dy], p_s.at[r * 3 + dy - 1],
                        p_r.at[r * 3 + dy - 1], at(dy=dy))

        for dy in (2, 1, 3):
            pcopy(dy).start()
        rcopy.wait_send()
        for n in nsteps:
            ncopy(*n).wait_send()
        fcopy(0, STEP).wait_send()
        fcopy(1, -STEP).wait_send()

        @pl.when(r == 0)
        def _():
            t_close()
            for j, (dx, dc) in enumerate(group):
                tg(j, dx, dc).wait_send()

        for dy in (1, 3, 2):
            pcopy(dy).wait_recv()
        pooled = ps[r * NY] + ps[r * NY + 1] + ps[r * NY + 2] + ps[r * NY + 3]
        theta[...] = (1.0 - MIXING) * theta[...] + (MIXING / (16 * NY)) * pooled
        for dy in (1, 2, 3):
            pcopy(dy).wait_send()
        return carry

    lax.fori_loop(0, ITERS, sweep, 0)
    out[...] = theta[...] * 65536.0


def body(counts, compat, link_owner, link_local, start):
    hbm = pl.BlockSpec(memory_space=pltpu.HBM)
    vmem = pl.BlockSpec(memory_space=pltpu.VMEM)
    f32, bf16 = jnp.float32, jnp.bfloat16
    dma = pltpu.SemaphoreType.DMA

    def buf(n, dtype):
        return pltpu.VMEM((n, 16, TILE), dtype)

    return pl.pallas_call(
        em_kernel,
        out_shape=jax.ShapeDtypeStruct(start.shape, f32),
        in_specs=[hbm] * 5,
        out_specs=vmem,
        scratch_shapes=[
            pltpu.VMEM((K, CT), jnp.int32),
            pltpu.VMEM((K, CT), jnp.int32),
            pltpu.VMEM(counts.shape, f32),
            pltpu.VMEM((NX * LINKS, TILE, TILE), bf16),
            pltpu.VMEM((NX, 8, TILE), jnp.int32),
            pltpu.VMEM((8, TILE), jnp.int32),
            pltpu.VMEM((8, TILE), jnp.int32),
            pltpu.SMEM((8, TILE), jnp.int32),
            buf(COL + 1, bf16),
            buf(3 * LINKS, bf16),
            buf(NX * LINKS, bf16),
            buf(NX * LINKS, bf16),
            buf(COL + 1, f32),
            buf(COL, f32),
            buf(HALF, f32),
            buf(13 * TD, f32),
            buf(2 * TD, f32),
            buf(2 * TD, f32),
            buf(NZ, f32),
            buf(NX * NC, f32),
            pltpu.VMEM((16, TILE), f32),
            pltpu.VMEM((ITERS * NY, 1, TD * TILE), f32),
            pltpu.VMEM((16, TD * TILE), f32),
            dma((15,)), dma((15,)),
            dma((16,)), dma((16,)),
            dma((3,)), dma((3,)),
            dma((3,)), dma((3,)),
            dma((1,)), dma((1,)),
            dma((13,)), dma((13,)),
            dma((2,)), dma((2,)),
            dma((15,)), dma((15,)),
            dma((7,)), dma((7,)),
            dma((9,)), dma((9,)),
            dma((3,)), dma((3,)), dma((6,)),
            buf(NX * CT, f32),
            buf(3 * CT, f32),
            buf(NX * CT, bf16),
            dma((3,)), dma((3,)),
            dma((9,)), dma((9,)),
            dma((3,)), dma((3,)),
            dma((3,)), dma((3,)),
        ],
        compiler_params=pltpu.CompilerParams(
            collective_id=0, has_side_effects=True, vmem_limit_bytes=60 << 20
        ),
        name="em_rounds",
    )(link_owner.T, link_local.T, counts, compat.reshape(LINKS, TILE, TILE), start)


def solution(mesh):
    placed = (
        P("smp", "cls"),
        P("cls", None, None, None),
        P("cls", None),
        P("cls", None),
        P("smp", "cls"),
    )
    return jax.shard_map(
        body, mesh=mesh, in_specs=placed, out_specs=P("smp", "cls"), check_vma=False
    )
```

```python
import functools

import jax
import jax.numpy as jnp
from jax import lax
from jax.experimental import pallas as pl
from jax.experimental.pallas import tpu as pltpu
from jax.sharding import PartitionSpec as P

TILE = 128
K = 4
ITERS = 3
MIXING = 0.3
MESH = pl.DeviceIdType.MESH
NX, NZ, NC, NY = 4, 16, 2, 4
TD = 4
CT = 8
LINKS = 32
COL = NZ * NC * TD
HALF = NZ * TD
STEP = 5
NEAR = (1, -1, 2, -2)


def em_kernel(
    owner_hbm, local_hbm, counts_hbm, compat_hbm, start_hbm, out,
    owner, local, counts, cb, tab, raw, lists, table, th, xs, xr, sr, cum, d, cr, nr, sf, fr, tt, tx, tot, ps, theta,
    fz_s, fz_r, fc_s, fc_r, fx_s, fx_r, rx_s, rx_r, rc_s, rc_r,
    rn_s, rn_r, rf_s, rf_r, tz_s, tz_r, tg_s, tg_r, p_s, p_r, l_s, l_r, in_s,
    tf, tf_s, tf_r, pq, rows, sums, pe, pr, rt, ex_s, ex_r, ey_s, ey_r, pe_s, pe_r, q_s, q_r,
):
    tid, perm, keep, pos, mytile = (table.at[i] for i in range(5))
    me = lax.axis_index("cls")
    y = lax.axis_index("smp")
    c = me % NC
    z = (me // NC) % NZ
    x = me // (NC * NZ)

    turn = 1 - 2 * c

    def zrel(off):
        return (z + turn * off + NZ) % NZ

    def at(dx=0, dz=0, dc=0, dy=0):
        return (
            ((((x + dx) % NX) * NZ + zrel(dz)) * NC + (c + dc) % NC),
            (y + dy) % NY,
        )

    def copy(src, dst, send, recv, dev):
        return pltpu.make_async_remote_copy(
            src_ref=src, dst_ref=dst, send_sem=send, recv_sem=recv,
            device_id=dev, device_id_type=MESH,
        )

    peers = [dict(dz=o) for o in (1, -1, 2, -2, 3, -3, STEP, -STEP)]
    peers += [dict(dc=1)] + [dict(dx=o) for o in (1, 2, 3)] + [dict(dy=o) for o in (1, 2, 3)]
    group = [(dx, dc) for dx in range(NX) for dc in range(NC) if (dx, dc) != (0, 0)]
    peers += [dict(dx=dx, dc=1) for dx in (1, 2, 3)]
    peers += [dict(dz=o, dy=dy) for o in (STEP, -STEP) for dy in (1, 2, 3)]
    barrier = pltpu.get_barrier_semaphore()
    for peer in peers:
        pl.semaphore_signal(barrier, inc=1, device_id=at(**peer), device_id_type=MESH)
    loads = [
        pltpu.make_async_copy(a, b, in_s.at[i])
        for i, (a, b) in enumerate(
            (
                (start_hbm, theta),
                (counts_hbm, counts),
                (compat_hbm, cb.at[pl.ds(x * LINKS, LINKS)]),
                (owner_hbm, owner),
                (local_hbm, local),
            )
        )
    ]
    for load in loads:
        load.start()
    lane = lax.broadcasted_iota(jnp.int32, (8, TILE), 1)
    raw[...] = jnp.zeros((8, TILE), jnp.int32)
    loads[3].wait()
    loads[4].wait()
    raw[0:K, 0:CT] = owner[...] * TD + local[...]
    row = raw[0:1, :]
    for k in range(1, K):
        row = row + pltpu.roll(raw[k : k + 1, :], k * CT, 1)
    for j in (1, 2):
        row = row + pltpu.roll(row, j * LINKS, 1)
    tab[0] = jnp.where(lane // LINKS == x, jnp.broadcast_to(row, (8, TILE)), 0)
    pl.semaphore_wait(barrier, len(peers))

    def lcopy(dx):
        return copy(tab.at[0], tab.at[dx], l_s.at[dx - 1], l_r.at[dx - 1], at(dx=dx))

    for dx in (2, 1, 3):
        lcopy(dx).start()

    def make_lists():
        for dx in (1, 3, 2):
            lcopy(dx).wait_recv()
        whole = tab[0, 0:1] + tab[1, 0:1] + tab[2, 0:1] + tab[3, 0:1]
        key = jnp.where(whole // COL == x, whole % COL, COL)
        keys = jnp.broadcast_to(key, (TILE, TILE))
        mine = jnp.transpose(keys)
        j = lax.broadcasted_iota(jnp.int32, (TILE, TILE), 0)
        i = lax.broadcasted_iota(jnp.int32, (TILE, TILE), 1)
        before = jnp.where(keys < mine, 1, 0) + jnp.where((keys == mine) & (i < j), 1, 0)
        rank = jnp.sum(before, axis=1, keepdims=True)
        place = rank == i
        order = jnp.sum(jnp.where(place, j, 0), axis=0, keepdims=True)
        ranked = jnp.sum(jnp.where(place, mine, 0), axis=0, keepdims=True)
        again = (ranked == pltpu.roll(ranked, 1, 1)) & (lane[0:1] > 0)
        upto = jnp.sum(jnp.where(mine <= i, 1, 0), axis=0, keepdims=True)
        some = jnp.sum(jnp.where(mine == i, 1, 0), axis=0, keepdims=True)
        lists[0:1, :] = whole
        lists[1:2, :] = order
        lists[2:3, :] = jnp.where(again, 1, 0)
        lists[3:4, :] = jnp.where(some > 0, upto - 1, COL)
        lists[4:5, :] = key
        load = pltpu.make_async_copy(lists, table, in_s.at[5])
        load.start()
        load.wait()
        for dx in (1, 2, 3):
            lcopy(dx).wait_send()

    far = [(0, 0, STEP), (1, 0, -STEP)]
    near_own = [(2 + j, 0, o) for j, o in enumerate(NEAR)]
    near_low = [(6 + j, -STEP, o) for j, o in enumerate(NEAR)] + [(10, -STEP, 3)]
    near_high = [(11 + j, STEP, o) for j, o in enumerate(NEAR)]
    every = far + near_own + near_low + near_high

    def spread(blk, send, recv, arrived):
        def move(k, off, way):
            ref = blk(zrel(off))
            return copy(ref, ref, send.at[k], recv.at[k], at(dz=way))

        def take(k, off, way):
            ref = blk(zrel(off - way))
            copy(ref, ref, send.at[k], recv.at[k], at(dz=way)).wait_recv()
            arrived(1 + k, off - way)

        def first():
            for k, off, way in far + near_own:
                move(k, off, way).start()
            arrived(0, 0)

        def second():
            take(*far[0])
            for step in near_low:
                move(*step).start()
            take(*far[1])
            for step in near_high:
                move(*step).start()

        def third():
            for step in near_own + near_low + near_high:
                take(*step)

        def close():
            for step in every:
                move(*step).wait_send()

        return first, second, third, close

    def th_blk(core):
        def ref(zz):
            return th.at[pl.ds((zz * NC + core) * TD, TD)]

        return ref

    def to_core(k, off, mine=True):
        ref = th_blk(c if mine else 1 - c)(zrel(off if mine else -off))
        return copy(ref, ref, fc_s.at[k], fc_r.at[k], at(dc=1))

    f_first, f_second, f_third, f_close = spread(
        th_blk(c), fz_s, fz_r, lambda k, off: to_core(k, off).start()
    )
    core_steps = [(0, 0)] + [(1 + k, off - way) for k, off, way in every]
    t_first, t_second, t_third, t_close = spread(
        lambda zz: tt.at[zz], tz_s, tz_r, lambda k, off: None
    )

    lists[...] = jnp.zeros((8, TILE), jnp.int32)
    loads[0].wait()
    cum[COL] = jnp.zeros((16, TILE), jnp.float32)
    th[COL] = jnp.zeros((16, TILE), jnp.bfloat16)

    def total_own():
        s = counts[:, 0:TILE]
        for i in range(1, counts.shape[1] // TILE):
            s = s + counts[:, i * TILE : (i + 1) * TILE]
        tt[z] = s

    def tg(j, dx, dc):
        return copy(tx.at[0], tx.at[1 + j], tg_s.at[j], tg_r.at[j], at(dx=dx, dc=dc))

    part = LINKS // NY

    def ex(dx, src_x):
        ref = cb.at[pl.ds(src_x * LINKS + y * part, part)]
        return copy(ref, ref, ex_s.at[dx - 1], ex_r.at[dx - 1], at(dx=dx))

    def ey(dx, dy, src_y):
        ref = cb.at[pl.ds(((x + NX - dx) % NX) * LINKS + src_y * part, part)]
        j = (dx - 1) * 3 + dy - 1
        return copy(ref, ref, ey_s.at[j], ey_r.at[j], at(dy=dy))

    def sweep(r, carry):
        for t in range(TD):
            th[(z * NC + c) * TD + t] = theta[:, t * TILE : (t + 1) * TILE].astype(jnp.bfloat16)
        f_first()

        @pl.when(r == 0)
        def _():
            loads[1].wait()
            total_own()
            t_first()
            loads[2].wait()
            for dx in (2, 1, 3):
                ex(dx, x).start()
            make_lists()

        f_second()

        @pl.when(r == 0)
        def _():
            t_second()

        f_third()

        def tcopy(j, way):
            k = r * 2 + j
            return copy(theta, tf.at[k], tf_s.at[k], tf_r.at[k], at(dz=way))

        relays = ((0, STEP), (1, -STEP))
        for j, way in relays:
            tcopy(j, way).start()
        for k, off in core_steps:
            to_core(k, off, mine=False).wait_recv()

        def xcopy(dx):
            return copy(
                xs.at[pl.ds((dx - 1) * LINKS, LINKS)],
                xr.at[pl.ds(x * LINKS, LINKS)],
                fx_s.at[dx - 1],
                fx_r.at[dx - 1],
                at(dx=dx),
            )

        def th_sent():
            f_close()
            for k, off in core_steps:
                to_core(k, off).wait_send()

        def by_tiles():
            for dx in (2, 1, 3):
                row = ((x + dx) % NX) * LINKS

                def pick(l, _, dx=dx, row=row):
                    xs[(dx - 1) * LINKS + l] = th[tid[row + l] % COL]
                    return 0

                lax.fori_loop(0, LINKS, pick, 0, unroll=8)
                xcopy(dx).start()

            def pick_own(l, _):
                xr[x * LINKS + l] = th[tid[x * LINKS + l] % COL]
                return 0

            lax.fori_loop(0, LINKS, pick_own, 0, unroll=8)

            t_third()
            s = tt[0]
            for i in range(1, NZ):
                s = s + tt[i]
            tx[0] = s
            for j, (dx, dc) in enumerate(group):
                tg(j, dx, dc).start()
            for dx in (1, 3, 2):
                ex(dx, (x + NX - dx) % NX).wait_recv()
                for dy in (2, 1, 3):
                    ey(dx, dy, y).start()

            def xwait(dx):
                ref = xr.at[pl.ds(((x + NX - dx) % NX) * LINKS, LINKS)]
                copy(ref, ref, fx_s.at[dx - 1], fx_r.at[dx - 1], at(dx=dx)).wait_recv()

            for dx in (1, 3, 2):
                xwait(dx)

            def tile(i, _):
                acc = jnp.zeros((16, TILE), jnp.float32)
                for k in range(K):
                    l = k * CT + i
                    got = xr[(tid[x * LINKS + l] // COL) * LINKS + l]
                    acc = acc + lax.dot_general(
                        got, cb[x * LINKS + i * K + k], (((1,), (1,)), ((), ())),
                        preferred_element_type=jnp.float32,
                    )
                ratio = (counts[:, pl.ds(pl.multiple_of(i * TILE, TILE), TILE)] / acc).astype(
                    jnp.bfloat16
                )
                for k in range(K):
                    sr[x * LINKS + k * CT + i] = jnp.dot(
                        ratio, cb[x * LINKS + i * K + k], preferred_element_type=jnp.float32
                    ).astype(jnp.bfloat16)
                return 0

            lax.fori_loop(0, LINKS // K, tile, 0, unroll=2)

            def scopy(dx, src_x):
                ref = sr.at[pl.ds(src_x * LINKS, LINKS)]
                return copy(ref, ref, rx_s.at[dx - 1], rx_r.at[dx - 1], at(dx=dx))

            for dx in (2, 1, 3):
                scopy(dx, x).start()
            th_sent()
            for dx in (1, 3, 2):
                scopy(dx, (x + NX - dx) % NX).wait_recv()
            for dx in (1, 2, 3):
                xcopy(dx).wait_send()
                scopy(dx, x).wait_send()
                ex(dx, x).wait_send()


        def pcopy_x(dx):
            return copy(
                pe.at[pl.ds(dx * CT, CT)], pr.at[pl.ds((dx - 1) * CT, CT)],
                pe_s.at[dx - 1], pe_r.at[dx - 1], at(dx=dx),
            )

        def qcopy(dx, src_x):
            ref = rt.at[pl.ds(src_x * CT, CT)]
            return copy(ref, ref, q_s.at[dx - 1], q_r.at[dx - 1], at(dx=dx))

        def by_sums():
            @pl.when(r == 1)
            def _():
                for dx in (1, 2, 3):
                    for dy in (1, 2, 3):
                        ey(dx, dy, (y + NY - dy) % NY).wait_recv()

            for dx in (2, 1, 3, 0):
                row = ((x + dx) % NX) * LINKS

                def part_sum(i, _, dx=dx, row=row):
                    acc = jnp.zeros((16, TILE), jnp.float32)
                    for k in range(K):
                        acc = acc + lax.dot_general(
                            th[mytile[row + k * CT + i]], cb[row + i * K + k],
                            (((1,), (1,)), ((), ())), preferred_element_type=jnp.float32,
                        )
                    pe[dx * CT + i] = acc
                    return 0

                lax.fori_loop(0, CT, part_sum, 0, unroll=4)
                if dx:
                    pcopy_x(dx).start()
            th_sent()
            for dx in (1, 3, 2):
                pcopy_x(dx).wait_recv()

            def ratio(i, _):
                acc = pe[i] + pr[i] + pr[CT + i] + pr[2 * CT + i]
                rt[x * CT + i] = (
                    counts[:, pl.ds(pl.multiple_of(i * TILE, TILE), TILE)] / acc
                ).astype(jnp.bfloat16)
                return 0

            lax.fori_loop(0, CT, ratio, 0, unroll=4)
            for dx in (2, 1, 3):
                qcopy(dx, x).start()
            for dx in (0, 1, 3, 2):
                src_x = (x + NX - dx) % NX
                if dx:
                    qcopy(dx, src_x).wait_recv()

                def shares(i, _, src_x=src_x):
                    for k in range(K):
                        sr[src_x * LINKS + k * CT + i] = jnp.dot(
                            rt[src_x * CT + i], cb[src_x * LINKS + i * K + k],
                            preferred_element_type=jnp.float32,
                        ).astype(jnp.bfloat16)
                    return 0

                lax.fori_loop(0, CT, shares, 0, unroll=4)
            for dx in (1, 2, 3):
                pcopy_x(dx).wait_send()
                qcopy(dx, x).wait_send()

            @pl.when(r == 1)
            def _():
                for dx in (1, 2, 3):
                    for dy in (1, 2, 3):
                        ey(dx, dy, y).wait_send()

        pl.when(r == 0)(by_tiles)
        pl.when(r > 0)(by_sums)

        def add(j, acc):
            acc = jnp.where(keep[j] > 0, acc, 0.0) + sr[perm[j]].astype(jnp.float32)
            cum[j] = acc
            return acc

        lax.fori_loop(0, COL, add, jnp.zeros((16, TILE), jnp.float32), unroll=8)

        def dense(core):
            def one(i, _):
                for t in range(TD):
                    g = (i * NC + core) * TD + t
                    d[core * HALF + i * TD + t] = cum[pos[g]]
                return 0

            lax.fori_loop(0, NZ, one, 0, unroll=4)

        dense(1 - c)
        rcopy = copy(
            d.at[pl.ds((1 - c) * HALF, HALF)], cr, rc_s.at[0], rc_r.at[0], at(dc=1)
        )
        rcopy.start()
        dense(c)
        rcopy.wait_recv()

        def join(i, _):
            d[c * HALF + i] = d[c * HALF + i] + cr[i]
            return 0

        lax.fori_loop(0, HALF, join, 0, unroll=8)

        def dz(off):
            return d.at[pl.ds(c * HALF + zrel(off) * TD, TD)]

        kinds = (0, STEP, -STEP)
        nsteps = [
            (j * 3 + k, way, way + kind)
            for j, way in enumerate(NEAR)
            for k, kind in enumerate(kinds)
        ] + [(12, 3, 8)]

        def ncopy(slot, way, dest):
            return copy(
                dz(dest), nr.at[pl.ds(slot * TD, TD)], rn_s.at[slot], rn_r.at[slot], at(dz=way)
            )

        def fcopy(j, way):
            return copy(
                sf.at[pl.ds(j * TD, TD)], fr.at[pl.ds(j * TD, TD)], rf_s.at[j], rf_r.at[j],
                at(dz=way),
            )

        order = [n for n in nsteps if n[0] % 3 or n[0] == 12] + [
            n for n in nsteps if n[0] % 3 == 0 and n[0] != 12
        ]
        for n in order:
            ncopy(*n).start()

        @pl.when(r == 0)
        def _():
            for j, (dx, dc) in enumerate(group):
                tg(j, dx, dc).wait_recv()
            s = tx[0]
            for j in range(len(group)):
                s = s + tx[1 + j]
            tot[...] = jnp.broadcast_to(jnp.sum(s, axis=1, keepdims=True), (16, TILE))

        def pcopy(kind, way, dy):
            j = (r * 3 + kind) * 3 + dy - 1
            return copy(ps.at[r * 3 + kind], pq.at[j], p_s.at[j], p_r.at[j], at(dz=way, dy=dy))

        def pool(kind, way, weight, sums):
            for t in range(TD):
                cols = slice(t * TILE, (t + 1) * TILE)
                part = weight(cols) * sums(t) / tot[...]
                ps[r * 3 + kind, :, cols] = jnp.sum(part, axis=0, keepdims=True)
            for dy in (2, 1, 3):
                pcopy(kind, way, dy).start()

        ways = ((0, 0), (1, STEP), (2, -STEP))
        for j, kind in relays:
            slots = [jj * 3 + 1 + j for jj in range(4)] + ([12] if j == 0 else [])
            for n in nsteps:
                if n[0] in slots:
                    ncopy(*n).wait_recv()
            for t in range(TD):
                acc = d[c * HALF + zrel(kind) * TD + t]
                for s in slots:
                    acc = acc + nr[s * TD + t]
                sf[j * TD + t] = acc
            fcopy(j, kind).start()
        for j, kind in relays:
            tcopy(1 - j, kind).wait_recv()
            pool(
                1 + j, kind, lambda cols, j=j: tf[r * 2 + 1 - j, :, cols],
                lambda t, j=j: sf[j * TD + t],
            )
        own = [jj * 3 for jj in range(4)]
        for n in nsteps:
            if n[0] in own:
                ncopy(*n).wait_recv()

        for t in range(TD):
            acc = d[c * HALF + z * TD + t]
            for i in own:
                acc = acc + nr[i * TD + t]
            sums[t] = acc
        pool(0, 0, lambda cols: theta[:, cols], lambda t: sums[t])
        for j, kind in relays:
            tcopy(j, kind).wait_send()
        fcopy(0, STEP).wait_recv()
        fcopy(1, -STEP).wait_recv()
        for t in range(TD):
            cols = slice(t * TILE, (t + 1) * TILE)
            updated = theta[:, cols] * (sums[t] + (fr[t] + fr[TD + t])) / tot[...]
            theta[:, cols] = updated
            rows[:, cols] = jnp.sum(updated, axis=0, keepdims=True)

        rcopy.wait_send()
        for n in nsteps:
            ncopy(*n).wait_send()
        fcopy(0, STEP).wait_send()
        fcopy(1, -STEP).wait_send()

        @pl.when(r == 0)
        def _():
            t_close()
            for j, (dx, dc) in enumerate(group):
                tg(j, dx, dc).wait_send()

        pooled = rows[...]
        for kind, way in ways:
            for dy in (1, 3, 2):
                pcopy(kind, way, dy).wait_recv()
                pooled = pooled + pq[(r * 3 + kind) * 3 + dy - 1]
        theta[...] = (1.0 - MIXING) * theta[...] + (MIXING / (16 * NY)) * pooled
        for kind, way in ways:
            for dy in (1, 2, 3):
                pcopy(kind, way, dy).wait_send()
        return carry

    lax.fori_loop(0, ITERS, sweep, 0)
    out[...] = theta[...] * 65536.0


def body(counts, compat, link_owner, link_local, start):
    hbm = pl.BlockSpec(memory_space=pltpu.HBM)
    vmem = pl.BlockSpec(memory_space=pltpu.VMEM)
    f32, bf16 = jnp.float32, jnp.bfloat16
    dma = pltpu.SemaphoreType.DMA

    def buf(n, dtype):
        return pltpu.VMEM((n, 16, TILE), dtype)

    return pl.pallas_call(
        em_kernel,
        out_shape=jax.ShapeDtypeStruct(start.shape, f32),
        in_specs=[hbm] * 5,
        out_specs=vmem,
        scratch_shapes=[
            pltpu.VMEM((K, CT), jnp.int32),
            pltpu.VMEM((K, CT), jnp.int32),
            pltpu.VMEM(counts.shape, f32),
            pltpu.VMEM((NX * LINKS, TILE, TILE), bf16),
            pltpu.VMEM((NX, 8, TILE), jnp.int32),
            pltpu.VMEM((8, TILE), jnp.int32),
            pltpu.VMEM((8, TILE), jnp.int32),
            pltpu.SMEM((8, TILE), jnp.int32),
            buf(COL + 1, bf16),
            buf(3 * LINKS, bf16),
            buf(NX * LINKS, bf16),
            buf(NX * LINKS, bf16),
            buf(COL + 1, f32),
            buf(COL, f32),
            buf(HALF, f32),
            buf(13 * TD, f32),
            buf(2 * TD, f32),
            buf(2 * TD, f32),
            buf(NZ, f32),
            buf(NX * NC, f32),
            pltpu.VMEM((16, TILE), f32),
            pltpu.VMEM((ITERS * 3, 1, TD * TILE), f32),
            pltpu.VMEM((16, TD * TILE), f32),
            dma((15,)), dma((15,)),
            dma((16,)), dma((16,)),
            dma((3,)), dma((3,)),
            dma((3,)), dma((3,)),
            dma((1,)), dma((1,)),
            dma((13,)), dma((13,)),
            dma((2,)), dma((2,)),
            dma((15,)), dma((15,)),
            dma((7,)), dma((7,)),
            dma((ITERS * 9,)), dma((ITERS * 9,)),
            dma((3,)), dma((3,)), dma((6,)),
            pltpu.VMEM((ITERS * 2, 16, TD * TILE), f32),
            dma((ITERS * 2,)), dma((ITERS * 2,)),
            pltpu.VMEM((ITERS * 9, 1, TD * TILE), f32),
            pltpu.VMEM((1, TD * TILE), f32),
            buf(TD, f32),
            buf(NX * CT, f32),
            buf(3 * CT, f32),
            buf(NX * CT, bf16),
            dma((3,)), dma((3,)),
            dma((9,)), dma((9,)),
            dma((3,)), dma((3,)),
            dma((3,)), dma((3,)),
        ],
        compiler_params=pltpu.CompilerParams(
            collective_id=0, has_side_effects=True, vmem_limit_bytes=60 << 20
        ),
        name="em_rounds",
    )(link_owner.T, link_local.T, counts, compat.reshape(LINKS, TILE, TILE), start)


def solution(mesh):
    placed = (
        P("smp", "cls"),
        P("cls", None, None, None),
        P("cls", None),
        P("cls", None),
        P("smp", "cls"),
    )
    return jax.shard_map(
        body, mesh=mesh, in_specs=placed, out_specs=P("smp", "cls"), check_vma=False
    )
```

```python
import functools

import jax
import jax.numpy as jnp
from jax import lax
from jax.experimental import pallas as pl
from jax.experimental.pallas import tpu as pltpu
from jax.sharding import PartitionSpec as P

TILE = 128
K = 4
ITERS = 3
MIXING = 0.3
MESH = pl.DeviceIdType.MESH
NX, NZ, NC, NY = 4, 16, 2, 4
TD = 4
CT = 8
LINKS = 32
COL = NZ * NC * TD
HALF = NZ * TD
FAR = (6, -6, 3, -3)
NEAR = (1, -1)


def em_kernel(
    owner_hbm, local_hbm, counts_hbm, compat_hbm, start_hbm, out,
    owner, local, counts, cb, tab, raw, lists, table, th, xs, xr, sr, cum, d, cr, nr, sf, fr, tt, tx, tot, ps, theta,
    fz_s, fz_r, fc_s, fc_r, fx_s, fx_r, rx_s, rx_r, rc_s, rc_r,
    rn_s, rn_r, rf_s, rf_r, tz_s, tz_r, tg_s, tg_r, p_s, p_r, l_s, l_r, in_s,
    sums, pe, pr, rt, ex_s, ex_r, ey_s, ey_r, pe_s, pe_r, q_s, q_r,
):
    tid, perm, keep, pos, mytile, place = (table.at[i] for i in range(6))
    me = lax.axis_index("cls")
    y = lax.axis_index("smp")
    c = me % NC
    z = (me // NC) % NZ
    x = me // (NC * NZ)

    turn = 1 - 2 * c

    zs = {off: lax.rem(z + turn * off + NZ, NZ) for off in range(-8, 9)}

    def zrel(off):
        return zs[off]

    devs = {}

    def at(dx=0, dz=0, dc=0, dy=0):
        return devs[(dx, dz, dc, dy)]

    def copy(src, dst, send, recv, dev):
        return pltpu.make_async_remote_copy(
            src_ref=src, dst_ref=dst, send_sem=send, recv_sem=recv,
            device_id=dev, device_id_type=MESH,
        )

    group = [(dx, dc) for dx in range(NX) for dc in range(NC) if (dx, dc) != (0, 0)]
    peers = [(0, o, 0, 0) for o in (1, -1, 2, -2) + FAR] + [(0, 0, 0, dy) for dy in (1, 2, 3)]
    peers += [(dx, 0, dc, 0) for dx, dc in group]
    for dx, dz, dc, dy in peers:
        devs[(dx, dz, dc, dy)] = (
            (lax.rem(x + dx, NX) * NZ + zs[dz]) * NC + lax.rem(c + dc, NC),
            lax.rem(y + dy, NY),
        )
    barrier = pltpu.get_barrier_semaphore()
    for peer in peers:
        pl.semaphore_signal(barrier, inc=1, device_id=at(*peer), device_id_type=MESH)
    loads = [
        pltpu.make_async_copy(a, b, in_s.at[i])
        for i, (a, b) in enumerate(
            (
                (start_hbm, theta),
                (counts_hbm, counts),
                (compat_hbm, cb.at[pl.ds(x * LINKS, LINKS)]),
                (owner_hbm, owner),
                (local_hbm, local),
            )
        )
    ]
    for load in loads:
        load.start()
    lane = lax.broadcasted_iota(jnp.int32, (8, TILE), 1)
    raw[...] = jnp.zeros((8, TILE), jnp.int32)
    loads[3].wait()
    loads[4].wait()
    raw[0:K, 0:CT] = owner[...] * TD + local[...]
    row = raw[0:1, :]
    for k in range(1, K):
        row = row + pltpu.roll(raw[k : k + 1, :], k * CT, 1)
    for j in (1, 2):
        row = row + pltpu.roll(row, j * LINKS, 1)
    tab[0] = jnp.where(lane // LINKS == x, jnp.broadcast_to(row, (8, TILE)), 0)
    pl.semaphore_wait(barrier, len(peers))

    def lcopy(dx):
        return copy(tab.at[0], tab.at[dx], l_s.at[dx - 1], l_r.at[dx - 1], at(dx=dx))

    for dx in (2, 1, 3):
        lcopy(dx).start()

    def make_lists():
        for dx in (1, 3, 2):
            lcopy(dx).wait_recv()
        whole = tab[0, 0:1] + tab[1, 0:1] + tab[2, 0:1] + tab[3, 0:1]
        key = jnp.where(whole // COL == x, whole % COL, COL)
        keys = jnp.broadcast_to(key, (TILE, TILE))
        mine = jnp.transpose(keys)
        j = lax.broadcasted_iota(jnp.int32, (TILE, TILE), 0)
        i = lax.broadcasted_iota(jnp.int32, (TILE, TILE), 1)
        before = jnp.where(keys < mine, 1, 0) + jnp.where((keys == mine) & (i < j), 1, 0)
        rank = jnp.sum(before, axis=1, keepdims=True)
        at_rank = rank == i
        order = jnp.sum(jnp.where(at_rank, j, 0), axis=0, keepdims=True)
        ranked = jnp.sum(jnp.where(at_rank, mine, 0), axis=0, keepdims=True)
        again = (ranked == pltpu.roll(ranked, 1, 1)) & (lane[0:1] > 0)
        upto = jnp.sum(jnp.where(mine <= i, 1, 0), axis=0, keepdims=True)
        some = jnp.sum(jnp.where(mine == i, 1, 0), axis=0, keepdims=True)
        lists[0:1, :] = whole
        lists[1:2, :] = order
        lists[2:3, :] = jnp.where(again, 1, 0)
        lists[3:4, :] = jnp.where(some > 0, upto - 1, COL)
        col = whole % COL
        lies = (col // TD) % NC * HALF + col // (TD * NC) * TD + col % TD
        lists[4:5, :] = jnp.where(key < COL, lies, COL)
        lists[5:6, :] = lies
        load = pltpu.make_async_copy(lists, table, in_s.at[5])
        load.start()
        load.wait()
        for dx in (1, 2, 3):
            lcopy(dx).wait_send()

    far = [(j, 0, o) for j, o in enumerate(FAR)]
    near_own = [(4 + j, 0, o) for j, o in enumerate(NEAR)]
    near_of = [[(6 + 2 * i + j, -w, o) for j, o in enumerate(NEAR)] for i, w in enumerate(FAR)]
    near_of[0].append((14, -FAR[0], 2))
    every = far + near_own + [step for steps in near_of for step in steps]

    def spread(blk, send, recv):
        def move(k, off, way):
            ref = blk(zrel(off))
            return copy(ref, ref, send.at[k], recv.at[k], at(dz=way))

        def take(k, off, way):
            ref = blk(zrel(off - way))
            copy(ref, ref, send.at[k], recv.at[k], at(dz=way)).wait_recv()

        def first():
            for k, off, way in far + near_own:
                move(k, off, way).start()

        def second():
            for i in (2, 3, 0, 1):
                take(*far[i])
                for step in near_of[i]:
                    move(*step).start()

        def third():
            for steps in [near_own] + [near_of[i] for i in (2, 3, 0, 1)]:
                for step in steps:
                    take(*step)

        def close():
            for step in every:
                move(*step).wait_send()

        return first, second, third, close

    def th_blk(zz):
        return th.at[pl.ds(c * HALF + zz * TD, TD)]

    def to_core(core):
        ref = th.at[pl.ds(core * HALF, HALF)]
        return copy(ref, ref, fc_s.at[0], fc_r.at[0], at(dc=1))

    f_first, f_second, f_third, f_close = spread(th_blk, fz_s, fz_r)
    t_first, t_second, t_third, t_close = spread(lambda zz: tt.at[zz], tz_s, tz_r)

    lists[...] = jnp.zeros((8, TILE), jnp.int32)
    loads[0].wait()
    cum[COL] = jnp.zeros((16, TILE), jnp.float32)
    th[COL] = jnp.zeros((16, TILE), jnp.bfloat16)

    def total_own():
        s = counts[:, 0:TILE]
        for i in range(1, counts.shape[1] // TILE):
            s = s + counts[:, i * TILE : (i + 1) * TILE]
        tt[z] = s

    def tg(j, dx, dc):
        return copy(tx.at[0], tx.at[1 + j], tg_s.at[j], tg_r.at[j], at(dx=dx, dc=dc))

    part = LINKS // NY

    def ex(dx, src_x):
        ref = cb.at[pl.ds(src_x * LINKS + y * part, part)]
        return copy(ref, ref, ex_s.at[dx - 1], ex_r.at[dx - 1], at(dx=dx))

    def ey(dx, dy, src_y):
        ref = cb.at[pl.ds(((x + NX - dx) % NX) * LINKS + src_y * part, part)]
        j = (dx - 1) * 3 + dy - 1
        return copy(ref, ref, ey_s.at[j], ey_r.at[j], at(dy=dy))

    def sweep(r, carry):
        for t in range(TD):
            th[c * HALF + z * TD + t] = theta[:, t * TILE : (t + 1) * TILE].astype(jnp.bfloat16)
        f_first()

        @pl.when(r == 0)
        def _():
            loads[1].wait()
            total_own()
            t_first()
            loads[2].wait()
            for dx in (2, 1, 3):
                ex(dx, x).start()
            make_lists()

        f_second()

        @pl.when(r == 0)
        def _():
            t_second()

        f_third()

        to_core(c).start()
        to_core(1 - c).wait_recv()

        def xcopy(dx):
            return copy(
                xs.at[pl.ds((dx - 1) * LINKS, LINKS)],
                xr.at[pl.ds(x * LINKS, LINKS)],
                fx_s.at[dx - 1],
                fx_r.at[dx - 1],
                at(dx=dx),
            )

        def th_sent():
            f_close()
            to_core(c).wait_send()

        def by_tiles():
            for dx in (2, 1, 3):
                row = ((x + dx) % NX) * LINKS

                def pick(l, _, dx=dx, row=row):
                    xs[(dx - 1) * LINKS + l] = th[place[row + l]]
                    return 0

                lax.fori_loop(0, LINKS, pick, 0, unroll=8)
                xcopy(dx).start()

            def pick_own(l, _):
                xr[x * LINKS + l] = th[place[x * LINKS + l]]
                return 0

            lax.fori_loop(0, LINKS, pick_own, 0, unroll=8)

            t_third()
            s = tt[0]
            for i in range(1, NZ):
                s = s + tt[i]
            tx[0] = s
            for j, (dx, dc) in enumerate(group):
                tg(j, dx, dc).start()
            for dx in (1, 3, 2):
                ex(dx, (x + NX - dx) % NX).wait_recv()
                for dy in (2, 1, 3):
                    ey(dx, dy, y).start()

            def xwait(dx):
                ref = xr.at[pl.ds(((x + NX - dx) % NX) * LINKS, LINKS)]
                copy(ref, ref, fx_s.at[dx - 1], fx_r.at[dx - 1], at(dx=dx)).wait_recv()

            for dx in (1, 3, 2):
                xwait(dx)

            def tile(i, _):
                acc = jnp.zeros((16, TILE), jnp.float32)
                for k in range(K):
                    l = k * CT + i
                    got = xr[(tid[x * LINKS + l] // COL) * LINKS + l]
                    acc = acc + lax.dot_general(
                        got, cb[x * LINKS + i * K + k], (((1,), (1,)), ((), ())),
                        preferred_element_type=jnp.float32,
                    )
                ratio = (counts[:, pl.ds(pl.multiple_of(i * TILE, TILE), TILE)] / acc).astype(
                    jnp.bfloat16
                )
                for k in range(K):
                    sr[x * LINKS + k * CT + i] = jnp.dot(
                        ratio, cb[x * LINKS + i * K + k], preferred_element_type=jnp.float32
                    ).astype(jnp.bfloat16)
                return 0

            lax.fori_loop(0, LINKS // K, tile, 0, unroll=2)

            def scopy(dx, src_x):
                ref = sr.at[pl.ds(src_x * LINKS, LINKS)]
                return copy(ref, ref, rx_s.at[dx - 1], rx_r.at[dx - 1], at(dx=dx))

            for dx in (2, 1, 3):
                scopy(dx, x).start()
            th_sent()
            for dx in (1, 3, 2):
                scopy(dx, (x + NX - dx) % NX).wait_recv()
            for dx in (1, 2, 3):
                xcopy(dx).wait_send()
                scopy(dx, x).wait_send()
                ex(dx, x).wait_send()


        def pcopy_x(dx):
            return copy(
                pe.at[pl.ds(dx * CT, CT)], pr.at[pl.ds((dx - 1) * CT, CT)],
                pe_s.at[dx - 1], pe_r.at[dx - 1], at(dx=dx),
            )

        def qcopy(dx, src_x):
            ref = rt.at[pl.ds(src_x * CT, CT)]
            return copy(ref, ref, q_s.at[dx - 1], q_r.at[dx - 1], at(dx=dx))

        def by_sums():
            @pl.when(r == 1)
            def _():
                for dx in (1, 2, 3):
                    for dy in (1, 2, 3):
                        ey(dx, dy, (y + NY - dy) % NY).wait_recv()

            for dx in (2, 1, 3, 0):
                row = ((x + dx) % NX) * LINKS

                def part_sum(i, _, dx=dx, row=row):
                    acc = jnp.zeros((16, TILE), jnp.float32)
                    for k in range(K):
                        acc = acc + lax.dot_general(
                            th[mytile[row + k * CT + i]], cb[row + i * K + k],
                            (((1,), (1,)), ((), ())), preferred_element_type=jnp.float32,
                        )
                    pe[dx * CT + i] = acc
                    return 0

                lax.fori_loop(0, CT, part_sum, 0, unroll=4)
                if dx:
                    pcopy_x(dx).start()
            th_sent()
            for dx in (1, 3, 2):
                pcopy_x(dx).wait_recv()

            def ratio(i, _):
                acc = pe[i] + pr[i] + pr[CT + i] + pr[2 * CT + i]
                rt[x * CT + i] = (
                    counts[:, pl.ds(pl.multiple_of(i * TILE, TILE), TILE)] / acc
                ).astype(jnp.bfloat16)
                return 0

            lax.fori_loop(0, CT, ratio, 0, unroll=4)
            for dx in (2, 1, 3):
                qcopy(dx, x).start()
            for dx in (0, 1, 3, 2):
                src_x = (x + NX - dx) % NX
                if dx:
                    qcopy(dx, src_x).wait_recv()

                def shares(i, _, src_x=src_x):
                    for k in range(K):
                        sr[src_x * LINKS + k * CT + i] = jnp.dot(
                            rt[src_x * CT + i], cb[src_x * LINKS + i * K + k],
                            preferred_element_type=jnp.float32,
                        ).astype(jnp.bfloat16)
                    return 0

                lax.fori_loop(0, CT, shares, 0, unroll=4)
            for dx in (1, 2, 3):
                pcopy_x(dx).wait_send()
                qcopy(dx, x).wait_send()

            @pl.when(r == 1)
            def _():
                for dx in (1, 2, 3):
                    for dy in (1, 2, 3):
                        ey(dx, dy, y).wait_send()

        pl.when(r == 0)(by_tiles)
        pl.when(r > 0)(by_sums)

        def add(j, acc):
            acc = jnp.where(keep[j] > 0, acc, 0.0) + sr[perm[j]].astype(jnp.float32)
            cum[j] = acc
            return acc

        lax.fori_loop(0, COL, add, jnp.zeros((16, TILE), jnp.float32), unroll=8)

        def dense(core):
            def one(i, _):
                for t in range(TD):
                    g = (i * NC + core) * TD + t
                    d[core * HALF + i * TD + t] = cum[pos[g]]
                return 0

            lax.fori_loop(0, NZ, one, 0, unroll=4)

        dense(1 - c)
        rcopy = copy(
            d.at[pl.ds((1 - c) * HALF, HALF)], cr, rc_s.at[0], rc_r.at[0], at(dc=1)
        )
        rcopy.start()
        dense(c)
        rcopy.wait_recv()

        def join(i, _):
            d[c * HALF + i] = d[c * HALF + i] + cr[i]
            return 0

        lax.fori_loop(0, HALF, join, 0, unroll=8)

        def dz(off):
            return d.at[pl.ds(c * HALF + zrel(off) * TD, TD)]

        kinds = (0,) + FAR
        nsteps = [
            [(q * 2 + j, way, way + kind) for j, way in enumerate(NEAR)]
            for q, kind in enumerate(kinds)
        ]
        nsteps[1].append((10, 2, 8))

        def ncopy(slot, way, dest):
            return copy(
                dz(dest), nr.at[pl.ds(slot * TD, TD)], rn_s.at[slot], rn_r.at[slot], at(dz=way)
            )

        def fcopy(j, way):
            return copy(
                sf.at[pl.ds(j * TD, TD)], fr.at[pl.ds(j * TD, TD)], rf_s.at[j], rf_r.at[j],
                at(dz=way),
            )

        for q in (1, 2, 3, 4):
            for n in nsteps[q]:
                ncopy(*n).start()

        @pl.when(r == 0)
        def _():
            for j, (dx, dc) in enumerate(group):
                tg(j, dx, dc).wait_recv()
            s = tx[0]
            for j in range(len(group)):
                s = s + tx[1 + j]
            tot[...] = jnp.broadcast_to(jnp.sum(s, axis=1, keepdims=True), (16, TILE))

        for q, kind in enumerate(kinds):
            if q == 0:
                continue
            for n in nsteps[q]:
                ncopy(*n).wait_recv()
            for t in range(TD):
                acc = d[c * HALF + zrel(kind) * TD + t]
                for n in nsteps[q]:
                    acc = acc + nr[n[0] * TD + t]
                sf[(q - 1) * TD + t] = acc
            fcopy(q - 1, kind).start()
            if q == 2:
                for n in nsteps[0]:
                    ncopy(*n).start()
        for n in nsteps[0]:
            ncopy(*n).wait_recv()
        for t in range(TD):
            acc = d[c * HALF + z * TD + t]
            for n in nsteps[0]:
                acc = acc + nr[n[0] * TD + t]
            sums[t] = acc
        for j in (2, 3, 0, 1):
            fcopy(j, FAR[j]).wait_recv()
        for t in range(TD):
            cols = slice(t * TILE, (t + 1) * TILE)
            acc = sums[t] + ((fr[t] + fr[TD + t]) + (fr[2 * TD + t] + fr[3 * TD + t]))
            updated = theta[:, cols] * acc / tot[...]
            theta[:, cols] = updated
            ps[r * NY, :, cols] = jnp.sum(updated, axis=0, keepdims=True)

        def pcopy(dy):
            j = r * 3 + dy - 1
            return copy(ps.at[r * NY], ps.at[r * NY + dy], p_s.at[j], p_r.at[j], at(dy=dy))

        for dy in (2, 1, 3):
            pcopy(dy).start()
        rcopy.wait_send()
        for steps in nsteps:
            for n in steps:
                ncopy(*n).wait_send()
        for j, way in enumerate(FAR):
            fcopy(j, way).wait_send()

        @pl.when(r == 0)
        def _():
            t_close()
            for j, (dx, dc) in enumerate(group):
                tg(j, dx, dc).wait_send()

        for dy in (1, 3, 2):
            pcopy(dy).wait_recv()
        pooled = ps[r * NY] + ps[r * NY + 1] + ps[r * NY + 2] + ps[r * NY + 3]
        theta[...] = (1.0 - MIXING) * theta[...] + (MIXING / (16 * NY)) * pooled
        for dy in (1, 2, 3):
            pcopy(dy).wait_send()
        return carry

    lax.fori_loop(0, ITERS, sweep, 0)
    out[...] = theta[...] * 65536.0


def body(counts, compat, link_owner, link_local, start):
    hbm = pl.BlockSpec(memory_space=pltpu.HBM)
    vmem = pl.BlockSpec(memory_space=pltpu.VMEM)
    f32, bf16 = jnp.float32, jnp.bfloat16
    dma = pltpu.SemaphoreType.DMA

    def buf(n, dtype):
        return pltpu.VMEM((n, 16, TILE), dtype)

    return pl.pallas_call(
        em_kernel,
        out_shape=jax.ShapeDtypeStruct(start.shape, f32),
        in_specs=[hbm] * 5,
        out_specs=vmem,
        scratch_shapes=[
            pltpu.VMEM((K, CT), jnp.int32),
            pltpu.VMEM((K, CT), jnp.int32),
            pltpu.VMEM(counts.shape, f32),
            pltpu.VMEM((NX * LINKS, TILE, TILE), bf16),
            pltpu.VMEM((NX, 8, TILE), jnp.int32),
            pltpu.VMEM((8, TILE), jnp.int32),
            pltpu.VMEM((8, TILE), jnp.int32),
            pltpu.SMEM((8, TILE), jnp.int32),
            buf(COL + 1, bf16),
            buf(3 * LINKS, bf16),
            buf(NX * LINKS, bf16),
            buf(NX * LINKS, bf16),
            buf(COL + 1, f32),
            buf(COL, f32),
            buf(HALF, f32),
            buf(11 * TD, f32),
            buf(4 * TD, f32),
            buf(4 * TD, f32),
            buf(NZ, f32),
            buf(NX * NC, f32),
            pltpu.VMEM((16, TILE), f32),
            pltpu.VMEM((ITERS * NY, 1, TD * TILE), f32),
            pltpu.VMEM((16, TD * TILE), f32),
            dma((15,)), dma((15,)),
            dma((1,)), dma((1,)),
            dma((3,)), dma((3,)),
            dma((3,)), dma((3,)),
            dma((1,)), dma((1,)),
            dma((11,)), dma((11,)),
            dma((4,)), dma((4,)),
            dma((15,)), dma((15,)),
            dma((7,)), dma((7,)),
            dma((ITERS * 3,)), dma((ITERS * 3,)),
            dma((3,)), dma((3,)), dma((6,)),
            buf(TD, f32),
            buf(NX * CT, f32),
            buf(3 * CT, f32),
            buf(NX * CT, bf16),
            dma((3,)), dma((3,)),
            dma((9,)), dma((9,)),
            dma((3,)), dma((3,)),
            dma((3,)), dma((3,)),
        ],
        compiler_params=pltpu.CompilerParams(
            collective_id=0, has_side_effects=True, vmem_limit_bytes=60 << 20
        ),
        name="em_rounds",
    )(link_owner.T, link_local.T, counts, compat.reshape(LINKS, TILE, TILE), start)


def solution(mesh):
    placed = (
        P("smp", "cls"),
        P("cls", None, None, None),
        P("cls", None),
        P("cls", None),
        P("smp", "cls"),
    )
    return jax.shard_map(
        body, mesh=mesh, in_specs=placed, out_specs=P("smp", "cls"), check_vma=False
    )
```

```python
import functools

import jax
import jax.numpy as jnp
from jax import lax
from jax.experimental import pallas as pl
from jax.experimental.pallas import tpu as pltpu
from jax.sharding import PartitionSpec as P

TILE = 128
K = 4
ITERS = 3
MIXING = 0.3
MESH = pl.DeviceIdType.MESH
NX, NZ, NC, NY = 4, 16, 2, 4
TD = 4
CT = 8
LINKS = 32
COL = NZ * NC * TD
HALF = NZ * TD
FAR = (6, -6, 3, -3)
NEAR = (1, -1)
PLACES = (5, 6, 7, 8, -7, -6, -5, 2, 3, 4, -4, -3, -2, -1, 0, 1)
GROUPS = ((0, 4), (4, 3), (7, 3), (10, 3), (13, 3))


def em_kernel(
    owner_hbm, local_hbm, counts_hbm, compat_hbm, start_hbm, out,
    owner, local, counts, cb, tab, raw, lists, table, th, xs, xr, sr, cum, d, cr, nr, sf, fr, tt, tx, tot, ps, theta,
    fz_s, fz_r, fc_s, fc_r, fx_s, fx_r, rx_s, rx_r, rc_s, rc_r,
    rn_s, rn_r, rf_s, rf_r, tz_s, tz_r, tg_s, tg_r, p_s, p_r, l_s, l_r, in_s,
    sums, pe, pr, rt, ex_s, ex_r, ey_s, ey_r, pe_s, pe_r, q_s, q_r,
):
    tid, perm, keep, pos, mytile, place = (table.at[i] for i in range(6))
    me = lax.axis_index("cls")
    y = lax.axis_index("smp")
    c = me % NC
    z = (me // NC) % NZ
    x = me // (NC * NZ)

    turn = 1 - 2 * c

    zs = {off: lax.rem(z + turn * off + NZ, NZ) for off in range(-8, 9)}

    def zrel(off):
        return zs[off]

    devs = {}

    def at(dx=0, dz=0, dc=0, dy=0):
        return devs[(dx, dz, dc, dy)]

    def copy(src, dst, send, recv, dev):
        return pltpu.make_async_remote_copy(
            src_ref=src, dst_ref=dst, send_sem=send, recv_sem=recv,
            device_id=dev, device_id_type=MESH,
        )

    group = [(dx, dc) for dx in range(NX) for dc in range(NC) if (dx, dc) != (0, 0)]
    peers = [(0, o, 0, 0) for o in (1, -1, 2, -2) + FAR] + [(0, 0, 0, dy) for dy in (1, 2, 3)]
    peers += [(dx, 0, dc, 0) for dx, dc in group]
    for dx, dz, dc, dy in peers:
        devs[(dx, dz, dc, dy)] = (
            (lax.rem(x + dx, NX) * NZ + zs[dz]) * NC + lax.rem(c + dc, NC),
            lax.rem(y + dy, NY),
        )
    barrier = pltpu.get_barrier_semaphore()
    for peer in peers:
        pl.semaphore_signal(barrier, inc=1, device_id=at(*peer), device_id_type=MESH)
    loads = [
        pltpu.make_async_copy(a, b, in_s.at[i])
        for i, (a, b) in enumerate(
            (
                (start_hbm, theta),
                (counts_hbm, counts),
                (compat_hbm, cb.at[pl.ds(x * LINKS, LINKS)]),
                (owner_hbm, owner),
                (local_hbm, local),
            )
        )
    ]
    for load in loads:
        load.start()
    lane = lax.broadcasted_iota(jnp.int32, (8, TILE), 1)
    raw[...] = jnp.zeros((8, TILE), jnp.int32)
    loads[3].wait()
    loads[4].wait()
    raw[0:K, 0:CT] = owner[...] * TD + local[...]
    row = raw[0:1, :]
    for k in range(1, K):
        row = row + pltpu.roll(raw[k : k + 1, :], k * CT, 1)
    for j in (1, 2):
        row = row + pltpu.roll(row, j * LINKS, 1)
    tab[0] = jnp.where(lane // LINKS == x, jnp.broadcast_to(row, (8, TILE)), 0)
    pl.semaphore_wait(barrier, len(peers))

    def lcopy(dx):
        return copy(tab.at[0], tab.at[dx], l_s.at[dx - 1], l_r.at[dx - 1], at(dx=dx))

    for dx in (2, 1, 3):
        lcopy(dx).start()

    def load_lists():
        return pltpu.make_async_copy(lists, table, in_s.at[5])

    def make_lists():
        for dx in (1, 3, 2):
            lcopy(dx).wait_recv()
        whole = tab[0, 0:1] + tab[1, 0:1] + tab[2, 0:1] + tab[3, 0:1]
        key = jnp.where(whole // COL == x, whole % COL, COL)
        keys = jnp.broadcast_to(key, (TILE, TILE))
        mine = jnp.transpose(keys)
        j = lax.broadcasted_iota(jnp.int32, (TILE, TILE), 0)
        i = lax.broadcasted_iota(jnp.int32, (TILE, TILE), 1)
        before = jnp.where(keys < mine, 1, 0) + jnp.where((keys == mine) & (i < j), 1, 0)
        rank = jnp.sum(before, axis=1, keepdims=True)
        at_rank = rank == i
        order = jnp.sum(jnp.where(at_rank, j, 0), axis=0, keepdims=True)
        ranked = jnp.sum(jnp.where(at_rank, mine, 0), axis=0, keepdims=True)
        again = (ranked == pltpu.roll(ranked, 1, 1)) & (lane[0:1] > 0)
        upto = jnp.sum(jnp.where(mine <= i, 1, 0), axis=0, keepdims=True)
        some = jnp.sum(jnp.where(mine == i, 1, 0), axis=0, keepdims=True)
        lists[0:1, :] = whole
        lists[1:2, :] = order
        lists[2:3, :] = jnp.where(again, 1, 0)
        lists[3:4, :] = jnp.where(some > 0, upto - 1, COL)
        col = whole % COL
        lies = (col // TD) % NC * HALF + col // (TD * NC) * TD + col % TD
        lists[4:5, :] = jnp.where(key < COL, lies, COL)
        lists[5:6, :] = lies
        load = load_lists()
        load.start()

    far = [(j, 0, o) for j, o in enumerate(FAR)]
    near_own = [(4 + j, 0, o) for j, o in enumerate(NEAR)]
    near_of = [[(6 + 2 * i + j, -w, o) for j, o in enumerate(NEAR)] for i, w in enumerate(FAR)]
    near_of[0].append((14, -FAR[0], 2))
    every = far + near_own + [step for steps in near_of for step in steps]

    def spread(blk, send, recv):
        def move(k, off, way):
            ref = blk(zrel(off))
            return copy(ref, ref, send.at[k], recv.at[k], at(dz=way))

        def take(k, off, way):
            ref = blk(zrel(off - way))
            copy(ref, ref, send.at[k], recv.at[k], at(dz=way)).wait_recv()

        def first():
            for k, off, way in far + near_own:
                move(k, off, way).start()

        def second():
            for i in (2, 3, 0, 1):
                take(*far[i])
                for step in near_of[i]:
                    move(*step).start()

        def third():
            for steps in [near_own] + [near_of[i] for i in (2, 3, 0, 1)]:
                for step in steps:
                    take(*step)

        def close():
            for step in every:
                move(*step).wait_send()

        return first, second, third, close

    def th_blk(zz):
        return th.at[pl.ds(c * HALF + zz * TD, TD)]

    def to_core(core):
        ref = th.at[pl.ds(core * HALF, HALF)]
        return copy(ref, ref, fc_s.at[0], fc_r.at[0], at(dc=1))

    f_first, f_second, f_third, f_close = spread(th_blk, fz_s, fz_r)
    t_first, t_second, t_third, t_close = spread(lambda zz: tt.at[zz], tz_s, tz_r)

    lists[...] = jnp.zeros((8, TILE), jnp.int32)
    loads[0].wait()
    cum[COL] = jnp.zeros((16, TILE), jnp.float32)
    th[COL] = jnp.zeros((16, TILE), jnp.bfloat16)

    def total_own():
        s = counts[:, 0:TILE]
        for i in range(1, counts.shape[1] // TILE):
            s = s + counts[:, i * TILE : (i + 1) * TILE]
        tt[z] = s

    def tg(j, dx, dc):
        return copy(tx.at[0], tx.at[1 + j], tg_s.at[j], tg_r.at[j], at(dx=dx, dc=dc))

    part = LINKS // NY

    def ex(dx, src_x):
        ref = cb.at[pl.ds(src_x * LINKS + y * part, part)]
        return copy(ref, ref, ex_s.at[dx - 1], ex_r.at[dx - 1], at(dx=dx))

    def ey(dx, dy, src_y):
        ref = cb.at[pl.ds(((x + NX - dx) % NX) * LINKS + src_y * part, part)]
        j = (dx - 1) * 3 + dy - 1
        return copy(ref, ref, ey_s.at[j], ey_r.at[j], at(dy=dy))

    def sweep(r, carry):
        for t in range(TD):
            th[c * HALF + z * TD + t] = theta[:, t * TILE : (t + 1) * TILE].astype(jnp.bfloat16)
        f_first()

        @pl.when(r == 0)
        def _():
            loads[1].wait()
            total_own()
            loads[2].wait()
            for dx in (2, 1, 3):
                ex(dx, x).start()
            make_lists()

        f_second()

        f_third()

        to_core(c).start()
        to_core(1 - c).wait_recv()

        def xcopy(dx):
            return copy(
                xs.at[pl.ds((dx - 1) * LINKS, LINKS)],
                xr.at[pl.ds(x * LINKS, LINKS)],
                fx_s.at[dx - 1],
                fx_r.at[dx - 1],
                at(dx=dx),
            )

        def th_sent():
            f_close()
            to_core(c).wait_send()

        def expect(tiles, at_row):
            weights = jnp.concatenate([cb[at_row + k] for k in range(K)], axis=1)
            return lax.dot_general(
                jnp.concatenate(tiles, axis=1), weights, (((1,), (1,)), ((), ())),
                preferred_element_type=jnp.float32,
            )

        def share(src_x, i, ratio):
            row = src_x * LINKS + i * K
            weights = jnp.concatenate([cb[row + k] for k in range(K)], axis=1)
            got = jnp.dot(ratio, weights, preferred_element_type=jnp.float32)
            for k in range(K):
                sr[src_x * LINKS + k * CT + i] = got[:, k * TILE : (k + 1) * TILE].astype(
                    jnp.bfloat16
                )

        def by_tiles():
            load_lists().wait()
            for dx in (2, 1, 3):
                row = ((x + dx) % NX) * LINKS

                def pick(l, _, dx=dx, row=row):
                    xs[(dx - 1) * LINKS + l] = th[place[row + l]]
                    return 0

                lax.fori_loop(0, LINKS, pick, 0, unroll=8)
                xcopy(dx).start()

            def pick_own(l, _):
                xr[x * LINKS + l] = th[place[x * LINKS + l]]
                return 0

            lax.fori_loop(0, LINKS, pick_own, 0, unroll=8)

            t_first()
            for dx in (1, 3, 2):
                ex(dx, (x + NX - dx) % NX).wait_recv()
                for dy in (2, 1, 3):
                    ey(dx, dy, y).start()

            def xwait(dx):
                ref = xr.at[pl.ds(((x + NX - dx) % NX) * LINKS, LINKS)]
                copy(ref, ref, fx_s.at[dx - 1], fx_r.at[dx - 1], at(dx=dx)).wait_recv()

            for dx in (1, 3, 2):
                xwait(dx)

            def tile(i, _):
                links = [k * CT + i for k in range(K)]
                acc = expect(
                    [xr[(tid[x * LINKS + l] // COL) * LINKS + l] for l in links], x * LINKS + i * K
                )
                ratio = (counts[:, pl.ds(pl.multiple_of(i * TILE, TILE), TILE)] / acc).astype(
                    jnp.bfloat16
                )
                share(x, i, ratio)
                return 0

            lax.fori_loop(0, LINKS // K, tile, 0, unroll=2)

            def scopy(dx, src_x):
                ref = sr.at[pl.ds(src_x * LINKS, LINKS)]
                return copy(ref, ref, rx_s.at[dx - 1], rx_r.at[dx - 1], at(dx=dx))

            for dx in (2, 1, 3):
                scopy(dx, x).start()
            th_sent()
            t_second()
            t_third()
            s = tt[0]
            for i in range(1, NZ):
                s = s + tt[i]
            tx[0] = s
            for j, (dx, dc) in enumerate(group):
                tg(j, dx, dc).start()
            for dx in (1, 3, 2):
                scopy(dx, (x + NX - dx) % NX).wait_recv()
            for dx in (1, 2, 3):
                xcopy(dx).wait_send()
                scopy(dx, x).wait_send()
                ex(dx, x).wait_send()
                lcopy(dx).wait_send()


        def pcopy_x(dx):
            return copy(
                pe.at[pl.ds(dx * CT, CT)], pr.at[pl.ds((dx - 1) * CT, CT)],
                pe_s.at[dx - 1], pe_r.at[dx - 1], at(dx=dx),
            )

        def qcopy(dx, src_x):
            ref = rt.at[pl.ds(src_x * CT, CT)]
            return copy(ref, ref, q_s.at[dx - 1], q_r.at[dx - 1], at(dx=dx))

        def by_sums():
            @pl.when(r == 1)
            def _():
                for dx in (1, 2, 3):
                    for dy in (1, 2, 3):
                        ey(dx, dy, (y + NY - dy) % NY).wait_recv()

            for dx in (2, 1, 3, 0):
                row = ((x + dx) % NX) * LINKS

                def part_sum(i, _, dx=dx, row=row):
                    pe[dx * CT + i] = expect(
                        [th[mytile[row + k * CT + i]] for k in range(K)], row + i * K
                    )
                    return 0

                lax.fori_loop(0, CT, part_sum, 0, unroll=4)
                if dx:
                    pcopy_x(dx).start()
            th_sent()
            for dx in (1, 3, 2):
                pcopy_x(dx).wait_recv()

            def ratio(i, _):
                acc = pe[i] + pr[i] + pr[CT + i] + pr[2 * CT + i]
                rt[x * CT + i] = (
                    counts[:, pl.ds(pl.multiple_of(i * TILE, TILE), TILE)] / acc
                ).astype(jnp.bfloat16)
                return 0

            lax.fori_loop(0, CT, ratio, 0, unroll=4)
            for dx in (2, 1, 3):
                qcopy(dx, x).start()
            for dx in (0, 1, 3, 2):
                src_x = (x + NX - dx) % NX
                if dx:
                    qcopy(dx, src_x).wait_recv()

                def shares(i, _, src_x=src_x):
                    share(src_x, i, rt[src_x * CT + i])
                    return 0

                lax.fori_loop(0, CT, shares, 0, unroll=4)
            for dx in (1, 2, 3):
                pcopy_x(dx).wait_send()
                qcopy(dx, x).wait_send()

            @pl.when(r == 1)
            def _():
                for dx in (1, 2, 3):
                    for dy in (1, 2, 3):
                        ey(dx, dy, y).wait_send()

        pl.when(r == 0)(by_tiles)
        pl.when(r > 0)(by_sums)

        def add(j, acc):
            acc = jnp.where(keep[j] > 0, acc, 0.0) + sr[perm[j]].astype(jnp.float32)
            cum[j] = acc
            return acc

        lax.fori_loop(0, COL, add, jnp.zeros((16, TILE), jnp.float32), unroll=8)

        def dense(core, off_sign, first, count):
            for p in range(first, first + count):
                zz = zs[off_sign * PLACES[p]]
                for t in range(TD):
                    d[core * HALF + p * TD + t] = cum[pos[(zz * NC + core) * TD + t]]

        def rcopy(g):
            first, count = GROUPS[g]
            return copy(
                d.at[pl.ds((1 - c) * HALF + first * TD, count * TD)],
                cr.at[pl.ds(first * TD, count * TD)], rc_s.at[g], rc_r.at[g], at(dc=1),
            )

        for g, (first, count) in enumerate(GROUPS):
            dense(1 - c, -1, first, count)
            rcopy(g).start()
        for first, count in GROUPS:
            dense(c, 1, first, count)

        def dz(off):
            return d.at[pl.ds(c * HALF + PLACES.index(off) * TD, TD)]

        kinds = (0,) + FAR
        nsteps = [
            [(q * 2 + j, way, way + kind) for j, way in enumerate(NEAR)]
            for q, kind in enumerate(kinds)
        ]
        nsteps[1].append((10, 2, 8))

        def ncopy(slot, way, dest):
            return copy(
                dz(dest), nr.at[pl.ds(slot * TD, TD)], rn_s.at[slot], rn_r.at[slot], at(dz=way)
            )

        def fcopy(j, way):
            return copy(
                sf.at[pl.ds(j * TD, TD)], fr.at[pl.ds(j * TD, TD)], rf_s.at[j], rf_r.at[j],
                at(dz=way),
            )

        for g, q in enumerate((1, 2, 3, 4, 0)):
            rcopy(g).wait_recv()
            first, count = GROUPS[g]
            for i in range(first * TD, (first + count) * TD):
                d[c * HALF + i] = d[c * HALF + i] + cr[i]
            for n in nsteps[q]:
                ncopy(*n).start()

        @pl.when(r == 0)
        def _():
            for j, (dx, dc) in enumerate(group):
                tg(j, dx, dc).wait_recv()
            s = tx[0]
            for j in range(len(group)):
                s = s + tx[1 + j]
            tot[...] = jnp.broadcast_to(jnp.sum(s, axis=1, keepdims=True), (16, TILE))

        for q, kind in enumerate(kinds):
            if q == 0:
                continue
            for n in nsteps[q]:
                ncopy(*n).wait_recv()
            for t in range(TD):
                acc = d[c * HALF + PLACES.index(kind) * TD + t]
                for n in nsteps[q]:
                    acc = acc + nr[n[0] * TD + t]
                sf[(q - 1) * TD + t] = acc
            fcopy(q - 1, kind).start()
        for n in nsteps[0]:
            ncopy(*n).wait_recv()
        for t in range(TD):
            acc = d[c * HALF + PLACES.index(0) * TD + t]
            for n in nsteps[0]:
                acc = acc + nr[n[0] * TD + t]
            sums[t] = acc
        for j in (2, 3, 0, 1):
            fcopy(j, FAR[j]).wait_recv()
        for t in range(TD):
            cols = slice(t * TILE, (t + 1) * TILE)
            acc = sums[t] + ((fr[t] + fr[TD + t]) + (fr[2 * TD + t] + fr[3 * TD + t]))
            updated = theta[:, cols] * acc / tot[...]
            theta[:, cols] = updated
            ps[r * NY, :, cols] = jnp.sum(updated, axis=0, keepdims=True)

        def pcopy(dy):
            j = r * 3 + dy - 1
            return copy(ps.at[r * NY], ps.at[r * NY + dy], p_s.at[j], p_r.at[j], at(dy=dy))

        for dy in (2, 1, 3):
            pcopy(dy).start()
        for g in range(len(GROUPS)):
            rcopy(g).wait_send()
        for steps in nsteps:
            for n in steps:
                ncopy(*n).wait_send()
        for j, way in enumerate(FAR):
            fcopy(j, way).wait_send()

        @pl.when(r == 0)
        def _():
            t_close()
            for j, (dx, dc) in enumerate(group):
                tg(j, dx, dc).wait_send()

        for dy in (1, 3, 2):
            pcopy(dy).wait_recv()
        pooled = ps[r * NY] + ps[r * NY + 1] + ps[r * NY + 2] + ps[r * NY + 3]
        theta[...] = (1.0 - MIXING) * theta[...] + (MIXING / (16 * NY)) * pooled
        for dy in (1, 2, 3):
            pcopy(dy).wait_send()
        return carry

    lax.fori_loop(0, ITERS, sweep, 0)
    out[...] = theta[...] * 65536.0


def body(counts, compat, link_owner, link_local, start):
    hbm = pl.BlockSpec(memory_space=pltpu.HBM)
    vmem = pl.BlockSpec(memory_space=pltpu.VMEM)
    f32, bf16 = jnp.float32, jnp.bfloat16
    dma = pltpu.SemaphoreType.DMA

    def buf(n, dtype):
        return pltpu.VMEM((n, 16, TILE), dtype)

    return pl.pallas_call(
        em_kernel,
        out_shape=jax.ShapeDtypeStruct(start.shape, f32),
        in_specs=[hbm] * 5,
        out_specs=vmem,
        scratch_shapes=[
            pltpu.VMEM((K, CT), jnp.int32),
            pltpu.VMEM((K, CT), jnp.int32),
            pltpu.VMEM(counts.shape, f32),
            pltpu.VMEM((NX * LINKS, TILE, TILE), bf16),
            pltpu.VMEM((NX, 8, TILE), jnp.int32),
            pltpu.VMEM((8, TILE), jnp.int32),
            pltpu.VMEM((8, TILE), jnp.int32),
            pltpu.SMEM((8, TILE), jnp.int32),
            buf(COL + 1, bf16),
            buf(3 * LINKS, bf16),
            buf(NX * LINKS, bf16),
            buf(NX * LINKS, bf16),
            buf(COL + 1, f32),
            buf(COL, f32),
            buf(HALF, f32),
            buf(11 * TD, f32),
            buf(4 * TD, f32),
            buf(4 * TD, f32),
            buf(NZ, f32),
            buf(NX * NC, f32),
            pltpu.VMEM((16, TILE), f32),
            pltpu.VMEM((ITERS * NY, 1, TD * TILE), f32),
            pltpu.VMEM((16, TD * TILE), f32),
            dma((15,)), dma((15,)),
            dma((1,)), dma((1,)),
            dma((3,)), dma((3,)),
            dma((3,)), dma((3,)),
            dma((5,)), dma((5,)),
            dma((11,)), dma((11,)),
            dma((4,)), dma((4,)),
            dma((15,)), dma((15,)),
            dma((7,)), dma((7,)),
            dma((ITERS * 3,)), dma((ITERS * 3,)),
            dma((3,)), dma((3,)), dma((6,)),
            buf(TD, f32),
            buf(NX * CT, f32),
            buf(3 * CT, f32),
            buf(NX * CT, bf16),
            dma((3,)), dma((3,)),
            dma((9,)), dma((9,)),
            dma((3,)), dma((3,)),
            dma((3,)), dma((3,)),
        ],
        compiler_params=pltpu.CompilerParams(
            collective_id=0, has_side_effects=True, vmem_limit_bytes=60 << 20
        ),
        name="em_rounds",
    )(link_owner.T, link_local.T, counts, compat.reshape(LINKS, TILE, TILE), start)


def solution(mesh):
    placed = (
        P("smp", "cls"),
        P("cls", None, None, None),
        P("cls", None),
        P("cls", None),
        P("smp", "cls"),
    )
    return jax.shard_map(
        body, mesh=mesh, in_specs=placed, out_specs=P("smp", "cls"), check_vma=False
    )
```

```python
import functools

import jax
import jax.numpy as jnp
from jax import lax
from jax.experimental import pallas as pl
from jax.experimental.pallas import tpu as pltpu
from jax.sharding import PartitionSpec as P

TILE = 128
K = 4
ITERS = 3
MIXING = 0.3
MESH = pl.DeviceIdType.MESH
NX, NZ, NC, NY = 4, 16, 2, 4
TD = 4
CT = 8
LINKS = 32
HALVES = 2
PCT, PLINKS = CT // HALVES, LINKS // HALVES
COL = NZ * NC * TD
HALF = NZ * TD
FAR = (6, -6, 3, -3)
NEAR = (1, -1)
PLACES = (5, 6, 7, 8, -7, -6, -5, 2, 3, 4, -4, -3, -2, -1, 0, 1)
GROUPS = ((0, 4), (4, 3), (7, 3), (10, 3), (13, 3))


def em_kernel(
    owner_hbm, local_hbm, counts_hbm, compat_hbm, start_hbm, out,
    owner, local, counts, cb, tab, raw, lists, table, th, xs, xr0, xr1, sr, cum, d, cr, nr, sf, fr, tt, tx, tot, ps, theta,
    fz_s, fz_r, fc_s, fc_r, fx_s, fx_r, rx_s, rx_r, rc_s, rc_r,
    rn_s, rn_r, rf_s, rf_r, tz_s, tz_r, tg_s, tg_r, p_s, p_r, l_s, l_r, in_s,
    sums, pe, pr, rt, ex_s, ex_r, ey_s, ey_r, pe_s, pe_r, q_s, q_r,
):
    xr = (xr0, xr1)
    tid, perm, keep, pos, mytile, place = (table.at[i] for i in range(6))
    me = lax.axis_index("cls")
    y = lax.axis_index("smp")
    c = me % NC
    z = (me // NC) % NZ
    x = me // (NC * NZ)

    turn = 1 - 2 * c

    zs = {off: lax.rem(z + turn * off + NZ, NZ) for off in range(-8, 9)}

    def zrel(off):
        return zs[off]

    devs = {}

    def at(dx=0, dz=0, dc=0, dy=0):
        return devs[(dx, dz, dc, dy)]

    def copy(src, dst, send, recv, dev):
        return pltpu.make_async_remote_copy(
            src_ref=src, dst_ref=dst, send_sem=send, recv_sem=recv,
            device_id=dev, device_id_type=MESH,
        )

    group = [(dx, dc) for dx in range(NX) for dc in range(NC) if (dx, dc) != (0, 0)]
    peers = [(0, o, 0, 0) for o in (1, -1, 2, -2) + FAR] + [(0, 0, 0, dy) for dy in (1, 2, 3)]
    peers += [(dx, 0, dc, 0) for dx, dc in group]
    for dx, dz, dc, dy in peers:
        devs[(dx, dz, dc, dy)] = (
            (lax.rem(x + dx, NX) * NZ + zs[dz]) * NC + lax.rem(c + dc, NC),
            lax.rem(y + dy, NY),
        )
    barrier = pltpu.get_barrier_semaphore()
    for peer in peers:
        pl.semaphore_signal(barrier, inc=1, device_id=at(*peer), device_id_type=MESH)
    loads = [
        pltpu.make_async_copy(a, b, in_s.at[i])
        for i, (a, b) in enumerate(
            (
                (start_hbm, theta),
                (counts_hbm, counts),
                (compat_hbm, cb.at[pl.ds(x * LINKS, LINKS)]),
                (owner_hbm, owner),
                (local_hbm, local),
            )
        )
    ]
    for load in loads:
        load.start()
    lane = lax.broadcasted_iota(jnp.int32, (8, TILE), 1)
    level = lax.broadcasted_iota(jnp.int32, (8, TILE), 0)
    loads[3].wait()
    loads[4].wait()
    raw[...] = jnp.zeros((8, TILE), jnp.int32)
    raw[0:K, 0:CT] = owner[...] * TD + local[...]
    rows = jnp.zeros((8, TILE), jnp.int32)
    for i in range(CT):
        one = jnp.broadcast_to(raw[:, i : i + 1], (8, TILE))
        rows = jnp.where((lane % LINKS // K == i) & (lane % K == level), one, rows)
    row = jnp.sum(rows, axis=0, keepdims=True)
    tab[0] = jnp.where(lane // LINKS == x, jnp.broadcast_to(row, (8, TILE)), 0)
    pl.semaphore_wait(barrier, len(peers))

    def lcopy(dx):
        return copy(tab.at[0], tab.at[dx], l_s.at[dx - 1], l_r.at[dx - 1], at(dx=dx))

    for dx in (2, 1, 3):
        lcopy(dx).start()

    def load_lists():
        return pltpu.make_async_copy(lists, table, in_s.at[5])

    def make_lists():
        for dx in (1, 3, 2):
            lcopy(dx).wait_recv()
        whole = tab[0, 0:1] + tab[1, 0:1] + tab[2, 0:1] + tab[3, 0:1]
        key = jnp.where(whole // COL == x, whole % COL, COL)
        keys = jnp.broadcast_to(key, (TILE, TILE))
        mine = jnp.transpose(keys)
        j = lax.broadcasted_iota(jnp.int32, (TILE, TILE), 0)
        i = lax.broadcasted_iota(jnp.int32, (TILE, TILE), 1)
        before = jnp.where(keys < mine, 1, 0) + jnp.where((keys == mine) & (i < j), 1, 0)
        rank = jnp.sum(before, axis=1, keepdims=True)
        at_rank = rank == i
        order = jnp.sum(jnp.where(at_rank, j, 0), axis=0, keepdims=True)
        ranked = jnp.sum(jnp.where(at_rank, mine, 0), axis=0, keepdims=True)
        again = (ranked == pltpu.roll(ranked, 1, 1)) & (lane[0:1] > 0)
        upto = jnp.sum(jnp.where(mine <= i, 1, 0), axis=0, keepdims=True)
        some = jnp.sum(jnp.where(mine == i, 1, 0), axis=0, keepdims=True)
        lists[0:1, :] = whole
        lists[1:2, :] = order
        lists[2:3, :] = jnp.where(again, 1, 0)
        lists[3:4, :] = jnp.where(some > 0, upto - 1, COL)
        col = whole % COL
        lies = (col // TD) % NC * HALF + col // (TD * NC) * TD + col % TD
        lists[4:5, :] = jnp.where(key < COL, lies, COL)
        lists[5:6, :] = lies
        load = load_lists()
        load.start()

    far = [(j, 0, o) for j, o in enumerate(FAR)]
    near_own = [(4 + j, 0, o) for j, o in enumerate(NEAR)]
    near_of = [[(6 + 2 * i + j, -w, o) for j, o in enumerate(NEAR)] for i, w in enumerate(FAR)]
    near_of[0].append((14, -FAR[0], 2))
    every = far + near_own + [step for steps in near_of for step in steps]

    def spread(blk, send, recv):
        def move(k, off, way):
            ref = blk(zrel(off))
            return copy(ref, ref, send.at[k], recv.at[k], at(dz=way))

        def take(k, off, way):
            ref = blk(zrel(off - way))
            copy(ref, ref, send.at[k], recv.at[k], at(dz=way)).wait_recv()

        def first():
            for k, off, way in far + near_own:
                move(k, off, way).start()

        def second():
            for i in (2, 3, 0, 1):
                take(*far[i])
                for step in near_of[i]:
                    move(*step).start()

        def third():
            for steps in [near_own] + [near_of[i] for i in (2, 3, 0, 1)]:
                for step in steps:
                    take(*step)

        def close():
            for step in every:
                move(*step).wait_send()

        return first, second, third, close

    def th_blk(zz):
        return th.at[pl.ds(c * HALF + zz * TD, TD)]

    def to_core(core):
        ref = th.at[pl.ds(core * HALF, HALF)]
        return copy(ref, ref, fc_s.at[0], fc_r.at[0], at(dc=1))

    f_first, f_second, f_third, f_close = spread(th_blk, fz_s, fz_r)
    t_first, t_second, t_third, t_close = spread(lambda zz: tt.at[zz], tz_s, tz_r)

    lists[...] = jnp.zeros((8, TILE), jnp.int32)
    loads[0].wait()
    cum[COL] = jnp.zeros((16, TILE), jnp.float32)
    th[COL] = jnp.zeros((16, TILE), jnp.bfloat16)

    def total_own():
        s = counts[:, 0:TILE]
        for i in range(1, counts.shape[1] // TILE):
            s = s + counts[:, i * TILE : (i + 1) * TILE]
        tt[z] = s

    def tg(j, dx, dc):
        return copy(tx.at[0], tx.at[1 + j], tg_s.at[j], tg_r.at[j], at(dx=dx, dc=dc))

    part = LINKS // NY

    def ex(dx, src_x):
        ref = cb.at[pl.ds(src_x * LINKS + y * part, part)]
        return copy(ref, ref, ex_s.at[dx - 1], ex_r.at[dx - 1], at(dx=dx))

    def ey(dx, dy, src_y):
        ref = cb.at[pl.ds(((x + NX - dx) % NX) * LINKS + src_y * part, part)]
        j = (dx - 1) * 3 + dy - 1
        return copy(ref, ref, ey_s.at[j], ey_r.at[j], at(dy=dy))

    def sweep(r, carry):
        for t in range(TD):
            th[c * HALF + z * TD + t] = theta[:, t * TILE : (t + 1) * TILE].astype(jnp.bfloat16)
        f_first()

        @pl.when(r == 0)
        def _():
            loads[1].wait()
            total_own()
            loads[2].wait()
            for dx in (2, 1, 3):
                ex(dx, x).start()
            make_lists()

        f_second()

        f_third()

        to_core(c).start()
        to_core(1 - c).wait_recv()

        def xcopy(dx, h):
            j = (dx - 1) * HALVES + h
            return copy(
                xs.at[pl.ds(j * PLINKS, PLINKS)], xr[h].at[pl.ds(x * PLINKS, PLINKS)],
                fx_s.at[j], fx_r.at[j], at(dx=dx),
            )

        def th_sent():
            f_close()
            to_core(c).wait_send()

        def expect(tiles, at_row):
            weights = jnp.concatenate([cb[at_row + k] for k in range(K)], axis=1)
            return lax.dot_general(
                jnp.concatenate(tiles, axis=1), weights, (((1,), (1,)), ((), ())),
                preferred_element_type=jnp.float32,
            )

        def share(src_x, i, ratio):
            row = src_x * LINKS + i * K
            weights = jnp.concatenate([cb[row + k] for k in range(K)], axis=1)
            got = jnp.dot(ratio, weights, preferred_element_type=jnp.float32)
            for k in range(K):
                sr[src_x * LINKS + i * K + k] = got[:, k * TILE : (k + 1) * TILE].astype(
                    jnp.bfloat16
                )

        def by_tiles():
            load_lists().wait()
            for h in range(HALVES):
                for dx in (2, 1, 3):
                    row = ((x + dx) % NX) * LINKS + h * PLINKS

                    def pick(l, _, base=((dx - 1) * HALVES + h) * PLINKS, row=row):
                        xs[base + l] = th[place[row + l]]
                        return 0

                    lax.fori_loop(0, PLINKS, pick, 0, unroll=8)
                    xcopy(dx, h).start()
            for h in range(HALVES):

                def pick_own(l, _, h=h):
                    xr[h][x * PLINKS + l] = th[place[x * LINKS + h * PLINKS + l]]
                    return 0

                lax.fori_loop(0, PLINKS, pick_own, 0, unroll=8)

            t_first()
            for dx in (1, 3, 2):
                ex(dx, (x + NX - dx) % NX).wait_recv()
                for dy in (2, 1, 3):
                    ey(dx, dy, y).start()

            def scopy(dx, h, src_x):
                ref = sr.at[pl.ds(src_x * LINKS + h * PLINKS, PLINKS)]
                j = (dx - 1) * HALVES + h
                return copy(ref, ref, rx_s.at[j], rx_r.at[j], at(dx=dx))

            for h in range(HALVES):
                for dx in (1, 3, 2):
                    ref = xr[h].at[pl.ds(((x + NX - dx) % NX) * PLINKS, PLINKS)]
                    j = (dx - 1) * HALVES + h
                    copy(ref, ref, fx_s.at[j], fx_r.at[j], at(dx=dx)).wait_recv()

                def tile(n, _, h=h):
                    i = h * PCT + n
                    tiles = []
                    for k in range(K):
                        l = n * K + k
                        src_x = tid[x * LINKS + h * PLINKS + l] // COL
                        tiles.append(xr[h][src_x * PLINKS + l])
                    acc = expect(tiles, x * LINKS + i * K)
                    ratio = (counts[:, pl.ds(pl.multiple_of(i * TILE, TILE), TILE)] / acc).astype(
                        jnp.bfloat16
                    )
                    share(x, i, ratio)
                    return 0

                lax.fori_loop(0, PCT, tile, 0, unroll=4)
                for dx in (2, 1, 3):
                    scopy(dx, h, x).start()
            th_sent()
            t_second()
            t_third()
            s = tt[0]
            for i in range(1, NZ):
                s = s + tt[i]
            tx[0] = s
            for j, (dx, dc) in enumerate(group):
                tg(j, dx, dc).start()
            for h in range(HALVES):
                for dx in (1, 3, 2):
                    scopy(dx, h, (x + NX - dx) % NX).wait_recv()
            for dx in (1, 2, 3):
                for h in range(HALVES):
                    xcopy(dx, h).wait_send()
                    scopy(dx, h, x).wait_send()
                ex(dx, x).wait_send()
                lcopy(dx).wait_send()

        def pcopy_x(dx, h):
            j = (dx - 1) * HALVES + h
            return copy(
                pe.at[pl.ds(dx * CT + h * PCT, PCT)], pr.at[pl.ds((dx - 1) * CT + h * PCT, PCT)],
                pe_s.at[j], pe_r.at[j], at(dx=dx),
            )

        def qcopy(dx, h, src_x):
            ref = rt.at[pl.ds(src_x * CT + h * PCT, PCT)]
            j = (dx - 1) * HALVES + h
            return copy(ref, ref, q_s.at[j], q_r.at[j], at(dx=dx))

        def by_sums():
            @pl.when(r == 1)
            def _():
                for dx in (1, 2, 3):
                    for dy in (1, 2, 3):
                        ey(dx, dy, (y + NY - dy) % NY).wait_recv()

            for h in range(HALVES):
                for dx in (2, 1, 3, 0):
                    row = ((x + dx) % NX) * LINKS

                    def part_sum(i, _, dx=dx, row=row):
                        pe[dx * CT + i] = expect(
                            [th[mytile[row + i * K + k]] for k in range(K)], row + i * K
                        )
                        return 0

                    lax.fori_loop(h * PCT, (h + 1) * PCT, part_sum, 0, unroll=4)
                    if dx:
                        pcopy_x(dx, h).start()
            th_sent()

            def shares(src_x, h):
                def one(i, _):
                    share(src_x, i, rt[src_x * CT + i])
                    return 0

                lax.fori_loop(h * PCT, (h + 1) * PCT, one, 0, unroll=4)

            for h in range(HALVES):
                for dx in (1, 3, 2):
                    pcopy_x(dx, h).wait_recv()

                def ratio(i, _):
                    acc = pe[i] + pr[i] + pr[CT + i] + pr[2 * CT + i]
                    rt[x * CT + i] = (
                        counts[:, pl.ds(pl.multiple_of(i * TILE, TILE), TILE)] / acc
                    ).astype(jnp.bfloat16)
                    return 0

                lax.fori_loop(h * PCT, (h + 1) * PCT, ratio, 0, unroll=4)
                for dx in (2, 1, 3):
                    qcopy(dx, h, x).start()
                shares(x, h)
            for h in range(HALVES):
                for dx in (1, 3, 2):
                    src_x = (x + NX - dx) % NX
                    qcopy(dx, h, src_x).wait_recv()
                    shares(src_x, h)
            for dx in (1, 2, 3):
                for h in range(HALVES):
                    pcopy_x(dx, h).wait_send()
                    qcopy(dx, h, x).wait_send()

            @pl.when(r == 1)
            def _():
                for dx in (1, 2, 3):
                    for dy in (1, 2, 3):
                        ey(dx, dy, y).wait_send()

        pl.when(r == 0)(by_tiles)
        pl.when(r > 0)(by_sums)

        def add(j, acc):
            acc = jnp.where(keep[j] > 0, acc, 0.0) + sr[perm[j]].astype(jnp.float32)
            cum[j] = acc
            return acc

        lax.fori_loop(0, COL, add, jnp.zeros((16, TILE), jnp.float32), unroll=8)

        def dense(core, off_sign, first, count):
            for p in range(first, first + count):
                zz = zs[off_sign * PLACES[p]]
                for t in range(TD):
                    d[core * HALF + p * TD + t] = cum[pos[(zz * NC + core) * TD + t]]

        def rcopy(g):
            first, count = GROUPS[g]
            return copy(
                d.at[pl.ds((1 - c) * HALF + first * TD, count * TD)],
                cr.at[pl.ds(first * TD, count * TD)], rc_s.at[g], rc_r.at[g], at(dc=1),
            )

        for g, (first, count) in enumerate(GROUPS):
            dense(1 - c, -1, first, count)
            rcopy(g).start()
        for first, count in GROUPS:
            dense(c, 1, first, count)

        def dz(off):
            return d.at[pl.ds(c * HALF + PLACES.index(off) * TD, TD)]

        kinds = (0,) + FAR
        nsteps = [
            [(q * 2 + j, way, way + kind) for j, way in enumerate(NEAR)]
            for q, kind in enumerate(kinds)
        ]
        nsteps[1].append((10, 2, 8))

        def ncopy(slot, way, dest):
            return copy(
                dz(dest), nr.at[pl.ds(slot * TD, TD)], rn_s.at[slot], rn_r.at[slot], at(dz=way)
            )

        def fcopy(j, way):
            return copy(
                sf.at[pl.ds(j * TD, TD)], fr.at[pl.ds(j * TD, TD)], rf_s.at[j], rf_r.at[j],
                at(dz=way),
            )

        for g, q in enumerate((1, 2, 3, 4, 0)):
            rcopy(g).wait_recv()
            first, count = GROUPS[g]
            for i in range(first * TD, (first + count) * TD):
                d[c * HALF + i] = d[c * HALF + i] + cr[i]
            for n in nsteps[q]:
                ncopy(*n).start()

        @pl.when(r == 0)
        def _():
            for j, (dx, dc) in enumerate(group):
                tg(j, dx, dc).wait_recv()
            s = tx[0]
            for j in range(len(group)):
                s = s + tx[1 + j]
            tot[...] = jnp.broadcast_to(jnp.sum(s, axis=1, keepdims=True), (16, TILE))

        for q, kind in enumerate(kinds):
            if q == 0:
                continue
            for n in nsteps[q]:
                ncopy(*n).wait_recv()
            for t in range(TD):
                acc = d[c * HALF + PLACES.index(kind) * TD + t]
                for n in nsteps[q]:
                    acc = acc + nr[n[0] * TD + t]
                sf[(q - 1) * TD + t] = acc
            fcopy(q - 1, kind).start()
        for n in nsteps[0]:
            ncopy(*n).wait_recv()
        for t in range(TD):
            acc = d[c * HALF + PLACES.index(0) * TD + t]
            for n in nsteps[0]:
                acc = acc + nr[n[0] * TD + t]
            sums[t] = acc
        for j in (2, 3, 0, 1):
            fcopy(j, FAR[j]).wait_recv()
        for t in range(TD):
            cols = slice(t * TILE, (t + 1) * TILE)
            acc = sums[t] + ((fr[t] + fr[TD + t]) + (fr[2 * TD + t] + fr[3 * TD + t]))
            updated = theta[:, cols] * acc / tot[...]
            theta[:, cols] = updated
            ps[r * NY, :, cols] = jnp.sum(updated, axis=0, keepdims=True)

        def pcopy(dy):
            j = r * 3 + dy - 1
            return copy(ps.at[r * NY], ps.at[r * NY + dy], p_s.at[j], p_r.at[j], at(dy=dy))

        for dy in (2, 1, 3):
            pcopy(dy).start()
        for g in range(len(GROUPS)):
            rcopy(g).wait_send()
        for steps in nsteps:
            for n in steps:
                ncopy(*n).wait_send()
        for j, way in enumerate(FAR):
            fcopy(j, way).wait_send()

        @pl.when(r == 0)
        def _():
            t_close()
            for j, (dx, dc) in enumerate(group):
                tg(j, dx, dc).wait_send()

        for dy in (1, 3, 2):
            pcopy(dy).wait_recv()
        pooled = ps[r * NY] + ps[r * NY + 1] + ps[r * NY + 2] + ps[r * NY + 3]
        theta[...] = (1.0 - MIXING) * theta[...] + (MIXING / (16 * NY)) * pooled
        for dy in (1, 2, 3):
            pcopy(dy).wait_send()
        return carry

    lax.fori_loop(0, ITERS, sweep, 0)
    out[...] = theta[...] * 65536.0


def body(counts, compat, link_owner, link_local, start):
    hbm = pl.BlockSpec(memory_space=pltpu.HBM)
    vmem = pl.BlockSpec(memory_space=pltpu.VMEM)
    f32, bf16 = jnp.float32, jnp.bfloat16
    dma = pltpu.SemaphoreType.DMA

    def buf(n, dtype):
        return pltpu.VMEM((n, 16, TILE), dtype)

    return pl.pallas_call(
        em_kernel,
        out_shape=jax.ShapeDtypeStruct(start.shape, f32),
        in_specs=[hbm] * 5,
        out_specs=vmem,
        scratch_shapes=[
            pltpu.VMEM((K, CT), jnp.int32),
            pltpu.VMEM((K, CT), jnp.int32),
            pltpu.VMEM(counts.shape, f32),
            pltpu.VMEM((NX * LINKS, TILE, TILE), bf16),
            pltpu.VMEM((NX, 8, TILE), jnp.int32),
            pltpu.VMEM((8, TILE), jnp.int32),
            pltpu.VMEM((8, TILE), jnp.int32),
            pltpu.SMEM((8, TILE), jnp.int32),
            buf(COL + 1, bf16),
            buf(3 * LINKS, bf16),
            buf(NX * PLINKS, bf16), buf(NX * PLINKS, bf16),
            buf(NX * LINKS, bf16),
            buf(COL + 1, f32),
            buf(COL, f32),
            buf(HALF, f32),
            buf(11 * TD, f32),
            buf(4 * TD, f32),
            buf(4 * TD, f32),
            buf(NZ, f32),
            buf(NX * NC, f32),
            pltpu.VMEM((16, TILE), f32),
            pltpu.VMEM((ITERS * NY, 1, TD * TILE), f32),
            pltpu.VMEM((16, TD * TILE), f32),
            dma((15,)), dma((15,)),
            dma((1,)), dma((1,)),
            dma((3 * HALVES,)), dma((3 * HALVES,)),
            dma((3 * HALVES,)), dma((3 * HALVES,)),
            dma((5,)), dma((5,)),
            dma((11,)), dma((11,)),
            dma((4,)), dma((4,)),
            dma((15,)), dma((15,)),
            dma((7,)), dma((7,)),
            dma((ITERS * 3,)), dma((ITERS * 3,)),
            dma((3,)), dma((3,)), dma((6,)),
            buf(TD, f32),
            buf(NX * CT, f32),
            buf(3 * CT, f32),
            buf(NX * CT, bf16),
            dma((3,)), dma((3,)),
            dma((9,)), dma((9,)),
            dma((3 * HALVES,)), dma((3 * HALVES,)),
            dma((3 * HALVES,)), dma((3 * HALVES,)),
        ],
        compiler_params=pltpu.CompilerParams(
            collective_id=0, has_side_effects=True, vmem_limit_bytes=60 << 20
        ),
        name="em_rounds",
    )(link_owner.T, link_local.T, counts, compat.reshape(LINKS, TILE, TILE), start)


def solution(mesh):
    placed = (
        P("smp", "cls"),
        P("cls", None, None, None),
        P("cls", None),
        P("cls", None),
        P("smp", "cls"),
    )
    return jax.shard_map(
        body, mesh=mesh, in_specs=placed, out_specs=P("smp", "cls"), check_vma=False
    )
```

```python
import functools

import jax
import jax.numpy as jnp
from jax import lax
from jax.experimental import pallas as pl
from jax.experimental.pallas import tpu as pltpu
from jax.sharding import PartitionSpec as P

TILE = 128
K = 4
ITERS = 3
MIXING = 0.3
MESH = pl.DeviceIdType.MESH
NX, NZ, NC, NY = 4, 16, 2, 4
TD = 4
CT = 8
LINKS = 32
HALVES = 2
PCT, PLINKS = CT // HALVES, LINKS // HALVES
COL = NZ * NC * TD
HALF = NZ * TD
FAR = (6, -6, 3, -3)
NEAR = (1, -1)
PLACES = (5, 6, 7, 8, -7, -6, -5, 2, 3, 4, -4, -3, -2, -1, 0, 1)
GROUPS = ((0, 4), (4, 3), (7, 3), (10, 3), (13, 3))


def em_kernel(
    owner_hbm, local_hbm, counts_hbm, compat_hbm, start_hbm, out,
    owner, local, counts, cb, tab, raw, lists, table, th, xs, xr0, xr1, sr, cum, d, cr, nr, sf, fr, tt, tx, tot, ps, theta,
    fz_s, fz_r, fc_s, fc_r, fx_s, fx_r, rx_s, rx_r, rc_s, rc_r,
    rn_s, rn_r, rf_s, rf_r, tz_s, tz_r, tg_s, tg_r, p_s, p_r, l_s, l_r, in_s,
    sums, pe, pr, rt, ex_s, ex_r, ey_s, ey_r, pe_s, pe_r, q_s, q_r,
):
    xr = (xr0, xr1)
    tid, perm, keep, pos, mytile, place = (table.at[i] for i in range(6))
    me = lax.axis_index("cls")
    y = lax.axis_index("smp")
    c = me % NC
    z = (me // NC) % NZ
    x = me // (NC * NZ)

    turn = 1 - 2 * c

    zs = {off: lax.rem(z + turn * off + NZ, NZ) for off in range(-8, 9)}

    def zrel(off):
        return zs[off]

    devs = {}

    def at(dx=0, dz=0, dc=0, dy=0):
        return devs[(dx, dz, dc, dy)]

    def copy(src, dst, send, recv, dev):
        return pltpu.make_async_remote_copy(
            src_ref=src, dst_ref=dst, send_sem=send, recv_sem=recv,
            device_id=dev, device_id_type=MESH,
        )

    group = [(dx, dc) for dx in range(NX) for dc in range(NC) if (dx, dc) != (0, 0)]
    peers = [(0, o, 0, 0) for o in (1, -1, 2, -2) + FAR] + [(0, 0, 0, dy) for dy in (1, 2, 3)]
    peers += [(dx, 0, dc, 0) for dx, dc in group]
    for dx, dz, dc, dy in peers:
        devs[(dx, dz, dc, dy)] = (
            (lax.rem(x + dx, NX) * NZ + zs[dz]) * NC + lax.rem(c + dc, NC),
            lax.rem(y + dy, NY),
        )
    barrier = pltpu.get_barrier_semaphore()
    for peer in peers:
        pl.semaphore_signal(barrier, inc=1, device_id=at(*peer), device_id_type=MESH)
    loads = [
        pltpu.make_async_copy(a, b, in_s.at[i])
        for i, (a, b) in enumerate(
            (
                (start_hbm, theta),
                (counts_hbm, counts),
                (compat_hbm, cb.at[pl.ds(x * LINKS, LINKS)]),
                (owner_hbm, owner),
                (local_hbm, local),
            )
        )
    ]
    for load in loads:
        load.start()
    lane = lax.broadcasted_iota(jnp.int32, (8, TILE), 1)
    level = lax.broadcasted_iota(jnp.int32, (8, TILE), 0)
    loads[3].wait()
    loads[4].wait()
    raw[...] = jnp.zeros((8, TILE), jnp.int32)
    raw[0:K, 0:CT] = owner[...] * TD + local[...]
    rows = jnp.zeros((8, TILE), jnp.int32)
    for i in range(CT):
        one = jnp.broadcast_to(raw[:, i : i + 1], (8, TILE))
        rows = jnp.where((lane % LINKS // K == i) & (lane % K == level), one, rows)
    row = jnp.sum(rows, axis=0, keepdims=True)
    tab[0] = jnp.where(lane // LINKS == x, jnp.broadcast_to(row, (8, TILE)), 0)
    pl.semaphore_wait(barrier, len(peers))

    def lcopy(dx):
        return copy(tab.at[0], tab.at[dx], l_s.at[dx - 1], l_r.at[dx - 1], at(dx=dx))

    for dx in (2, 1, 3):
        lcopy(dx).start()

    def load_lists():
        return pltpu.make_async_copy(lists, table, in_s.at[5])

    def make_lists():
        for dx in (1, 3, 2):
            lcopy(dx).wait_recv()
        whole = tab[0, 0:1] + tab[1, 0:1] + tab[2, 0:1] + tab[3, 0:1]
        key = jnp.where(whole // COL == x, whole % COL, COL)
        keys = jnp.broadcast_to(key, (TILE, TILE))
        mine = jnp.transpose(keys)
        j = lax.broadcasted_iota(jnp.int32, (TILE, TILE), 0)
        i = lax.broadcasted_iota(jnp.int32, (TILE, TILE), 1)
        before = jnp.where(keys < mine, 1, 0) + jnp.where((keys == mine) & (i < j), 1, 0)
        rank = jnp.sum(before, axis=1, keepdims=True)
        at_rank = rank == i
        order = jnp.sum(jnp.where(at_rank, j, 0), axis=0, keepdims=True)
        ranked = jnp.sum(jnp.where(at_rank, mine, 0), axis=0, keepdims=True)
        again = (ranked == pltpu.roll(ranked, 1, 1)) & (lane[0:1] > 0)
        upto = jnp.sum(jnp.where(mine <= i, 1, 0), axis=0, keepdims=True)
        some = jnp.sum(jnp.where(mine == i, 1, 0), axis=0, keepdims=True)
        lists[0:1, :] = whole
        lists[1:2, :] = order
        lists[2:3, :] = jnp.where(again, 1, 0)
        lists[3:4, :] = jnp.where(some > 0, upto - 1, COL)
        col = whole % COL
        lies = (col // TD) % NC * HALF + col // (TD * NC) * TD + col % TD
        lists[4:5, :] = jnp.where(key < COL, lies, COL)
        lists[5:6, :] = lies
        load = load_lists()
        load.start()

    far = [(j, 0, o) for j, o in enumerate(FAR)]
    near_own = [(4 + j, 0, o) for j, o in enumerate(NEAR)]
    near_of = [[(6 + 2 * i + j, -w, o) for j, o in enumerate(NEAR)] for i, w in enumerate(FAR)]
    near_of[0].append((14, -FAR[0], 2))
    every = far + near_own + [step for steps in near_of for step in steps]

    def spread(blk, send, recv):
        def move(k, off, way):
            ref = blk(zrel(off))
            return copy(ref, ref, send.at[k], recv.at[k], at(dz=way))

        def take(k, off, way):
            ref = blk(zrel(off - way))
            copy(ref, ref, send.at[k], recv.at[k], at(dz=way)).wait_recv()

        def first():
            for k, off, way in far + near_own:
                move(k, off, way).start()

        def second():
            for i in (2, 3, 0, 1):
                take(*far[i])
                for step in near_of[i]:
                    move(*step).start()

        def third():
            for steps in [near_own] + [near_of[i] for i in (2, 3, 0, 1)]:
                for step in steps:
                    take(*step)

        def close():
            for step in every:
                move(*step).wait_send()

        return first, second, third, close

    def th_blk(zz):
        return th.at[pl.ds(c * HALF + zz * TD, TD)]

    def to_core(core):
        ref = th.at[pl.ds(core * HALF, HALF)]
        return copy(ref, ref, fc_s.at[0], fc_r.at[0], at(dc=1))

    f_first, f_second, f_third, f_close = spread(th_blk, fz_s, fz_r)
    t_first, t_second, t_third, t_close = spread(lambda zz: tt.at[zz], tz_s, tz_r)

    lists[...] = jnp.zeros((8, TILE), jnp.int32)
    loads[0].wait()
    cum[COL] = jnp.zeros((16, TILE), jnp.float32)
    th[COL] = jnp.zeros((16, TILE), jnp.bfloat16)

    def total_own():
        s = counts[:, 0:TILE]
        for i in range(1, counts.shape[1] // TILE):
            s = s + counts[:, i * TILE : (i + 1) * TILE]
        tt[z] = s

    def tg(j, dx, dc):
        return copy(tx.at[0], tx.at[1 + j], tg_s.at[j], tg_r.at[j], at(dx=dx, dc=dc))

    part = 6
    rest = LINKS - NY * part

    def ex(dx, src_x, step):
        if step < 2:
            ref = cb.at[pl.ds(src_x * LINKS + (y + 2 * step) % NY * part, part)]
        else:
            ref = cb.at[pl.ds(src_x * LINKS + NY * part, rest)]
        j = step * 3 + dx - 1
        return copy(ref, ref, ex_s.at[j], ex_r.at[j], at(dx=dx))

    def ey(dx, dy, src_y):
        ref = cb.at[pl.ds(((x + NX - dx) % NX) * LINKS + src_y * part, part)]
        j = (dx - 1) * 3 + dy - 1
        return copy(ref, ref, ey_s.at[j], ey_r.at[j], at(dy=dy))

    def sweep(r, carry):
        for t in range(TD):
            th[c * HALF + z * TD + t] = theta[:, t * TILE : (t + 1) * TILE].astype(jnp.bfloat16)
        f_first()

        @pl.when(r == 0)
        def _():
            loads[1].wait()
            total_own()
            loads[2].wait()
            for dx in (2, 1, 3):
                ex(dx, x, 0).start()
            make_lists()

        f_second()

        f_third()

        to_core(c).start()
        to_core(1 - c).wait_recv()

        def xcopy(dx, h):
            j = (dx - 1) * HALVES + h
            return copy(
                xs.at[pl.ds(j * PLINKS, PLINKS)], xr[h].at[pl.ds(x * PLINKS, PLINKS)],
                fx_s.at[j], fx_r.at[j], at(dx=dx),
            )

        def th_sent():
            f_close()
            to_core(c).wait_send()

        def expect(tiles, at_row):
            weights = jnp.concatenate([cb[at_row + k] for k in range(K)], axis=1)
            return lax.dot_general(
                jnp.concatenate(tiles, axis=1), weights, (((1,), (1,)), ((), ())),
                preferred_element_type=jnp.float32,
            )

        def share(src_x, i, ratio):
            row = src_x * LINKS + i * K
            weights = jnp.concatenate([cb[row + k] for k in range(K)], axis=1)
            got = jnp.dot(ratio, weights, preferred_element_type=jnp.float32)
            for k in range(K):
                sr[src_x * LINKS + i * K + k] = got[:, k * TILE : (k + 1) * TILE].astype(
                    jnp.bfloat16
                )

        def by_tiles():
            load_lists().wait()
            for h in range(HALVES):
                for dx in (2, 1, 3):
                    row = ((x + dx) % NX) * LINKS + h * PLINKS

                    def pick(l, _, base=((dx - 1) * HALVES + h) * PLINKS, row=row):
                        xs[base + l] = th[place[row + l]]
                        return 0

                    lax.fori_loop(0, PLINKS, pick, 0, unroll=8)
                    xcopy(dx, h).start()
            for h in range(HALVES):

                def pick_own(l, _, h=h):
                    xr[h][x * PLINKS + l] = th[place[x * LINKS + h * PLINKS + l]]
                    return 0

                lax.fori_loop(0, PLINKS, pick_own, 0, unroll=8)

            t_first()
            for dx in (1, 3, 2):
                ex(dx, (x + NX - dx) % NX, 0).wait_recv()
                for dy in (1, 3):
                    ey(dx, dy, y).start()

            def scopy(dx, h, src_x):
                ref = sr.at[pl.ds(src_x * LINKS + h * PLINKS, PLINKS)]
                j = (dx - 1) * HALVES + h
                return copy(ref, ref, rx_s.at[j], rx_r.at[j], at(dx=dx))

            for h in range(HALVES):
                for dx in (1, 3, 2):
                    ref = xr[h].at[pl.ds(((x + NX - dx) % NX) * PLINKS, PLINKS)]
                    j = (dx - 1) * HALVES + h
                    copy(ref, ref, fx_s.at[j], fx_r.at[j], at(dx=dx)).wait_recv()

                def tile(n, _, h=h):
                    i = h * PCT + n
                    tiles = []
                    for k in range(K):
                        l = n * K + k
                        src_x = tid[x * LINKS + h * PLINKS + l] // COL
                        tiles.append(xr[h][src_x * PLINKS + l])
                    acc = expect(tiles, x * LINKS + i * K)
                    ratio = (counts[:, pl.ds(pl.multiple_of(i * TILE, TILE), TILE)] / acc).astype(
                        jnp.bfloat16
                    )
                    share(x, i, ratio)
                    return 0

                lax.fori_loop(0, PCT, tile, 0, unroll=4)
                for dx in (2, 1, 3):
                    scopy(dx, h, x).start()
            th_sent()
            t_second()
            t_third()
            s = tt[0]
            for i in range(1, NZ):
                s = s + tt[i]
            tx[0] = s
            for j, (dx, dc) in enumerate(group):
                tg(j, dx, dc).start()
            for h in range(HALVES):
                for dx in (1, 3, 2):
                    scopy(dx, h, (x + NX - dx) % NX).wait_recv()
            for dx in (1, 2, 3):
                for h in range(HALVES):
                    xcopy(dx, h).wait_send()
                    scopy(dx, h, x).wait_send()
                ex(dx, x, 0).wait_send()
                lcopy(dx).wait_send()

        def pcopy_x(dx, h):
            j = (dx - 1) * HALVES + h
            return copy(
                pe.at[pl.ds(dx * CT + h * PCT, PCT)], pr.at[pl.ds((dx - 1) * CT + h * PCT, PCT)],
                pe_s.at[j], pe_r.at[j], at(dx=dx),
            )

        def qcopy(dx, h, src_x):
            ref = rt.at[pl.ds(src_x * CT + h * PCT, PCT)]
            j = (dx - 1) * HALVES + h
            return copy(ref, ref, q_s.at[j], q_r.at[j], at(dx=dx))

        def by_sums():
            @pl.when(r == 1)
            def _():
                for dx in (1, 2, 3):
                    ex(dx, (x + NX - dx) % NX, 1).wait_recv()
                    ex(dx, (x + NX - dx) % NX, 2).wait_recv()
                    for dy in (1, 3):
                        ey(dx, dy, (y + NY - dy) % NY).wait_recv()

            for h in range(HALVES):
                for dx in (2, 1, 3, 0):
                    row = ((x + dx) % NX) * LINKS

                    def part_sum(i, _, dx=dx, row=row):
                        pe[dx * CT + i] = expect(
                            [th[mytile[row + i * K + k]] for k in range(K)], row + i * K
                        )
                        return 0

                    lax.fori_loop(h * PCT, (h + 1) * PCT, part_sum, 0, unroll=4)
                    if dx:
                        pcopy_x(dx, h).start()
            th_sent()

            def shares(src_x, h):
                def one(i, _):
                    share(src_x, i, rt[src_x * CT + i])
                    return 0

                lax.fori_loop(h * PCT, (h + 1) * PCT, one, 0, unroll=4)

            for h in range(HALVES):
                for dx in (1, 3, 2):
                    pcopy_x(dx, h).wait_recv()

                def ratio(i, _):
                    acc = pe[i] + pr[i] + pr[CT + i] + pr[2 * CT + i]
                    rt[x * CT + i] = (
                        counts[:, pl.ds(pl.multiple_of(i * TILE, TILE), TILE)] / acc
                    ).astype(jnp.bfloat16)
                    return 0

                lax.fori_loop(h * PCT, (h + 1) * PCT, ratio, 0, unroll=4)
                for dx in (2, 1, 3):
                    qcopy(dx, h, x).start()
                shares(x, h)
            for h in range(HALVES):
                for dx in (1, 3, 2):
                    src_x = (x + NX - dx) % NX
                    qcopy(dx, h, src_x).wait_recv()
                    shares(src_x, h)
            for dx in (1, 2, 3):
                for h in range(HALVES):
                    pcopy_x(dx, h).wait_send()
                    qcopy(dx, h, x).wait_send()

            @pl.when(r == 1)
            def _():
                for dx in (1, 2, 3):
                    ex(dx, x, 1).wait_send()
                    ex(dx, x, 2).wait_send()
                    for dy in (1, 3):
                        ey(dx, dy, y).wait_send()

        pl.when(r == 0)(by_tiles)
        pl.when(r > 0)(by_sums)

        def add(j, acc):
            acc = jnp.where(keep[j] > 0, acc, 0.0) + sr[perm[j]].astype(jnp.float32)
            cum[j] = acc
            return acc

        lax.fori_loop(0, COL, add, jnp.zeros((16, TILE), jnp.float32), unroll=8)

        def dense(core, off_sign, first, count):
            for p in range(first, first + count):
                zz = zs[off_sign * PLACES[p]]
                for t in range(TD):
                    d[core * HALF + p * TD + t] = cum[pos[(zz * NC + core) * TD + t]]

        def rcopy(g):
            first, count = GROUPS[g]
            return copy(
                d.at[pl.ds((1 - c) * HALF + first * TD, count * TD)],
                cr.at[pl.ds(first * TD, count * TD)], rc_s.at[g], rc_r.at[g], at(dc=1),
            )

        for g, (first, count) in enumerate(GROUPS):
            dense(1 - c, -1, first, count)
            rcopy(g).start()
        for first, count in GROUPS:
            dense(c, 1, first, count)

        def dz(off):
            return d.at[pl.ds(c * HALF + PLACES.index(off) * TD, TD)]

        kinds = (0,) + FAR
        nsteps = [
            [(q * 2 + j, way, way + kind) for j, way in enumerate(NEAR)]
            for q, kind in enumerate(kinds)
        ]
        nsteps[1].append((10, 2, 8))

        def ncopy(slot, way, dest):
            return copy(
                dz(dest), nr.at[pl.ds(slot * TD, TD)], rn_s.at[slot], rn_r.at[slot], at(dz=way)
            )

        def fcopy(j, way):
            return copy(
                sf.at[pl.ds(j * TD, TD)], fr.at[pl.ds(j * TD, TD)], rf_s.at[j], rf_r.at[j],
                at(dz=way),
            )

        for g, q in enumerate((1, 2, 3, 4, 0)):
            rcopy(g).wait_recv()
            first, count = GROUPS[g]
            for i in range(first * TD, (first + count) * TD):
                d[c * HALF + i] = d[c * HALF + i] + cr[i]
            for n in nsteps[q]:
                ncopy(*n).start()

        @pl.when(r == 0)
        def _():
            for j, (dx, dc) in enumerate(group):
                tg(j, dx, dc).wait_recv()
            s = tx[0]
            for j in range(len(group)):
                s = s + tx[1 + j]
            tot[...] = jnp.broadcast_to(jnp.sum(s, axis=1, keepdims=True), (16, TILE))

        for q, kind in enumerate(kinds):
            if q == 0:
                continue
            for n in nsteps[q]:
                ncopy(*n).wait_recv()
            for t in range(TD):
                acc = d[c * HALF + PLACES.index(kind) * TD + t]
                for n in nsteps[q]:
                    acc = acc + nr[n[0] * TD + t]
                sf[(q - 1) * TD + t] = acc
            fcopy(q - 1, kind).start()
        @pl.when(r == 0)
        def _():
            for dx in (2, 1, 3):
                ex(dx, x, 1).start()
                ex(dx, x, 2).start()

        for n in nsteps[0]:
            ncopy(*n).wait_recv()
        for t in range(TD):
            acc = d[c * HALF + PLACES.index(0) * TD + t]
            for n in nsteps[0]:
                acc = acc + nr[n[0] * TD + t]
            sums[t] = acc
        for j in (2, 3, 0, 1):
            fcopy(j, FAR[j]).wait_recv()
        for t in range(TD):
            cols = slice(t * TILE, (t + 1) * TILE)
            acc = sums[t] + ((fr[t] + fr[TD + t]) + (fr[2 * TD + t] + fr[3 * TD + t]))
            updated = theta[:, cols] * acc / tot[...]
            theta[:, cols] = updated
            ps[r * NY, :, cols] = jnp.sum(updated, axis=0, keepdims=True)

        def pcopy(dy):
            j = r * 3 + dy - 1
            return copy(ps.at[r * NY], ps.at[r * NY + dy], p_s.at[j], p_r.at[j], at(dy=dy))

        for dy in (2, 1, 3):
            pcopy(dy).start()
        for g in range(len(GROUPS)):
            rcopy(g).wait_send()
        for steps in nsteps:
            for n in steps:
                ncopy(*n).wait_send()
        for j, way in enumerate(FAR):
            fcopy(j, way).wait_send()

        @pl.when(r == 0)
        def _():
            t_close()
            for j, (dx, dc) in enumerate(group):
                tg(j, dx, dc).wait_send()

        for dy in (1, 3, 2):
            pcopy(dy).wait_recv()
        pooled = ps[r * NY] + ps[r * NY + 1] + ps[r * NY + 2] + ps[r * NY + 3]
        theta[...] = (1.0 - MIXING) * theta[...] + (MIXING / (16 * NY)) * pooled
        for dy in (1, 2, 3):
            pcopy(dy).wait_send()
        return carry

    lax.fori_loop(0, ITERS, sweep, 0)
    out[...] = theta[...] * 65536.0


def body(counts, compat, link_owner, link_local, start):
    hbm = pl.BlockSpec(memory_space=pltpu.HBM)
    vmem = pl.BlockSpec(memory_space=pltpu.VMEM)
    f32, bf16 = jnp.float32, jnp.bfloat16
    dma = pltpu.SemaphoreType.DMA

    def buf(n, dtype):
        return pltpu.VMEM((n, 16, TILE), dtype)

    return pl.pallas_call(
        em_kernel,
        out_shape=jax.ShapeDtypeStruct(start.shape, f32),
        in_specs=[hbm] * 5,
        out_specs=vmem,
        scratch_shapes=[
            pltpu.VMEM((K, CT), jnp.int32),
            pltpu.VMEM((K, CT), jnp.int32),
            pltpu.VMEM(counts.shape, f32),
            pltpu.VMEM((NX * LINKS, TILE, TILE), bf16),
            pltpu.VMEM((NX, 8, TILE), jnp.int32),
            pltpu.VMEM((8, TILE), jnp.int32),
            pltpu.VMEM((8, TILE), jnp.int32),
            pltpu.SMEM((8, TILE), jnp.int32),
            buf(COL + 1, bf16),
            buf(3 * LINKS, bf16),
            buf(NX * PLINKS, bf16), buf(NX * PLINKS, bf16),
            buf(NX * LINKS, bf16),
            buf(COL + 1, f32),
            buf(COL, f32),
            buf(HALF, f32),
            buf(11 * TD, f32),
            buf(4 * TD, f32),
            buf(4 * TD, f32),
            buf(NZ, f32),
            buf(NX * NC, f32),
            pltpu.VMEM((16, TILE), f32),
            pltpu.VMEM((ITERS * NY, 1, TD * TILE), f32),
            pltpu.VMEM((16, TD * TILE), f32),
            dma((15,)), dma((15,)),
            dma((1,)), dma((1,)),
            dma((3 * HALVES,)), dma((3 * HALVES,)),
            dma((3 * HALVES,)), dma((3 * HALVES,)),
            dma((5,)), dma((5,)),
            dma((11,)), dma((11,)),
            dma((4,)), dma((4,)),
            dma((15,)), dma((15,)),
            dma((7,)), dma((7,)),
            dma((ITERS * 3,)), dma((ITERS * 3,)),
            dma((3,)), dma((3,)), dma((6,)),
            buf(TD, f32),
            buf(NX * CT, f32),
            buf(3 * CT, f32),
            buf(NX * CT, bf16),
            dma((9,)), dma((9,)),
            dma((9,)), dma((9,)),
            dma((3 * HALVES,)), dma((3 * HALVES,)),
            dma((3 * HALVES,)), dma((3 * HALVES,)),
        ],
        compiler_params=pltpu.CompilerParams(
            collective_id=0, has_side_effects=True, vmem_limit_bytes=60 << 20
        ),
        name="em_rounds",
    )(link_owner.T, link_local.T, counts, compat.reshape(LINKS, TILE, TILE), start)


def solution(mesh):
    placed = (
        P("smp", "cls"),
        P("cls", None, None, None),
        P("cls", None),
        P("cls", None),
        P("smp", "cls"),
    )
    return jax.shard_map(
        body, mesh=mesh, in_specs=placed, out_specs=P("smp", "cls"), check_vma=False
    )
```

```python
import functools

import jax
import jax.numpy as jnp
from jax import lax
from jax.experimental import pallas as pl
from jax.experimental.pallas import tpu as pltpu
from jax.sharding import PartitionSpec as P

TILE = 128
K = 4
ITERS = 3
MIXING = 0.3
MESH = pl.DeviceIdType.MESH
NX, NZ, NC, NY = 4, 16, 2, 4
TD = 4
CT = 8
LINKS = 32
HALVES = 2
PCT, PLINKS = CT // HALVES, LINKS // HALVES
COL = NZ * NC * TD
HALF = NZ * TD
FAR = (6, -6, 3, -3)
NEAR = (1, -1)
PLACES = (5, 6, 7, 8, -7, -6, -5, 2, 3, 4, -4, -3, -2, -1, 0, 1)
GROUPS = ((0, 4), (4, 3), (7, 3), (10, 3), (13, 3))


def em_kernel(
    owner_hbm, local_hbm, counts_hbm, compat_hbm, start_hbm, out,
    owner, local, counts, cb, tab, raw, lists, table, th, xs, xr0, xr1, sr, cum, d, cr, nr, sf, fr, tt, tx, tot, ps, theta,
    fz_s, fz_r, fc_s, fc_r, fx_s, fx_r, rx_s, rx_r, rc_s, rc_r,
    rn_s, rn_r, rf_s, rf_r, tz_s, tz_r, tg_s, tg_r, p_s, p_r, l_s, l_r, in_s,
    sums, pe, pr, rt, ex_s, ex_r, ey_s, ey_r, pe_s, pe_r, q_s, q_r,
):
    xr = (xr0, xr1)
    tid, perm, keep, pos, mytile, place = (table.at[i] for i in range(6))
    me = lax.axis_index("cls")
    y = lax.axis_index("smp")
    c = me % NC
    z = (me // NC) % NZ
    x = me // (NC * NZ)

    turn = 1 - 2 * c

    zs = {off: lax.rem(z + turn * off + NZ, NZ) for off in range(-8, 9)}

    def zrel(off):
        return zs[off]

    devs = {}

    def at(dx=0, dz=0, dc=0, dy=0):
        return devs[(dx, dz, dc, dy)]

    def copy(src, dst, send, recv, dev):
        return pltpu.make_async_remote_copy(
            src_ref=src, dst_ref=dst, send_sem=send, recv_sem=recv,
            device_id=dev, device_id_type=MESH,
        )

    group = [(dx, dc) for dx in range(NX) for dc in range(NC) if (dx, dc) != (0, 0)]
    peers = [(0, o, 0, 0) for o in (1, -1, 2, -2) + FAR] + [(0, 0, 0, dy) for dy in (1, 2, 3)]
    peers += [(dx, 0, dc, 0) for dx, dc in group]
    for dx, dz, dc, dy in peers:
        devs[(dx, dz, dc, dy)] = (
            (lax.rem(x + dx, NX) * NZ + zs[dz]) * NC + lax.rem(c + dc, NC),
            lax.rem(y + dy, NY),
        )
    barrier = pltpu.get_barrier_semaphore()
    for peer in peers:
        pl.semaphore_signal(barrier, inc=1, device_id=at(*peer), device_id_type=MESH)
    loads = [
        pltpu.make_async_copy(a, b, in_s.at[i])
        for i, (a, b) in enumerate(
            (
                (start_hbm, theta),
                (counts_hbm, counts),
                (compat_hbm, cb.at[pl.ds(x * LINKS, LINKS)]),
                (owner_hbm, owner),
                (local_hbm, local),
            )
        )
    ]
    for load in loads:
        load.start()
    lane = lax.broadcasted_iota(jnp.int32, (8, TILE), 1)
    level = lax.broadcasted_iota(jnp.int32, (8, TILE), 0)
    loads[3].wait()
    loads[4].wait()
    raw[...] = jnp.zeros((8, TILE), jnp.int32)
    raw[0:K, 0:CT] = owner[...] * TD + local[...]
    rows = jnp.zeros((8, TILE), jnp.int32)
    for i in range(CT):
        one = jnp.broadcast_to(raw[:, i : i + 1], (8, TILE))
        rows = jnp.where((lane % LINKS // K == i) & (lane % K == level), one, rows)
    row = jnp.sum(rows, axis=0, keepdims=True)
    tab[0] = jnp.where(lane // LINKS == x, jnp.broadcast_to(row, (8, TILE)), 0)
    pl.semaphore_wait(barrier, len(peers))

    def lcopy(dx):
        return copy(tab.at[0], tab.at[dx], l_s.at[dx - 1], l_r.at[dx - 1], at(dx=dx))

    for dx in (2, 1, 3):
        lcopy(dx).start()

    def load_lists():
        return pltpu.make_async_copy(lists, table, in_s.at[5])

    def make_lists():
        for dx in (1, 3, 2):
            lcopy(dx).wait_recv()
        whole = tab[0, 0:1] + tab[1, 0:1] + tab[2, 0:1] + tab[3, 0:1]
        key = jnp.where(whole // COL == x, whole % COL, COL)
        keys = jnp.broadcast_to(key, (TILE, TILE))
        mine = jnp.transpose(keys)
        j = lax.broadcasted_iota(jnp.int32, (TILE, TILE), 0)
        i = lax.broadcasted_iota(jnp.int32, (TILE, TILE), 1)
        before = jnp.where(keys < mine, 1, 0) + jnp.where((keys == mine) & (i < j), 1, 0)
        rank = jnp.sum(before, axis=1, keepdims=True)
        at_rank = rank == i
        order = jnp.sum(jnp.where(at_rank, j, 0), axis=0, keepdims=True)
        ranked = jnp.sum(jnp.where(at_rank, mine, 0), axis=0, keepdims=True)
        again = (ranked == pltpu.roll(ranked, 1, 1)) & (lane[0:1] > 0)
        upto = jnp.sum(jnp.where(mine <= i, 1, 0), axis=0, keepdims=True)
        some = jnp.sum(jnp.where(mine == i, 1, 0), axis=0, keepdims=True)
        lists[0:1, :] = whole
        lists[1:2, :] = order
        lists[2:3, :] = jnp.where(again, 1, 0)
        lists[3:4, :] = jnp.where(some > 0, upto - 1, COL)
        col = whole % COL
        lies = (col // TD) % NC * HALF + col // (TD * NC) * TD + col % TD
        lists[4:5, :] = jnp.where(key < COL, lies, COL)
        lists[5:6, :] = lies
        load = load_lists()
        load.start()

    far = [(j, 0, o) for j, o in enumerate(FAR)]
    near_own = [(4 + j, 0, o) for j, o in enumerate(NEAR)]
    near_of = [[(6 + 2 * i + j, -w, o) for j, o in enumerate(NEAR)] for i, w in enumerate(FAR)]
    near_of[0].append((14, -FAR[0], 2))
    every = far + near_own + [step for steps in near_of for step in steps]

    def spread(blk, send, recv):
        def move(k, off, way):
            ref = blk(zrel(off))
            return copy(ref, ref, send.at[k], recv.at[k], at(dz=way))

        def take(k, off, way):
            ref = blk(zrel(off - way))
            copy(ref, ref, send.at[k], recv.at[k], at(dz=way)).wait_recv()

        def first():
            for k, off, way in far + near_own:
                move(k, off, way).start()

        def second():
            for i in (2, 3, 0, 1):
                take(*far[i])
                for step in near_of[i]:
                    move(*step).start()

        def third():
            for steps in [near_own] + [near_of[i] for i in (2, 3, 0, 1)]:
                for step in steps:
                    take(*step)

        def close():
            for step in every:
                move(*step).wait_send()

        return first, second, third, close

    def th_blk(zz):
        return th.at[pl.ds(c * HALF + zz * TD, TD)]

    def to_core(core):
        ref = th.at[pl.ds(core * HALF, HALF)]
        return copy(ref, ref, fc_s.at[0], fc_r.at[0], at(dc=1))

    f_first, f_second, f_third, f_close = spread(th_blk, fz_s, fz_r)
    t_first, t_second, t_third, t_close = spread(lambda zz: tt.at[zz], tz_s, tz_r)

    lists[...] = jnp.zeros((8, TILE), jnp.int32)
    loads[0].wait()
    cum[COL] = jnp.zeros((16, TILE), jnp.float32)
    th[COL] = jnp.zeros((16, TILE), jnp.bfloat16)

    def total_own():
        s = counts[:, 0:TILE]
        for i in range(1, counts.shape[1] // TILE):
            s = s + counts[:, i * TILE : (i + 1) * TILE]
        tt[z] = s

    def tg(j, dx, dc):
        return copy(tx.at[0], tx.at[1 + j], tg_s.at[j], tg_r.at[j], at(dx=dx, dc=dc))

    part = 6
    rest = LINKS - NY * part

    def ex(dx, src_x, step):
        if step < 2:
            ref = cb.at[pl.ds(src_x * LINKS + (y + 2 * step) % NY * part, part)]
        else:
            ref = cb.at[pl.ds(src_x * LINKS + NY * part, rest)]
        j = step * 3 + dx - 1
        return copy(ref, ref, ex_s.at[j], ex_r.at[j], at(dx=dx))

    def ey(dx, dy, src_y):
        ref = cb.at[pl.ds(((x + NX - dx) % NX) * LINKS + src_y * part, part)]
        j = (dx - 1) * 3 + dy - 1
        return copy(ref, ref, ey_s.at[j], ey_r.at[j], at(dy=dy))

    def sweep(r, carry):
        for t in range(TD):
            th[c * HALF + z * TD + t] = theta[:, t * TILE : (t + 1) * TILE].astype(jnp.bfloat16)
        f_first()

        @pl.when(r == 0)
        def _():
            loads[1].wait()
            total_own()
            loads[2].wait()
            for dx in (2, 1, 3):
                ex(dx, x, 0).start()
            make_lists()

        f_second()

        f_third()

        to_core(c).start()
        to_core(1 - c).wait_recv()

        def xcopy(dx, h):
            j = (dx - 1) * HALVES + h
            return copy(
                xs.at[pl.ds(j * PLINKS, PLINKS)], xr[h].at[pl.ds(x * PLINKS, PLINKS)],
                fx_s.at[j], fx_r.at[j], at(dx=dx),
            )

        def th_sent():
            f_close()
            to_core(c).wait_send()

        def expect(tiles, at_row):
            weights = jnp.concatenate([cb[at_row + k] for k in range(K)], axis=1)
            return lax.dot_general(
                jnp.concatenate(tiles, axis=1), weights, (((1,), (1,)), ((), ())),
                preferred_element_type=jnp.float32,
            )

        def share(src_x, i, ratio):
            row = src_x * LINKS + i * K
            weights = jnp.concatenate([cb[row + k] for k in range(K)], axis=1)
            got = jnp.dot(ratio, weights, preferred_element_type=jnp.float32)
            for k in range(K):
                sr[src_x * LINKS + i * K + k] = got[:, k * TILE : (k + 1) * TILE].astype(
                    jnp.bfloat16
                )

        def by_tiles():
            load_lists().wait()
            for h in range(HALVES):
                for dx in (2, 1, 3):
                    row = ((x + dx) % NX) * LINKS + h * PLINKS

                    def pick(l, _, base=((dx - 1) * HALVES + h) * PLINKS, row=row):
                        xs[base + l] = th[place[row + l]]
                        return 0

                    lax.fori_loop(0, PLINKS, pick, 0, unroll=8)
                    xcopy(dx, h).start()
            for h in range(HALVES):

                def pick_own(l, _, h=h):
                    xr[h][x * PLINKS + l] = th[place[x * LINKS + h * PLINKS + l]]
                    return 0

                lax.fori_loop(0, PLINKS, pick_own, 0, unroll=8)

            t_first()
            for dx in (1, 3, 2):
                ex(dx, (x + NX - dx) % NX, 0).wait_recv()
                for dy in (1, 3):
                    ey(dx, dy, y).start()

            def scopy(dx, h, src_x):
                ref = sr.at[pl.ds(src_x * LINKS + h * PLINKS, PLINKS)]
                j = (dx - 1) * HALVES + h
                return copy(ref, ref, rx_s.at[j], rx_r.at[j], at(dx=dx))

            for h in range(HALVES):
                for dx in (1, 3, 2):
                    ref = xr[h].at[pl.ds(((x + NX - dx) % NX) * PLINKS, PLINKS)]
                    j = (dx - 1) * HALVES + h
                    copy(ref, ref, fx_s.at[j], fx_r.at[j], at(dx=dx)).wait_recv()

                def tile(n, _, h=h):
                    i = h * PCT + n
                    tiles = []
                    for k in range(K):
                        l = n * K + k
                        src_x = tid[x * LINKS + h * PLINKS + l] // COL
                        tiles.append(xr[h][src_x * PLINKS + l])
                    acc = expect(tiles, x * LINKS + i * K)
                    ratio = (counts[:, pl.ds(pl.multiple_of(i * TILE, TILE), TILE)] / acc).astype(
                        jnp.bfloat16
                    )
                    share(x, i, ratio)
                    return 0

                lax.fori_loop(0, PCT, tile, 0, unroll=4)
                for dx in (2, 1, 3):
                    scopy(dx, h, x).start()
            th_sent()
            t_second()
            t_third()
            s = tt[0]
            for i in range(1, NZ):
                s = s + tt[i]
            tx[0] = s
            for j, (dx, dc) in enumerate(group):
                tg(j, dx, dc).start()
            for h in range(HALVES):
                for dx in (1, 3, 2):
                    scopy(dx, h, (x + NX - dx) % NX).wait_recv()
            for dx in (1, 2, 3):
                for h in range(HALVES):
                    xcopy(dx, h).wait_send()
                    scopy(dx, h, x).wait_send()
                ex(dx, x, 0).wait_send()
                lcopy(dx).wait_send()

        def pcopy_x(dx, h):
            j = (dx - 1) * HALVES + h
            return copy(
                pe.at[pl.ds(dx * CT + h * PCT, PCT)], pr.at[pl.ds((dx - 1) * CT + h * PCT, PCT)],
                pe_s.at[j], pe_r.at[j], at(dx=dx),
            )

        def qcopy(dx, h, src_x):
            ref = rt.at[pl.ds(src_x * CT + h * PCT, PCT)]
            j = (dx - 1) * HALVES + h
            return copy(ref, ref, q_s.at[j], q_r.at[j], at(dx=dx))

        def by_sums():
            @pl.when(r == 1)
            def _():
                for dx in (1, 2, 3):
                    ex(dx, (x + NX - dx) % NX, 1).wait_recv()
                    ex(dx, (x + NX - dx) % NX, 2).wait_recv()
                    for dy in (1, 3):
                        ey(dx, dy, (y + NY - dy) % NY).wait_recv()

            for h in range(HALVES):
                for dx in (2, 1, 3) + ((0,) if h == HALVES - 1 else ()):
                    row = ((x + dx) % NX) * LINKS

                    def part_sum(i, _, dx=dx, row=row):
                        pe[dx * CT + i] = expect(
                            [th[mytile[row + i * K + k]] for k in range(K)], row + i * K
                        )
                        return 0

                    lax.fori_loop(h * PCT if dx else 0, (h + 1) * PCT, part_sum, 0, unroll=4)
                    if dx:
                        pcopy_x(dx, h).start()
            th_sent()

            def shares(src_x, h):
                def one(i, _):
                    share(src_x, i, rt[src_x * CT + i])
                    return 0

                lax.fori_loop(h * PCT, (h + 1) * PCT, one, 0, unroll=4)

            for h in range(HALVES):
                for dx in (1, 3, 2):
                    pcopy_x(dx, h).wait_recv()

                def ratio(i, _):
                    acc = pe[i] + pr[i] + pr[CT + i] + pr[2 * CT + i]
                    rt[x * CT + i] = (
                        counts[:, pl.ds(pl.multiple_of(i * TILE, TILE), TILE)] / acc
                    ).astype(jnp.bfloat16)
                    return 0

                lax.fori_loop(h * PCT, (h + 1) * PCT, ratio, 0, unroll=4)
                for dx in (2, 1, 3):
                    qcopy(dx, h, x).start()
                shares(x, h)
            for h in range(HALVES):
                for dx in (1, 3, 2):
                    src_x = (x + NX - dx) % NX
                    qcopy(dx, h, src_x).wait_recv()
                    shares(src_x, h)
            for dx in (1, 2, 3):
                for h in range(HALVES):
                    pcopy_x(dx, h).wait_send()
                    qcopy(dx, h, x).wait_send()

            @pl.when(r == 1)
            def _():
                for dx in (1, 2, 3):
                    ex(dx, x, 1).wait_send()
                    ex(dx, x, 2).wait_send()
                    for dy in (1, 3):
                        ey(dx, dy, y).wait_send()

        pl.when(r == 0)(by_tiles)
        pl.when(r > 0)(by_sums)

        def add(j, acc):
            acc = jnp.where(keep[j] > 0, acc, 0.0) + sr[perm[j]].astype(jnp.float32)
            cum[j] = acc
            return acc

        lax.fori_loop(0, COL, add, jnp.zeros((16, TILE), jnp.float32), unroll=8)

        def dense(core, off_sign, first, count):
            for p in range(first, first + count):
                zz = zs[off_sign * PLACES[p]]
                for t in range(TD):
                    d[core * HALF + p * TD + t] = cum[pos[(zz * NC + core) * TD + t]]

        def rcopy(g):
            first, count = GROUPS[g]
            return copy(
                d.at[pl.ds((1 - c) * HALF + first * TD, count * TD)],
                cr.at[pl.ds(first * TD, count * TD)], rc_s.at[g], rc_r.at[g], at(dc=1),
            )

        for g, (first, count) in enumerate(GROUPS):
            dense(1 - c, -1, first, count)
            rcopy(g).start()
        for first, count in GROUPS:
            dense(c, 1, first, count)

        def dz(off):
            return d.at[pl.ds(c * HALF + PLACES.index(off) * TD, TD)]

        kinds = (0,) + FAR
        nsteps = [
            [(q * 2 + j, way, way + kind) for j, way in enumerate(NEAR)]
            for q, kind in enumerate(kinds)
        ]
        nsteps[1].append((10, 2, 8))

        def ncopy(slot, way, dest):
            return copy(
                dz(dest), nr.at[pl.ds(slot * TD, TD)], rn_s.at[slot], rn_r.at[slot], at(dz=way)
            )

        def fcopy(j, way):
            return copy(
                sf.at[pl.ds(j * TD, TD)], fr.at[pl.ds(j * TD, TD)], rf_s.at[j], rf_r.at[j],
                at(dz=way),
            )

        for g, q in enumerate((1, 2, 3, 4, 0)):
            rcopy(g).wait_recv()
            first, count = GROUPS[g]
            for i in range(first * TD, (first + count) * TD):
                d[c * HALF + i] = d[c * HALF + i] + cr[i]
            for n in nsteps[q]:
                ncopy(*n).start()

        @pl.when(r == 0)
        def _():
            for j, (dx, dc) in enumerate(group):
                tg(j, dx, dc).wait_recv()
            s = tx[0]
            for j in range(len(group)):
                s = s + tx[1 + j]
            tot[...] = jnp.broadcast_to(jnp.sum(s, axis=1, keepdims=True), (16, TILE))

        for q, kind in enumerate(kinds):
            if q == 0:
                continue
            for n in nsteps[q]:
                ncopy(*n).wait_recv()
            for t in range(TD):
                acc = d[c * HALF + PLACES.index(kind) * TD + t]
                for n in nsteps[q]:
                    acc = acc + nr[n[0] * TD + t]
                sf[(q - 1) * TD + t] = acc
            fcopy(q - 1, kind).start()
        @pl.when(r == 0)
        def _():
            for dx in (2, 1, 3):
                ex(dx, x, 1).start()
                ex(dx, x, 2).start()

        for n in nsteps[0]:
            ncopy(*n).wait_recv()
        for t in range(TD):
            acc = d[c * HALF + PLACES.index(0) * TD + t]
            for n in nsteps[0]:
                acc = acc + nr[n[0] * TD + t]
            sums[t] = acc
        for j in (2, 3, 0, 1):
            fcopy(j, FAR[j]).wait_recv()
        for t in range(TD):
            cols = slice(t * TILE, (t + 1) * TILE)
            acc = sums[t] + ((fr[t] + fr[TD + t]) + (fr[2 * TD + t] + fr[3 * TD + t]))
            updated = theta[:, cols] * acc / tot[...]
            theta[:, cols] = updated
            ps[r * NY, :, cols] = jnp.sum(updated, axis=0, keepdims=True)

        def pcopy(dy):
            j = r * 3 + dy - 1
            return copy(ps.at[r * NY], ps.at[r * NY + dy], p_s.at[j], p_r.at[j], at(dy=dy))

        for dy in (2, 1, 3):
            pcopy(dy).start()
        for g in range(len(GROUPS)):
            rcopy(g).wait_send()
        for steps in nsteps:
            for n in steps:
                ncopy(*n).wait_send()
        for j, way in enumerate(FAR):
            fcopy(j, way).wait_send()

        @pl.when(r == 0)
        def _():
            t_close()
            for j, (dx, dc) in enumerate(group):
                tg(j, dx, dc).wait_send()

        for dy in (1, 3, 2):
            pcopy(dy).wait_recv()
        pooled = ps[r * NY] + ps[r * NY + 1] + ps[r * NY + 2] + ps[r * NY + 3]
        theta[...] = (1.0 - MIXING) * theta[...] + (MIXING / (16 * NY)) * pooled
        for dy in (1, 2, 3):
            pcopy(dy).wait_send()
        return carry

    lax.fori_loop(0, ITERS, sweep, 0)
    out[...] = theta[...] * 65536.0


def body(counts, compat, link_owner, link_local, start):
    hbm = pl.BlockSpec(memory_space=pltpu.HBM)
    vmem = pl.BlockSpec(memory_space=pltpu.VMEM)
    f32, bf16 = jnp.float32, jnp.bfloat16
    dma = pltpu.SemaphoreType.DMA

    def buf(n, dtype):
        return pltpu.VMEM((n, 16, TILE), dtype)

    return pl.pallas_call(
        em_kernel,
        out_shape=jax.ShapeDtypeStruct(start.shape, f32),
        in_specs=[hbm] * 5,
        out_specs=vmem,
        scratch_shapes=[
            pltpu.VMEM((K, CT), jnp.int32),
            pltpu.VMEM((K, CT), jnp.int32),
            pltpu.VMEM(counts.shape, f32),
            pltpu.VMEM((NX * LINKS, TILE, TILE), bf16),
            pltpu.VMEM((NX, 8, TILE), jnp.int32),
            pltpu.VMEM((8, TILE), jnp.int32),
            pltpu.VMEM((8, TILE), jnp.int32),
            pltpu.SMEM((8, TILE), jnp.int32),
            buf(COL + 1, bf16),
            buf(3 * LINKS, bf16),
            buf(NX * PLINKS, bf16), buf(NX * PLINKS, bf16),
            buf(NX * LINKS, bf16),
            buf(COL + 1, f32),
            buf(COL, f32),
            buf(HALF, f32),
            buf(11 * TD, f32),
            buf(4 * TD, f32),
            buf(4 * TD, f32),
            buf(NZ, f32),
            buf(NX * NC, f32),
            pltpu.VMEM((16, TILE), f32),
            pltpu.VMEM((ITERS * NY, 1, TD * TILE), f32),
            pltpu.VMEM((16, TD * TILE), f32),
            dma((15,)), dma((15,)),
            dma((1,)), dma((1,)),
            dma((3 * HALVES,)), dma((3 * HALVES,)),
            dma((3 * HALVES,)), dma((3 * HALVES,)),
            dma((5,)), dma((5,)),
            dma((11,)), dma((11,)),
            dma((4,)), dma((4,)),
            dma((15,)), dma((15,)),
            dma((7,)), dma((7,)),
            dma((ITERS * 3,)), dma((ITERS * 3,)),
            dma((3,)), dma((3,)), dma((6,)),
            buf(TD, f32),
            buf(NX * CT, f32),
            buf(3 * CT, f32),
            buf(NX * CT, bf16),
            dma((9,)), dma((9,)),
            dma((9,)), dma((9,)),
            dma((3 * HALVES,)), dma((3 * HALVES,)),
            dma((3 * HALVES,)), dma((3 * HALVES,)),
        ],
        compiler_params=pltpu.CompilerParams(
            collective_id=0, has_side_effects=True, vmem_limit_bytes=60 << 20
        ),
        name="em_rounds",
    )(link_owner.T, link_local.T, counts, compat.reshape(LINKS, TILE, TILE), start)


def solution(mesh):
    placed = (
        P("smp", "cls"),
        P("cls", None, None, None),
        P("cls", None),
        P("cls", None),
        P("smp", "cls"),
    )
    return jax.shard_map(
        body, mesh=mesh, in_specs=placed, out_specs=P("smp", "cls"), check_vma=False
    )
```

```python
import functools

import jax
import jax.numpy as jnp
from jax import lax
from jax.experimental import pallas as pl
from jax.experimental.pallas import tpu as pltpu
from jax.sharding import PartitionSpec as P

TILE = 128
K = 4
ITERS = 3
MIXING = 0.3
MESH = pl.DeviceIdType.MESH
NX, NZ, NC, NY = 4, 16, 2, 4
TD = 4
CT = 8
LINKS = 32
HALVES = 2
PCT, PLINKS = CT // HALVES, LINKS // HALVES
COL = NZ * NC * TD
HALF = NZ * TD
FAR = (6, -6, 3, -3)
NEAR = (1, -1)
PLACES = (5, 6, 7, 8, -7, -6, -5, 2, 3, 4, -4, -3, -2, -1, 0, 1)
GROUPS = ((0, 4), (4, 3), (7, 3), (10, 3), (13, 3))


def em_kernel(
    owner_hbm, local_hbm, counts_hbm, compat_hbm, start_hbm, out,
    owner, local, counts, cb, tab, raw, lists, table, th, xs, xr0, xr1, sr, cum, d, cr, nr, sf, fr, tt, tx, tot, ps, theta,
    fz_s, fz_r, fc_s, fc_r, fx_s, fx_r, rx_s, rx_r, rc_s, rc_r,
    rn_s, rn_r, rf_s, rf_r, tz_s, tz_r, tg_s, tg_r, p_s, p_r, l_s, l_r, in_s,
    sums, pe, pr, rt, ex_s, ex_r, ey_s, ey_r, pe_s, pe_r, q_s, q_r,
):
    xr = (xr0, xr1)
    tid, perm, keep, pos, mytile, place = (table.at[i] for i in range(6))
    me = lax.axis_index("cls")
    y = lax.axis_index("smp")
    c = me % NC
    z = (me // NC) % NZ
    x = me // (NC * NZ)

    turn = 1 - 2 * c

    zs = {off: lax.rem(z + turn * off + NZ, NZ) for off in range(-8, 9)}

    def zrel(off):
        return zs[off]

    devs = {}

    def at(dx=0, dz=0, dc=0, dy=0):
        return devs[(dx, dz, dc, dy)]

    def copy(src, dst, send, recv, dev):
        return pltpu.make_async_remote_copy(
            src_ref=src, dst_ref=dst, send_sem=send, recv_sem=recv,
            device_id=dev, device_id_type=MESH,
        )

    group = [(dx, dc) for dx in range(NX) for dc in range(NC) if (dx, dc) != (0, 0)]
    peers = [(0, o, 0, 0) for o in (1, -1, 2, -2) + FAR] + [(0, 0, 0, dy) for dy in (1, 2, 3)]
    peers += [(dx, 0, dc, 0) for dx, dc in group]
    for dx, dz, dc, dy in peers:
        devs[(dx, dz, dc, dy)] = (
            (lax.rem(x + dx, NX) * NZ + zs[dz]) * NC + lax.rem(c + dc, NC),
            lax.rem(y + dy, NY),
        )
    barrier = pltpu.get_barrier_semaphore()
    for peer in peers:
        pl.semaphore_signal(barrier, inc=1, device_id=at(*peer), device_id_type=MESH)
    loads = [
        pltpu.make_async_copy(a, b, in_s.at[i])
        for i, (a, b) in enumerate(
            (
                (start_hbm, theta),
                (counts_hbm, counts),
                (compat_hbm, cb.at[pl.ds(x * LINKS, LINKS)]),
                (owner_hbm, owner),
                (local_hbm, local),
            )
        )
    ]
    for load in loads:
        load.start()
    lane = lax.broadcasted_iota(jnp.int32, (8, TILE), 1)
    level = lax.broadcasted_iota(jnp.int32, (8, TILE), 0)
    loads[3].wait()
    loads[4].wait()
    raw[...] = jnp.zeros((8, TILE), jnp.int32)
    raw[0:K, 0:CT] = owner[...] * TD + local[...]
    rows = jnp.zeros((8, TILE), jnp.int32)
    for i in range(CT):
        one = jnp.broadcast_to(raw[:, i : i + 1], (8, TILE))
        rows = jnp.where((lane % LINKS // K == i) & (lane % K == level), one, rows)
    row = jnp.sum(rows, axis=0, keepdims=True)
    tab[0] = jnp.where(lane // LINKS == x, jnp.broadcast_to(row, (8, TILE)), 0)
    pl.semaphore_wait(barrier, len(peers))

    def lcopy(dx):
        return copy(tab.at[0], tab.at[dx], l_s.at[dx - 1], l_r.at[dx - 1], at(dx=dx))

    for dx in (2, 1, 3):
        lcopy(dx).start()

    def load_lists():
        return pltpu.make_async_copy(lists, table, in_s.at[5])

    def make_lists():
        for dx in (1, 3, 2):
            lcopy(dx).wait_recv()
        whole = tab[0, 0:1] + tab[1, 0:1] + tab[2, 0:1] + tab[3, 0:1]
        key = jnp.where(whole // COL == x, whole % COL, COL)
        keys = jnp.broadcast_to(key, (TILE, TILE))
        mine = jnp.transpose(keys)
        j = lax.broadcasted_iota(jnp.int32, (TILE, TILE), 0)
        i = lax.broadcasted_iota(jnp.int32, (TILE, TILE), 1)
        before = jnp.where(keys < mine, 1, 0) + jnp.where((keys == mine) & (i < j), 1, 0)
        rank = jnp.sum(before, axis=1, keepdims=True)
        at_rank = rank == i
        order = jnp.sum(jnp.where(at_rank, j, 0), axis=0, keepdims=True)
        ranked = jnp.sum(jnp.where(at_rank, mine, 0), axis=0, keepdims=True)
        again = (ranked == pltpu.roll(ranked, 1, 1)) & (lane[0:1] > 0)
        upto = jnp.sum(jnp.where(mine <= i, 1, 0), axis=0, keepdims=True)
        some = jnp.sum(jnp.where(mine == i, 1, 0), axis=0, keepdims=True)
        lists[0:1, :] = whole
        lists[1:2, :] = order
        lists[2:3, :] = jnp.where(again, 1, 0)
        lists[3:4, :] = jnp.where(some > 0, upto - 1, COL)
        col = whole % COL
        lies = (col // TD) % NC * HALF + col // (TD * NC) * TD + col % TD
        lists[4:5, :] = jnp.where(key < COL, lies, COL)
        lists[5:6, :] = lies
        load = load_lists()
        load.start()

    far = [(j, 0, o) for j, o in enumerate(FAR)]
    near_own = [(4 + j, 0, o) for j, o in enumerate(NEAR)]
    near_of = [[(6 + 2 * i + j, -w, o) for j, o in enumerate(NEAR)] for i, w in enumerate(FAR)]
    near_of[0].append((14, -FAR[0], 2))
    every = far + near_own + [step for steps in near_of for step in steps]

    def spread(blk, send, recv):
        def move(k, off, way):
            ref = blk(zrel(off))
            return copy(ref, ref, send.at[k], recv.at[k], at(dz=way))

        def take(k, off, way):
            ref = blk(zrel(off - way))
            copy(ref, ref, send.at[k], recv.at[k], at(dz=way)).wait_recv()

        def first():
            for k, off, way in far + near_own:
                move(k, off, way).start()

        def second():
            for i in (2, 3, 0, 1):
                take(*far[i])
                for step in near_of[i]:
                    move(*step).start()

        def third():
            for steps in [near_own] + [near_of[i] for i in (2, 3, 0, 1)]:
                for step in steps:
                    take(*step)

        def close():
            for step in every:
                move(*step).wait_send()

        return first, second, third, close

    def th_blk(zz):
        return th.at[pl.ds(c * HALF + zz * TD, TD)]

    def to_core(core):
        ref = th.at[pl.ds(core * HALF, HALF)]
        return copy(ref, ref, fc_s.at[0], fc_r.at[0], at(dc=1))

    f_first, f_second, f_third, f_close = spread(th_blk, fz_s, fz_r)
    t_first, t_second, t_third, t_close = spread(lambda zz: tt.at[zz], tz_s, tz_r)

    lists[...] = jnp.zeros((8, TILE), jnp.int32)
    loads[0].wait()
    cum[COL] = jnp.zeros((16, TILE), jnp.float32)
    th[COL] = jnp.zeros((16, TILE), jnp.bfloat16)

    def total_own():
        s = counts[:, 0:TILE]
        for i in range(1, counts.shape[1] // TILE):
            s = s + counts[:, i * TILE : (i + 1) * TILE]
        tt[z] = s

    def tg(j, dx, dc):
        return copy(tx.at[0], tx.at[1 + j], tg_s.at[j], tg_r.at[j], at(dx=dx, dc=dc))

    part = 6
    rest = LINKS - NY * part

    def ex(dx, src_x, step):
        if step < 2:
            ref = cb.at[pl.ds(src_x * LINKS + (y + 2 * step) % NY * part, part)]
        else:
            ref = cb.at[pl.ds(src_x * LINKS + NY * part, rest)]
        j = step * 3 + dx - 1
        return copy(ref, ref, ex_s.at[j], ex_r.at[j], at(dx=dx))

    def ey(dx, dy, src_y):
        ref = cb.at[pl.ds(((x + NX - dx) % NX) * LINKS + src_y * part, part)]
        j = (dx - 1) * 3 + dy - 1
        return copy(ref, ref, ey_s.at[j], ey_r.at[j], at(dy=dy))

    def sweep(r, carry):
        for t in range(TD):
            th[c * HALF + z * TD + t] = theta[:, t * TILE : (t + 1) * TILE].astype(jnp.bfloat16)
        f_first()

        @pl.when(r == 0)
        def _():
            loads[1].wait()
            total_own()
            loads[2].wait()
            for dx in (2, 1, 3):
                ex(dx, x, 0).start()
            make_lists()

        f_second()

        f_third()

        to_core(c).start()
        to_core(1 - c).wait_recv()

        def xcopy(dx, h):
            j = (dx - 1) * HALVES + h
            return copy(
                xs.at[pl.ds(j * PLINKS, PLINKS)], xr[h].at[pl.ds(x * PLINKS, PLINKS)],
                fx_s.at[j], fx_r.at[j], at(dx=dx),
            )

        def th_sent():
            f_close()
            to_core(c).wait_send()

        def expect(tiles, at_row):
            weights = jnp.concatenate([cb[at_row + k] for k in range(K)], axis=1)
            return lax.dot_general(
                jnp.concatenate(tiles, axis=1), weights, (((1,), (1,)), ((), ())),
                preferred_element_type=jnp.float32,
            )

        def share(src_x, i, ratio):
            row = src_x * LINKS + i * K
            weights = jnp.concatenate([cb[row + k] for k in range(K)], axis=1)
            got = jnp.dot(ratio, weights, preferred_element_type=jnp.float32)
            for k in range(K):
                sr[src_x * LINKS + i * K + k] = got[:, k * TILE : (k + 1) * TILE].astype(
                    jnp.bfloat16
                )

        def by_tiles():
            load_lists().wait()
            for h in range(HALVES):
                for dx in (2, 1, 3):
                    row = ((x + dx) % NX) * LINKS + h * PLINKS

                    def pick(l, _, base=((dx - 1) * HALVES + h) * PLINKS, row=row):
                        xs[base + l] = th[place[row + l]]
                        return 0

                    lax.fori_loop(0, PLINKS, pick, 0, unroll=8)
                    xcopy(dx, h).start()
            for h in range(HALVES):

                def pick_own(l, _, h=h):
                    xr[h][x * PLINKS + l] = th[place[x * LINKS + h * PLINKS + l]]
                    return 0

                lax.fori_loop(0, PLINKS, pick_own, 0, unroll=8)

            t_first()
            for dx in (1, 3, 2):
                ex(dx, (x + NX - dx) % NX, 0).wait_recv()
                for dy in (1, 3):
                    ey(dx, dy, y).start()

            def scopy(dx, h, src_x):
                ref = sr.at[pl.ds(src_x * LINKS + h * PLINKS, PLINKS)]
                j = (dx - 1) * HALVES + h
                return copy(ref, ref, rx_s.at[j], rx_r.at[j], at(dx=dx))

            for h in range(HALVES):
                for dx in (1, 3, 2):
                    ref = xr[h].at[pl.ds(((x + NX - dx) % NX) * PLINKS, PLINKS)]
                    j = (dx - 1) * HALVES + h
                    copy(ref, ref, fx_s.at[j], fx_r.at[j], at(dx=dx)).wait_recv()

                def tile(n, _, h=h):
                    i = h * PCT + n
                    tiles = []
                    for k in range(K):
                        l = n * K + k
                        src_x = tid[x * LINKS + h * PLINKS + l] // COL
                        tiles.append(xr[h][src_x * PLINKS + l])
                    acc = expect(tiles, x * LINKS + i * K)
                    ratio = (counts[:, pl.ds(pl.multiple_of(i * TILE, TILE), TILE)] / acc).astype(
                        jnp.bfloat16
                    )
                    share(x, i, ratio)
                    return 0

                lax.fori_loop(0, PCT, tile, 0, unroll=4)
                for dx in (2, 1, 3):
                    scopy(dx, h, x).start()
            th_sent()
            t_second()
            t_third()
            s = tt[0]
            for i in range(1, NZ):
                s = s + tt[i]
            tx[0] = s
            for j, (dx, dc) in enumerate(group):
                tg(j, dx, dc).start()
            for h in range(HALVES):
                for dx in (1, 3, 2):
                    scopy(dx, h, (x + NX - dx) % NX).wait_recv()
            for dx in (1, 2, 3):
                for h in range(HALVES):
                    xcopy(dx, h).wait_send()
                    scopy(dx, h, x).wait_send()
                ex(dx, x, 0).wait_send()
                lcopy(dx).wait_send()

        def pcopy_x(dx, h):
            j = (dx - 1) * HALVES + h
            return copy(
                pe.at[pl.ds(dx * CT + h * PCT, PCT)], pr.at[pl.ds((dx - 1) * CT + h * PCT, PCT)],
                pe_s.at[j], pe_r.at[j], at(dx=dx),
            )

        def qcopy(dx, h, src_x):
            ref = rt.at[pl.ds(src_x * CT + h * PCT, PCT)]
            j = (dx - 1) * HALVES + h
            return copy(ref, ref, q_s.at[j], q_r.at[j], at(dx=dx))

        def by_sums():
            @pl.when(r == 1)
            def _():
                for dx in (1, 2, 3):
                    ex(dx, (x + NX - dx) % NX, 1).wait_recv()
                    ex(dx, (x + NX - dx) % NX, 2).wait_recv()
                    for dy in (1, 3):
                        ey(dx, dy, (y + NY - dy) % NY).wait_recv()

            for h in range(HALVES):
                for dx in (2, 1, 3, 0):
                    row = ((x + dx) % NX) * LINKS

                    def part_sum(i, _, dx=dx, row=row):
                        pe[dx * CT + i] = expect(
                            [th[mytile[row + i * K + k]] for k in range(K)], row + i * K
                        )
                        return 0

                    lax.fori_loop(h * PCT, (h + 1) * PCT, part_sum, 0, unroll=4)
                    if dx:
                        pcopy_x(dx, h).start()
            th_sent()

            def shares(src_x, h):
                def one(i, _):
                    share(src_x, i, rt[src_x * CT + i])
                    return 0

                lax.fori_loop(h * PCT, (h + 1) * PCT, one, 0, unroll=4)

            for h in range(HALVES):
                for dx in (1, 3, 2):
                    pcopy_x(dx, h).wait_recv()

                def ratio(i, _):
                    acc = pe[i] + pr[i] + pr[CT + i] + pr[2 * CT + i]
                    rt[x * CT + i] = (
                        counts[:, pl.ds(pl.multiple_of(i * TILE, TILE), TILE)] / acc
                    ).astype(jnp.bfloat16)
                    return 0

                lax.fori_loop(h * PCT, (h + 1) * PCT, ratio, 0, unroll=4)
                for dx in (2, 1, 3):
                    qcopy(dx, h, x).start()
                shares(x, h)
            for h in range(HALVES):
                for dx in (1, 3, 2):
                    src_x = (x + NX - dx) % NX
                    qcopy(dx, h, src_x).wait_recv()
                    shares(src_x, h)
            for dx in (1, 2, 3):
                for h in range(HALVES):
                    pcopy_x(dx, h).wait_send()
                    qcopy(dx, h, x).wait_send()

            @pl.when(r == 1)
            def _():
                for dx in (1, 2, 3):
                    ex(dx, x, 1).wait_send()
                    ex(dx, x, 2).wait_send()
                    for dy in (1, 3):
                        ey(dx, dy, y).wait_send()

        pl.when(r == 0)(by_tiles)
        pl.when(r > 0)(by_sums)

        def add(j, acc):
            acc = jnp.where(keep[j] > 0, acc, 0.0) + sr[perm[j]].astype(jnp.float32)
            cum[j] = acc
            return acc

        lax.fori_loop(0, COL, add, jnp.zeros((16, TILE), jnp.float32), unroll=8)

        def dense(core, off_sign, first, count):
            for p in range(first, first + count):
                zz = zs[off_sign * PLACES[p]]
                for t in range(TD):
                    d[core * HALF + p * TD + t] = cum[pos[(zz * NC + core) * TD + t]]

        def rcopy(g):
            first, count = GROUPS[g]
            return copy(
                d.at[pl.ds((1 - c) * HALF + first * TD, count * TD)],
                cr.at[pl.ds(first * TD, count * TD)], rc_s.at[0], rc_r.at[g], at(dc=1),
            )

        for g, (first, count) in enumerate(GROUPS):
            dense(1 - c, -1, first, count)
            rcopy(g).start()
        for first, count in GROUPS:
            dense(c, 1, first, count)

        def dz(off):
            return d.at[pl.ds(c * HALF + PLACES.index(off) * TD, TD)]

        kinds = (0,) + FAR
        nsteps = [
            [(q * 2 + j, way, way + kind) for j, way in enumerate(NEAR)]
            for q, kind in enumerate(kinds)
        ]
        nsteps[1].append((10, 2, 8))

        def ncopy(slot, way, dest):
            return copy(
                dz(dest), nr.at[pl.ds(slot * TD, TD)], rn_s.at[0], rn_r.at[slot], at(dz=way)
            )

        def fcopy(j, way):
            return copy(
                sf.at[pl.ds(j * TD, TD)], fr.at[pl.ds(j * TD, TD)], rf_s.at[0], rf_r.at[j],
                at(dz=way),
            )

        for g, q in enumerate((1, 2, 3, 4, 0)):
            rcopy(g).wait_recv()
            first, count = GROUPS[g]
            for i in range(first * TD, (first + count) * TD):
                d[c * HALF + i] = d[c * HALF + i] + cr[i]
            for n in nsteps[q]:
                ncopy(*n).start()

        @pl.when(r == 0)
        def _():
            for j, (dx, dc) in enumerate(group):
                tg(j, dx, dc).wait_recv()
            s = tx[0]
            for j in range(len(group)):
                s = s + tx[1 + j]
            tot[...] = jnp.broadcast_to(jnp.sum(s, axis=1, keepdims=True), (16, TILE))

        for q, kind in enumerate(kinds):
            if q == 0:
                continue
            for n in nsteps[q]:
                ncopy(*n).wait_recv()
            for t in range(TD):
                acc = d[c * HALF + PLACES.index(kind) * TD + t]
                for n in nsteps[q]:
                    acc = acc + nr[n[0] * TD + t]
                sf[(q - 1) * TD + t] = acc
            fcopy(q - 1, kind).start()
        @pl.when(r == 0)
        def _():
            for dx in (2, 1, 3):
                ex(dx, x, 1).start()
                ex(dx, x, 2).start()

        for n in nsteps[0]:
            ncopy(*n).wait_recv()
        for t in range(TD):
            acc = d[c * HALF + PLACES.index(0) * TD + t]
            for n in nsteps[0]:
                acc = acc + nr[n[0] * TD + t]
            sums[t] = acc
        for j in (2, 3, 0, 1):
            fcopy(j, FAR[j]).wait_recv()
        for t in range(TD):
            cols = slice(t * TILE, (t + 1) * TILE)
            acc = sums[t] + ((fr[t] + fr[TD + t]) + (fr[2 * TD + t] + fr[3 * TD + t]))
            updated = theta[:, cols] * acc / tot[...]
            theta[:, cols] = updated
            ps[r * NY, :, cols] = jnp.sum(updated, axis=0, keepdims=True)

        def pcopy(dy):
            j = r * 3 + dy - 1
            return copy(ps.at[r * NY], ps.at[r * NY + dy], p_s.at[j], p_r.at[j], at(dy=dy))

        for dy in (2, 1, 3):
            pcopy(dy).start()
        for ref, sem in ((cr, rc_s), (nr, rn_s), (fr, rf_s)):
            copy(ref, ref, sem.at[0], sem.at[0], at(dc=1)).wait_send()

        @pl.when(r == 0)
        def _():
            t_close()
            for j, (dx, dc) in enumerate(group):
                tg(j, dx, dc).wait_send()

        for dy in (1, 3, 2):
            pcopy(dy).wait_recv()
        pooled = ps[r * NY] + ps[r * NY + 1] + ps[r * NY + 2] + ps[r * NY + 3]
        theta[...] = (1.0 - MIXING) * theta[...] + (MIXING / (16 * NY)) * pooled
        for dy in (1, 2, 3):
            pcopy(dy).wait_send()
        return carry

    lax.fori_loop(0, ITERS, sweep, 0)
    out[...] = theta[...] * 65536.0


def body(counts, compat, link_owner, link_local, start):
    hbm = pl.BlockSpec(memory_space=pltpu.HBM)
    vmem = pl.BlockSpec(memory_space=pltpu.VMEM)
    f32, bf16 = jnp.float32, jnp.bfloat16
    dma = pltpu.SemaphoreType.DMA

    def buf(n, dtype):
        return pltpu.VMEM((n, 16, TILE), dtype)

    return pl.pallas_call(
        em_kernel,
        out_shape=jax.ShapeDtypeStruct(start.shape, f32),
        in_specs=[hbm] * 5,
        out_specs=vmem,
        scratch_shapes=[
            pltpu.VMEM((K, CT), jnp.int32),
            pltpu.VMEM((K, CT), jnp.int32),
            pltpu.VMEM(counts.shape, f32),
            pltpu.VMEM((NX * LINKS, TILE, TILE), bf16),
            pltpu.VMEM((NX, 8, TILE), jnp.int32),
            pltpu.VMEM((8, TILE), jnp.int32),
            pltpu.VMEM((8, TILE), jnp.int32),
            pltpu.SMEM((8, TILE), jnp.int32),
            buf(COL + 1, bf16),
            buf(3 * LINKS, bf16),
            buf(NX * PLINKS, bf16), buf(NX * PLINKS, bf16),
            buf(NX * LINKS, bf16),
            buf(COL + 1, f32),
            buf(COL, f32),
            buf(HALF, f32),
            buf(11 * TD, f32),
            buf(4 * TD, f32),
            buf(4 * TD, f32),
            buf(NZ, f32),
            buf(NX * NC, f32),
            pltpu.VMEM((16, TILE), f32),
            pltpu.VMEM((ITERS * NY, 1, TD * TILE), f32),
            pltpu.VMEM((16, TD * TILE), f32),
            dma((15,)), dma((15,)),
            dma((1,)), dma((1,)),
            dma((3 * HALVES,)), dma((3 * HALVES,)),
            dma((3 * HALVES,)), dma((3 * HALVES,)),
            dma((5,)), dma((5,)),
            dma((11,)), dma((11,)),
            dma((4,)), dma((4,)),
            dma((15,)), dma((15,)),
            dma((7,)), dma((7,)),
            dma((ITERS * 3,)), dma((ITERS * 3,)),
            dma((3,)), dma((3,)), dma((6,)),
            buf(TD, f32),
            buf(NX * CT, f32),
            buf(3 * CT, f32),
            buf(NX * CT, bf16),
            dma((9,)), dma((9,)),
            dma((9,)), dma((9,)),
            dma((3 * HALVES,)), dma((3 * HALVES,)),
            dma((3 * HALVES,)), dma((3 * HALVES,)),
        ],
        compiler_params=pltpu.CompilerParams(
            collective_id=0, has_side_effects=True, vmem_limit_bytes=60 << 20
        ),
        name="em_rounds",
    )(link_owner.T, link_local.T, counts, compat.reshape(LINKS, TILE, TILE), start)


def solution(mesh):
    placed = (
        P("smp", "cls"),
        P("cls", None, None, None),
        P("cls", None),
        P("cls", None),
        P("smp", "cls"),
    )
    return jax.shard_map(
        body, mesh=mesh, in_specs=placed, out_specs=P("smp", "cls"), check_vma=False
    )
```
